32 devices in a mesh: gx: 4 (over z), gy: 8 (over y, x, core).
Axes of the slice: x: 2, y: 2, z: 4, core: 2. Of those that a mesh axis runs over, the one named last changes fastest.
Arguments:
- embeddings: bfloat16 [65536, 4096], P(('gx', 'gy'))
- signs: int32 [4096, 256], replicated, may hold values from -1 to 1, as said below
Outputs:
- triangle: float32 [256, 256], replicated
- basis: bfloat16 [65536, 256], P(('gx', 'gy'))
- projected: float32 [256, 4096], replicated
The draws below stay inside these ranges and needn't reach their ends.
Inputs may be any that keep to these rules, and one draw needn't show every extreme that they name: Every entry of signs is -1 or 1.
All inputs are finite; a program needn't handle non-finite values.
Results may differ from the reference program's by a relative error of at most 0.0024.
Values sent between devices are 32-bit elements; how exact they have to be, the bound alone decides.
No kernel may reach another device: no remote copies, remote signals or barrier semaphores. Data moves between devices by JAX's collectives and lax.ppermute only.
A program may use at most 128 MiB of HBM per device.

```python
import math
import jax
import jax.numpy as jnp
from jax import lax

D = 4096
K = 256
ROWS_DEV = 2048
ROWS = 65536
N_GY = 8


def draw_embeddings(key, part):
    key = jax.random.fold_in(key, 11)
    key_noise, key_rows, key_cols = jax.random.split(key, 3)
    ramp = jnp.exp(math.log(3.0) * jnp.arange(ROWS, dtype=jnp.float32) / max(ROWS - 1, 1))
    cols = jnp.exp(jax.random.uniform(key_cols, (1, D), jnp.float32) * math.log(10.0)) / 4.6
    noise = jax.random.normal(key_noise, (ROWS, D), jnp.float32)
    rows = jnp.exp(jax.random.uniform(key_rows, (ROWS,), jnp.float32) * math.log(4.0)) / 2.0
    scale = (ramp * rows)[:, None] * cols
    return (noise * scale).astype(jnp.bfloat16)


def draw_signs(key, part):
    key = jax.random.fold_in(key, 23)
    bits = jax.random.randint(key, (D, K), 0, 2, jnp.int32)
    return 2 * bits - 1


def setup_inputs(seed: int = 0) -> dict:
    arg_keys = jax.random.split(jax.random.key(seed), 3)
    return {
        "embeddings": draw_embeddings(jax.random.fold_in(arg_keys[2], 71), 0),
        "signs": draw_signs(jax.random.fold_in(arg_keys[2], 71), 0),
    }


def reference(embeddings, signs):
    sign_mat = signs.astype(jnp.bfloat16)
    block_rows = ROWS_DEV * N_GY
    blocks = embeddings.reshape(-1, block_rows, D)
    in_scale = 1.0 / math.sqrt(D)

    def sketch_block(block):
        return jnp.dot(block.astype(jnp.float32), sign_mat.astype(jnp.float32), preferred_element_type=jnp.float32) * in_scale
    sketch = lax.map(sketch_block, blocks).reshape(-1, K)
    gram = jnp.dot(sketch.T, sketch, precision=lax.Precision.HIGHEST) / ROWS
    lower = jnp.linalg.cholesky(gram)
    basis = lax.linalg.triangular_solve(lower, sketch, left_side=False, lower=True, transpose_a=True).astype(jnp.bfloat16)
    sketch_half = sketch.astype(jnp.bfloat16).reshape(-1, block_rows, K)

    def add_block(total, pair):
        left, right = pair
        return (total + jnp.dot(left.T.astype(jnp.float32), right.astype(jnp.float32), preferred_element_type=jnp.float32), None)
    start = jnp.zeros((K, D), jnp.float32)
    total, unused = lax.scan(add_block, start, (sketch_half, blocks))
    cross = total * (1.0 / math.sqrt(ROWS))
    projected = lax.linalg.triangular_solve(lower, cross, left_side=True, lower=True)
    return (lower.T, basis, projected)
```

```python
import functools
import math

import jax
import jax.numpy as jnp
from jax import lax
from jax.experimental import pallas as pl
from jax.experimental.pallas import tpu as pltpu
from jax.sharding import PartitionSpec as P

AXES = ("gx", "gy")
CHUNKS = 1
MIB = 1 << 20


def dot(a, b, dims=((1,), (0,))):
    return lax.dot_general(a, b, (dims, ((), ())), preferred_element_type=jnp.float32)


def split(a):
    high = a.astype(jnp.bfloat16)
    return high, (a - high.astype(jnp.float32)).astype(jnp.bfloat16)


def orders_of(n_devices):
    bits = list(range(1, n_devices.bit_length() - 1))
    swapped = bits[:]
    for i in range(0, len(bits) - 1, 2):
        swapped[i], swapped[i + 1] = bits[i + 1], bits[i]
    return bits, swapped


def bits_of(me, order):
    value = jnp.int32(0)
    for b in order:
        value = value * 2 + ((me >> b) & 1)
    return value


def sketch_kernel(in_scale, gram_scale, me, e, signs, sketch, rounded_t, gram_sent, gram_kept, s16, acc, mixed):
    step = pl.program_id(0)

    @pl.when(step == 0)
    def _():
        s16[...] = signs[...].astype(jnp.bfloat16)
        acc[...] = jnp.zeros_like(acc)
        mixed[...] = jnp.zeros_like(mixed)

    sk = dot(e[...], s16[...]) * in_scale
    sketch[...] = sk
    high, low = split(sk)
    high_t = high.T
    rounded_t[...] = high_t
    acc[...] += dot(high_t, high)
    mixed[...] += dot(high_t, low)

    @pl.when(step == pl.num_programs(0) - 1)
    def _():
        cross = mixed[...]
        acc[...] = (acc[...] + cross + cross.T) * gram_scale
        half = acc.shape[0] // 2
        own = me[0] & 1
        gram_kept[...] = acc[pl.ds(pl.multiple_of(own * half, half), half), :]
        gram_sent[...] = acc[pl.ds(pl.multiple_of((1 - own) * half, half), half), :]


def sketch_call(me, e, signs, rows_all):
    rows, d = e.shape
    k = signs.shape[1]
    block = 256
    return pl.pallas_call(
        functools.partial(sketch_kernel, 1.0 / math.sqrt(d), 1.0 / rows_all),
        grid_spec=pltpu.PrefetchScalarGridSpec(
            num_scalar_prefetch=1,
            grid=(rows // block,),
            in_specs=[
                pl.BlockSpec((block, d), lambda i, me: (i, 0)),
                pl.BlockSpec((d, k), lambda i, me: (0, 0), pipeline_mode=pl.Buffered(1)),
            ],
            out_specs=[
                pl.BlockSpec((block, k), lambda i, me: (i, 0)),
                pl.BlockSpec((k, block), lambda i, me: (0, i)),
                pl.BlockSpec((k // 2, k), lambda i, me: (0, 0)),
                pl.BlockSpec((k // 2, k), lambda i, me: (0, 0)),
            ],
            scratch_shapes=[
                pltpu.VMEM((d, k), jnp.bfloat16),
                pltpu.VMEM((k, k), jnp.float32),
                pltpu.VMEM((k, k), jnp.float32),
            ],
        ),
        out_shape=[
            jax.ShapeDtypeStruct((rows, k), jnp.float32),
            jax.ShapeDtypeStruct((k, rows), jnp.bfloat16),
            jax.ShapeDtypeStruct((k // 2, k), jnp.float32),
            jax.ShapeDtypeStruct((k // 2, k), jnp.float32),
        ],
        compiler_params=pltpu.CompilerParams(vmem_limit_bytes=40 * MIB),
        cost_estimate=pl.CostEstimate(flops=2 * rows * d * k, bytes_accessed=rows * d * 2 + d * k * 4, transcendentals=0),
        name="sketch",
    )(me, e, signs)


def cross_kernel(scale, groups, info, e, rounded_t, *outs):
    step = pl.program_id(0)
    value = dot(rounded_t[...], e[...]) * scale
    size = value.shape[0] // groups
    per = 4 // len(outs)
    for o, out in enumerate(outs):

        @pl.when(step // per == o)
        def _(out=out):
            for g in range(groups):
                at = pl.multiple_of((info[4] ^ g) * size, size)
                out[0, pl.ds(at, size), :] = value[g * size : (g + 1) * size]


def cross_call(info, e, rounded_t, scale, groups, width, n_outs):
    rows, d = e.shape
    k = rounded_t.shape[0]
    per = 4 // n_outs
    return pl.pallas_call(
        functools.partial(cross_kernel, scale, groups),
        grid_spec=pltpu.PrefetchScalarGridSpec(
            num_scalar_prefetch=1,
            grid=(4,),
            in_specs=[
                pl.BlockSpec((rows, width), lambda i, info: (0, info[i])),
                pl.BlockSpec((k, rows), lambda i, info: (0, 0), pipeline_mode=pl.Buffered(1)),
            ],
            out_specs=[
                pl.BlockSpec((1, k, width), lambda i, info, o=o: (jnp.clip(i - o * per, 0, per - 1), 0, 0))
                for o in range(n_outs)
            ],
        ),
        out_shape=[jax.ShapeDtypeStruct((per, k, width), jnp.float32)] * n_outs,
        compiler_params=pltpu.CompilerParams(vmem_limit_bytes=40 * MIB),
        cost_estimate=pl.CostEstimate(flops=2 * rows * k * width * 4, bytes_accessed=rows * width * 8, transcendentals=0),
        name="cross",
    )(info, e, rounded_t)


def factor_kernel(me, kept, got, triangle, high, low, work):
    k = triangle.shape[0]
    half = k // 2
    own = me[0] & 1
    work[pl.ds(pl.multiple_of(own * half, half), half), :k] = kept[...]
    work[pl.ds(pl.multiple_of((1 - own) * half, half), half), :k] = got[...]
    b = 64
    rows_k = lax.broadcasted_iota(jnp.int32, (k, k), 0)
    cols_k = lax.broadcasted_iota(jnp.int32, (k, k), 1)
    work[:, k:] = jnp.where(rows_k == cols_k, 1.0, 0.0)
    lane = lax.broadcasted_iota(jnp.int32, (8, 2 * b), 1)
    sub = lax.broadcasted_iota(jnp.int32, (8, 2 * b), 0)
    for n in range(k // b):
        first = (n % 2) * b
        pair = (n // 2) * 2 * b
        own_lanes = (lane >= first) & (lane < first + b)
        w = []
        for v in range(b // 8):
            a = work[n * b + 8 * v : n * b + 8 * v + 8, pair : pair + 2 * b]
            ident = jnp.where(lane == (b - first) + 8 * v + sub, 1.0, 0.0)
            w.append(jnp.where(own_lanes, a, ident))
        for j in range(b):
            v0, r = divmod(j, 8)
            row = jnp.broadcast_to(w[v0][r : r + 1, :], (8, 2 * b))
            pivot = jnp.broadcast_to(row[:, first + j : first + j + 1], (8, 2 * b))
            row = row * (1.0 / pivot)
            for v in range(v0, b // 8):
                col = jnp.broadcast_to(w[v][:, first + j : first + j + 1], (8, 2 * b))
                if v == v0:
                    if r == 7:
                        continue
                    col = jnp.where(sub > r, col, 0.0)
                w[v] = w[v] - col * row
        inv = []
        for v in range(b // 8):
            diag = jnp.sum(jnp.where(lane == first + 8 * v + sub, w[v], 0.0), axis=1, keepdims=True)
            moved = pltpu.roll(w[v], b, 1)
            inv.append(jnp.where(own_lanes, moved * (1.0 / jnp.sqrt(diag)), 0.0))
        inv = jnp.concatenate(inv, axis=0)
        y = lax.dot_general(
            inv, work[pair : pair + 2 * b, :], (((1,), (0,)), ((), ())),
            precision=lax.Precision.HIGHEST, preferred_element_type=jnp.float32,
        )
        r_rows, i_rows = y[:, :k], y[:, k:]
        at = lax.broadcasted_iota(jnp.int32, (b, k), 0) + n * b
        to = lax.broadcasted_iota(jnp.int32, (b, k), 1)
        triangle[n * b : (n + 1) * b, :] = jnp.where(to >= at, r_rows, 0.0)
        i_rows = jnp.where(to <= at, i_rows, 0.0)
        i_high, i_low = split(i_rows)
        high[n * b : (n + 1) * b, :] = i_high
        low[n * b : (n + 1) * b, :] = i_low
        if (n + 1) * b < k:
            later = jnp.where(to >= (n + 1) * b, r_rows, 0.0)
            work[...] -= lax.dot_general(
                later, y, (((0,), (0,)), ((), ())),
                precision=lax.Precision.HIGHEST, preferred_element_type=jnp.float32,
            )


def factor_call(me, kept, got):
    k = kept.shape[1]
    whole = lambda shape: pl.BlockSpec(shape, lambda i, me: (0, 0))
    return pl.pallas_call(
        factor_kernel,
        grid_spec=pltpu.PrefetchScalarGridSpec(
            num_scalar_prefetch=1,
            grid=(1,),
            in_specs=[whole((k // 2, k))] * 2,
            out_specs=[whole((k, k))] * 3,
            scratch_shapes=[pltpu.VMEM((k, 2 * k), jnp.float32)],
        ),
        out_shape=[
            jax.ShapeDtypeStruct((k, k), jnp.float32),
            jax.ShapeDtypeStruct((k, k), jnp.bfloat16),
            jax.ShapeDtypeStruct((k, k), jnp.bfloat16),
        ],
        compiler_params=pltpu.CompilerParams(vmem_limit_bytes=24 * MIB),
        cost_estimate=pl.CostEstimate(flops=10**10, bytes_accessed=k * k * 8, transcendentals=0),
        name="factor",
    )(me, kept, got)


def basis_kernel(sketch, high, low, out):
    s_high, s_low = split(sketch[...])
    right = ((1,), (1,))
    out[...] = (
        dot(s_high, high[...], right) + (dot(s_high, low[...], right) + dot(s_low, high[...], right))
    ).astype(out.dtype)


def basis_call(sketch, high, low):
    rows, k = sketch.shape
    block = 512
    whole = pl.BlockSpec((k, k), lambda i: (0, 0))
    return pl.pallas_call(
        basis_kernel,
        grid=(rows // block,),
        in_specs=[pl.BlockSpec((block, k), lambda i: (i, 0)), whole, whole],
        out_specs=pl.BlockSpec((block, k), lambda i: (i, 0)),
        out_shape=jax.ShapeDtypeStruct((rows, k), jnp.bfloat16),
        compiler_params=pltpu.CompilerParams(vmem_limit_bytes=24 * MIB),
        cost_estimate=pl.CostEstimate(flops=6 * rows * k * k, bytes_accessed=rows * k * 6, transcendentals=0),
        name="basis",
    )(sketch, high, low)


def project_kernel(groups, info, high, low, *refs):
    *blocks, out = refs[-5:]
    which = pl.program_id(0)
    for n, block in enumerate(blocks):

        @pl.when(which == n)
        def _(n=n, block=block):
            size = block.shape[1] // groups
            order = info[8 + n // 2]
            value = jnp.concatenate(
                [block[0, pl.ds(pl.multiple_of((order ^ g) * size, size), size), :] for g in range(groups)], axis=0
            )
            c_high, c_low = split(value)
            out[...] = dot(high[...], c_high) + (dot(high[...], c_low) + dot(low[...], c_high))


def project_call(info, high, low, blocks, groups, d, before):
    per, k, width = blocks[0].shape
    whole = pl.BlockSpec((k, k), lambda i, j, info: (0, 0))
    pick = lambda n: lambda i, j, info: (jnp.where(i < n, 0, jnp.where(i > n, per - 1, j)), 0, 0)
    extra = [] if before is None else [before]
    return pl.pallas_call(
        functools.partial(project_kernel, groups),
        grid_spec=pltpu.PrefetchScalarGridSpec(
            num_scalar_prefetch=1,
            grid=(4, per),
            in_specs=[whole, whole]
            + [pl.BlockSpec(memory_space=pl.ANY)] * len(extra)
            + [pl.BlockSpec((1, k, width), pick(n)) for n in range(4)],
            out_specs=pl.BlockSpec((k, width), lambda i, j, info: (0, info[i * per + j])),
        ),
        out_shape=jax.ShapeDtypeStruct((k, d), jnp.float32),
        input_output_aliases={3: 0} if extra else {},
        compiler_params=pltpu.CompilerParams(vmem_limit_bytes=24 * MIB),
        cost_estimate=pl.CostEstimate(flops=6 * k * k * width * 8, bytes_accessed=k * width * 64, transcendentals=0),
        name="project",
    )(info, high, low, *extra, *blocks)


def solution(mesh):
    n_devices = math.prod(mesh.shape.values())
    orders = orders_of(n_devices)
    steps = len(orders[0])
    groups = 1 << (steps - 2)
    pairs = [(i, i ^ 1) for i in range(n_devices)]
    swaps = [[(i, i ^ (1 << orders[i & 1][s])) for i in range(n_devices)] for s in range(steps)]

    def with_pair(a):
        return lax.ppermute(a, AXES, pairs)

    def swap(a, s):
        return lax.ppermute(a, AXES, swaps[s])

    def shards(e, signs):
        rows_all = e.shape[0] * n_devices
        d = e.shape[1]
        width = d // (8 * CHUNKS)
        me = lax.axis_index(AXES).astype(jnp.int32)
        own = me & 1
        place = [bits_of(me, o[:2]) for o in orders]
        rest = [bits_of(me, o[2:]) for o in orders]
        mine = lambda pair: jnp.where(own == 0, pair[0], pair[1])
        other = lambda pair: jnp.where(own == 0, pair[1], pair[0])

        def blocks_at(chunk, region, at):
            return [(chunk * 2 + region) * 4 + (at ^ n) for n in range(4)]

        def vector(*values):
            return jnp.stack([jnp.asarray(v, jnp.int32) for v in values])

        me1 = me[None]
        sketch, rounded_t, gram_sent, gram = sketch_call(me1, e, signs, rows_all)

        gram = gram + with_pair(gram_sent)
        for s in range(steps):
            gram = gram + swap(gram, s)
        triangle, high, low = factor_call(me1, gram, with_pair(gram))

        projected = None
        for chunk in range(CHUNKS):
            own_at = blocks_at(chunk, own, mine(place))
            other_at = blocks_at(chunk, 1 - own, other(place))
            scale = 1.0 / math.sqrt(rows_all)
            (sent,) = cross_call(vector(*other_at, other(rest)), e, rounded_t, scale, groups, width, 1)
            kept, first = cross_call(vector(*own_at, mine(rest)), e, rounded_t, scale, groups, width, 2)
            got = with_pair(sent)
            r = swap(first + got[2:], 0)
            kept = kept + got[:2]
            r2 = swap(kept[1] + r[1], 1)
            a = kept[0] + r[0] + r2
            for s in range(2, steps):
                half = a.shape[0] // 2
                a = a[:half] + swap(a[half:], s)
            for s in range(steps - 1, 1, -1):
                a = jnp.concatenate([a, swap(a, s)], axis=0)
            a = jnp.stack([a, swap(a, 1)])
            a2 = swap(a, 0)
            b = with_pair(a)
            b2 = with_pair(a2)
            info = vector(*own_at, *other_at, mine(rest), other(rest))
            projected = project_call(info, high, low, [a, a2, b, b2], groups, d, projected)
        basis = basis_call(sketch, high, low)
        return triangle, basis, projected

    return jax.shard_map(
        shards,
        mesh=mesh,
        in_specs=(P(AXES, None), P()),
        out_specs=(P(), P(AXES, None), P()),
        check_vma=False,
    )
```

```python
import functools
import math

import jax
import jax.numpy as jnp
from jax import lax
from jax.experimental import pallas as pl
from jax.experimental.pallas import tpu as pltpu
from jax.sharding import PartitionSpec as P

AXES = ("gx", "gy")
CHUNKS = 2
MIB = 1 << 20


def dot(a, b, dims=((1,), (0,))):
    return lax.dot_general(a, b, (dims, ((), ())), preferred_element_type=jnp.float32)


def split(a):
    high = a.astype(jnp.bfloat16)
    return high, (a - high.astype(jnp.float32)).astype(jnp.bfloat16)


def orders_of(n_devices):
    bits = list(range(1, n_devices.bit_length() - 1))
    swapped = bits[:]
    for i in range(0, len(bits) - 1, 2):
        swapped[i], swapped[i + 1] = bits[i + 1], bits[i]
    return bits, swapped


def bits_of(me, order):
    value = jnp.int32(0)
    for b in order:
        value = value * 2 + ((me >> b) & 1)
    return value


def in_vmem(*shape_dtype):
    return pltpu.VMEM(*shape_dtype)


def pinned(*arrays):
    return [pltpu.with_memory_space_constraint(a, pltpu.VMEM) for a in arrays]


VMEM_SPEC = pl.BlockSpec(memory_space=pltpu.VMEM)
SMEM_SPEC = pl.BlockSpec(memory_space=pltpu.SMEM)
ANY_SPEC = pl.BlockSpec(memory_space=pl.ANY)


def front_kernel(in_scale, gram_scale, me, e, signs, e_kept, sketch, rounded_t, gram_sent, gram_kept, s32, s16, acc, sem):
    rows = e.shape[0]
    n = sem.shape[0] - 1
    block = rows // n
    signs_copy = pltpu.make_async_copy(signs, s32, sem.at[n])
    signs_copy.start()

    def rows_copy(i):
        at = pl.ds(pl.multiple_of(i * block, block), block)
        return pltpu.make_async_copy(e.at[at], e_kept.at[at], sem.at[i])

    for i in range(n):
        rows_copy(i).start()
    signs_copy.wait()
    s16[...] = s32[...].astype(jnp.bfloat16)

    def step(i, carry):
        rows_copy(i).wait()
        at = pl.ds(pl.multiple_of(i * block, block), block)
        sk = dot(e_kept[at, :], s16[...]) * in_scale
        sketch[at, :] = sk
        rounded_t[:, at] = sk.astype(jnp.bfloat16).T
        return carry

    lax.fori_loop(0, n, step, 0)
    high, low = split(sketch[...])
    acc[...] = dot(rounded_t[...], low)
    acc[...] = (dot(rounded_t[...], high) + (acc[...] + acc[...].T)) * gram_scale
    half = acc.shape[0] // 2
    own = me[0] & 1
    gram_kept[...] = acc[pl.ds(pl.multiple_of(own * half, half), half), :]
    gram_sent[...] = acc[pl.ds(pl.multiple_of((1 - own) * half, half), half), :]


def front_call(me, e, signs, rows_all):
    rows, d = e.shape
    k = signs.shape[1]
    copies = 4
    return pl.pallas_call(
        functools.partial(front_kernel, 1.0 / math.sqrt(d), 1.0 / rows_all),
        in_specs=[SMEM_SPEC, ANY_SPEC, ANY_SPEC],
        out_specs=[VMEM_SPEC] * 5,
        out_shape=[
            in_vmem((rows, d), e.dtype),
            in_vmem((rows, k), jnp.float32),
            in_vmem((k, rows), jnp.bfloat16),
            in_vmem((k // 2, k), jnp.float32),
            in_vmem((k // 2, k), jnp.float32),
        ],
        scratch_shapes=[
            pltpu.VMEM((d, k), jnp.int32),
            pltpu.VMEM((d, k), jnp.bfloat16),
            pltpu.VMEM((k, k), jnp.float32),
            pltpu.SemaphoreType.DMA((copies + 1,)),
        ],
        compiler_params=pltpu.CompilerParams(vmem_limit_bytes=24 * MIB),
        cost_estimate=pl.CostEstimate(flops=2 * rows * d * k, bytes_accessed=rows * d * 2 + d * k * 4, transcendentals=0),
        name="front",
    )(me, e, pltpu.with_memory_space_constraint(signs, pltpu.HBM))


def cross_kernel(scale, groups, width, info, e, rounded_t, *outs):
    k = rounded_t.shape[0]
    size = k // groups
    per = 4 // len(outs)
    for n in range(4):
        at = pl.ds(pl.multiple_of(info[n] * width, width), width)
        value = dot(rounded_t[...], e[:, at]) * scale
        for g in range(groups):
            to = pl.multiple_of((n % per) * k + (info[4] ^ g) * size, size)
            outs[n // per][pl.ds(to, size), :] = value[g * size : (g + 1) * size]


def cross_call(info, e, rounded_t, scale, groups, width, n_outs):
    rows, d = e.shape
    k = rounded_t.shape[0]
    return pl.pallas_call(
        functools.partial(cross_kernel, scale, groups, width),
        in_specs=[SMEM_SPEC, VMEM_SPEC, VMEM_SPEC],
        out_specs=[VMEM_SPEC] * n_outs,
        out_shape=[in_vmem((4 // n_outs * k, width), jnp.float32)] * n_outs,
        compiler_params=pltpu.CompilerParams(vmem_limit_bytes=16 * MIB),
        cost_estimate=pl.CostEstimate(flops=2 * rows * k * width * 4, bytes_accessed=0, transcendentals=0),
        name="cross",
    )(info, *pinned(e, rounded_t))


def factor_kernel(me, kept, got, triangle, high, low, work):
    k = triangle.shape[0]
    half = k // 2
    own = me[0] & 1
    work[pl.ds(pl.multiple_of(own * half, half), half), :k] = kept[...]
    work[pl.ds(pl.multiple_of((1 - own) * half, half), half), :k] = got[...]
    b = 64
    rows_k = lax.broadcasted_iota(jnp.int32, (k, k), 0)
    cols_k = lax.broadcasted_iota(jnp.int32, (k, k), 1)
    work[:, k:] = jnp.where(rows_k == cols_k, 1.0, 0.0)
    lane = lax.broadcasted_iota(jnp.int32, (8, 2 * b), 1)
    sub = lax.broadcasted_iota(jnp.int32, (8, 2 * b), 0)

    def over_lanes(a, at):
        return jnp.broadcast_to(a[:, at : at + 1], (8, 2 * b))

    for n in range(k // b):
        first = (n % 2) * b
        pair = (n // 2) * 2 * b
        own_lanes = (lane >= first) & (lane < first + b)
        w = []
        for v in range(b // 8):
            a = work[n * b + 8 * v : n * b + 8 * v + 8, pair : pair + 2 * b]
            ident = jnp.where(lane == (b - first) + 8 * v + sub, 1.0, 0.0)
            w.append(jnp.where(own_lanes, a, ident))
        inv = []
        for q in range(b // 8):
            at = first + 8 * q
            row = [jnp.broadcast_to(w[q][i : i + 1, :], (8, 2 * b)) for i in range(8)]
            s = {(i, j): over_lanes(row[i], at + j) for i in range(8) for j in range(i, 8)}
            factor = {}
            scaled = []
            for j in range(8):
                r = 1.0 / s[j, j]
                for i in range(j + 1, 8):
                    factor[i, j] = s[j, i] * r
                    for m in range(i, 8):
                        s[i, m] = s[i, m] - factor[i, j] * s[j, m]
                    row[i] = row[i] - factor[i, j] * row[j]
                scaled.append(row[j] * r)
            new, pivots = row[0], s[0, 0]
            for i in range(1, 8):
                new = jnp.where(sub == i, row[i], new)
                pivots = jnp.where(sub == i, s[i, i], pivots)
            for v in range(q + 1, b // 8):
                col = [over_lanes(w[v], at + j) for j in range(8)]
                for j in range(8):
                    for m in range(j + 1, 8):
                        col[m] = col[m] - col[j] * factor[m, j]
                t = [col[j] * scaled[j] for j in range(8)]
                w[v] = w[v] - (((t[0] + t[1]) + (t[2] + t[3])) + ((t[4] + t[5]) + (t[6] + t[7])))
            moved = pltpu.roll(new * (1.0 / jnp.sqrt(pivots)), b, 1)
            inv.append(jnp.where(own_lanes, moved, 0.0))
        inv = jnp.concatenate(inv, axis=0)
        y = lax.dot_general(
            inv, work[pair : pair + 2 * b, :], (((1,), (0,)), ((), ())),
            precision=lax.Precision.HIGHEST, preferred_element_type=jnp.float32,
        )
        r_rows, i_rows = y[:, :k], y[:, k:]
        at = lax.broadcasted_iota(jnp.int32, (b, k), 0) + n * b
        to = lax.broadcasted_iota(jnp.int32, (b, k), 1)
        triangle[n * b : (n + 1) * b, :] = jnp.where(to >= at, r_rows, 0.0)
        i_rows = jnp.where(to <= at, i_rows, 0.0)
        i_high, i_low = split(i_rows)
        high[n * b : (n + 1) * b, :] = i_high
        low[n * b : (n + 1) * b, :] = i_low
        if (n + 1) * b < k:
            later = jnp.where(to >= (n + 1) * b, r_rows, 0.0)
            work[...] -= lax.dot_general(
                later, y, (((0,), (0,)), ((), ())),
                precision=lax.Precision.HIGHEST, preferred_element_type=jnp.float32,
            )


def factor_call(me, kept, got):
    k = kept.shape[1]
    return pl.pallas_call(
        factor_kernel,
        in_specs=[SMEM_SPEC, VMEM_SPEC, VMEM_SPEC],
        out_specs=[VMEM_SPEC] * 3,
        out_shape=[
            jax.ShapeDtypeStruct((k, k), jnp.float32),
            in_vmem((k, k), jnp.bfloat16),
            in_vmem((k, k), jnp.bfloat16),
        ],
        scratch_shapes=[pltpu.VMEM((k, 2 * k), jnp.float32)],
        compiler_params=pltpu.CompilerParams(vmem_limit_bytes=16 * MIB),
        cost_estimate=pl.CostEstimate(flops=10**10, bytes_accessed=k * k * 8, transcendentals=0),
        name="factor",
    )(me, kept, got)


def basis_kernel(sketch, high, low, out):
    s_high, s_low = split(sketch[...])
    right = ((1,), (1,))
    out[...] = (
        dot(s_high, high[...], right) + (dot(s_high, low[...], right) + dot(s_low, high[...], right))
    ).astype(out.dtype)


def basis_call(sketch, high, low):
    rows, k = sketch.shape
    block = rows // 4
    return pl.pallas_call(
        basis_kernel,
        grid=(rows // block,),
        in_specs=[pl.BlockSpec((block, k), lambda i: (i, 0))] + [pl.BlockSpec((k, k), lambda i: (0, 0))] * 2,
        out_specs=pl.BlockSpec((block, k), lambda i: (i, 0)),
        out_shape=jax.ShapeDtypeStruct((rows, k), jnp.bfloat16),
        compiler_params=pltpu.CompilerParams(vmem_limit_bytes=16 * MIB),
        cost_estimate=pl.CostEstimate(flops=6 * rows * k * k, bytes_accessed=rows * k * 6, transcendentals=0),
        name="basis",
    )(sketch, high, low)


def project_kernel(groups, width, info, high, low, *refs):
    *blocks, out, value, sem = refs
    blocks = blocks[-4:]
    k = high.shape[0]
    size = k // groups
    copies = []
    for n in range(8):
        block, order = blocks[n // 2], info[8 + n // 4]
        c_high, c_low = split(
            jnp.concatenate(
                [
                    block[pl.ds(pl.multiple_of((n % 2) * k + (order ^ g) * size, size), size), :]
                    for g in range(groups)
                ],
                axis=0,
            )
        )
        value[n] = dot(high[...], c_high) + (dot(high[...], c_low) + dot(low[...], c_high))
        at = pl.ds(pl.multiple_of(info[n] * width, width), width)
        copies.append(pltpu.make_async_copy(value.at[n], out.at[:, at], sem.at[n]))
        copies[-1].start()
    for copy in copies:
        copy.wait()


def project_call(info, high, low, blocks, groups, d, before):
    k, width = high.shape[0], blocks[0].shape[1]
    extra = [] if before is None else [before]
    return pl.pallas_call(
        functools.partial(project_kernel, groups, width),
        in_specs=[SMEM_SPEC, VMEM_SPEC, VMEM_SPEC] + [ANY_SPEC] * len(extra) + [VMEM_SPEC] * 4,
        out_specs=ANY_SPEC,
        out_shape=jax.ShapeDtypeStruct((k, d), jnp.float32),
        input_output_aliases={3: 0} if extra else {},
        scratch_shapes=[pltpu.VMEM((8, k, width), jnp.float32), pltpu.SemaphoreType.DMA((8,))],
        compiler_params=pltpu.CompilerParams(vmem_limit_bytes=16 * MIB),
        cost_estimate=pl.CostEstimate(flops=6 * k * k * width * 8, bytes_accessed=k * width * 32, transcendentals=0),
        name="project",
    )(info, *pinned(high, low), *extra, *pinned(*blocks))


def solution(mesh):
    n_devices = math.prod(mesh.shape.values())
    orders = orders_of(n_devices)
    steps = len(orders[0])
    groups = 1 << (steps - 2)
    pairs = [(i, i ^ 1) for i in range(n_devices)]
    swaps = [[(i, i ^ (1 << orders[i & 1][s])) for i in range(n_devices)] for s in range(steps)]

    def with_pair(a):
        return lax.ppermute(a, AXES, pairs)

    def swap(a, s):
        return lax.ppermute(a, AXES, swaps[s])

    def join(*arrays):
        return arrays[0] if len(arrays) == 1 else jnp.concatenate(arrays, axis=0)

    def shards(e, signs):
        rows_all = e.shape[0] * n_devices
        d = e.shape[1]
        k = signs.shape[1]
        width = d // (8 * CHUNKS)
        scale = 1.0 / math.sqrt(rows_all)
        me = lax.axis_index(AXES).astype(jnp.int32)
        own = me & 1
        place = [bits_of(me, o[:2]) for o in orders]
        rest = [bits_of(me, o[2:]) for o in orders]
        mine = lambda pair: jnp.where(own == 0, pair[0], pair[1])
        other = lambda pair: jnp.where(own == 0, pair[1], pair[0])

        def blocks_at(chunk, region, at):
            return [(chunk * 2 + region) * 4 + (at ^ n) for n in range(4)]

        def vector(*values):
            return jnp.stack([jnp.asarray(v, jnp.int32) for v in values])

        me1 = me[None]
        e_kept, sketch, rounded_t, gram_sent, gram = front_call(me1, e, signs, rows_all)
        gram = gram + with_pair(gram_sent)

        stay, go, whole = [], [], []
        for chunk in range(CHUNKS):
            (sent,) = cross_call(
                vector(*blocks_at(chunk, 1 - own, other(place)), other(rest)), e_kept, rounded_t, scale, groups, width, 1
            )
            kept, first = cross_call(
                vector(*blocks_at(chunk, own, mine(place)), mine(rest)), e_kept, rounded_t, scale, groups, width, 2
            )
            got = with_pair(sent)
            stay.append(kept + got[: 2 * k])
            go.append(first + got[2 * k :])
            whole.append([gram] if chunk == 0 else [])
        for s in range(steps):
            for chunk in range(CHUNKS):
                r = swap(join(go[chunk], *whole[chunk]), s)
                n = stay[chunk].shape[0]
                a = stay[chunk] + r[:n]
                whole[chunk] = [g + r[n:] for g in whole[chunk]]
                stay[chunk], go[chunk] = a[: n // 2], a[n // 2 :]
                if s == steps - 1:
                    stay[chunk] = a
        triangle, high, low = factor_call(me1, whole[0][0], with_pair(whole[0][0]))
        last = []
        for s in range(steps - 1, -1, -1):
            for chunk in range(CHUNKS):
                r = swap(stay[chunk], s)
                if s:
                    stay[chunk] = join(stay[chunk], r)
                else:
                    last.append(r)
        basis = basis_call(sketch, high, low)
        projected = None
        for chunk in range(CHUNKS):
            blocks = [stay[chunk], last[chunk], with_pair(stay[chunk]), with_pair(last[chunk])]
            info = vector(
                *blocks_at(chunk, own, mine(place)), *blocks_at(chunk, 1 - own, other(place)), mine(rest), other(rest)
            )
            projected = project_call(info, high, low, blocks, groups, d, projected)
        return triangle, basis, projected

    return jax.shard_map(
        shards,
        mesh=mesh,
        in_specs=(P(AXES, None), P()),
        out_specs=(P(), P(AXES, None), P()),
        check_vma=False,
    )
```

```python
import functools
import math

import jax
import jax.numpy as jnp
from jax import lax
from jax.experimental import pallas as pl
from jax.experimental.pallas import tpu as pltpu
from jax.sharding import PartitionSpec as P

AXES = ("gx", "gy")
CHUNKS = 2
MIB = 1 << 20


def dot(a, b, dims=((1,), (0,))):
    return lax.dot_general(a, b, (dims, ((), ())), preferred_element_type=jnp.float32)


def split(a):
    high = a.astype(jnp.bfloat16)
    return high, (a - high.astype(jnp.float32)).astype(jnp.bfloat16)


def orders_of(n_devices):
    bits = list(range(1, n_devices.bit_length() - 1))
    swapped = bits[:]
    for i in range(0, len(bits) - 1, 2):
        swapped[i], swapped[i + 1] = bits[i + 1], bits[i]
    return bits, swapped


def bits_of(me, order):
    value = jnp.int32(0)
    for b in order:
        value = value * 2 + ((me >> b) & 1)
    return value

VMEM_SPEC = pl.BlockSpec(memory_space=pltpu.VMEM)
SMEM_SPEC = pl.BlockSpec(memory_space=pltpu.SMEM)
ANY_SPEC = pl.BlockSpec(memory_space=pl.ANY)


def pinned(*arrays):
    return [pltpu.with_memory_space_constraint(a, pltpu.VMEM) for a in arrays]


def front_kernel(
    in_scale, gram_scale, scale, groups, width,
    info, e, signs, sketch_out, rounded_out, gram_sent, gram_kept, sent, kept, first,
    e_kept, sketch, rounded_t, s32, s16, acc, pieces, sem, out_sem,
):
    rows = e.shape[0]
    k = rounded_t.shape[0]
    n = sem.shape[0] - 1
    block = rows // n
    signs_copy = pltpu.make_async_copy(signs, s32, sem.at[n])
    signs_copy.start()

    def rows_copy(i):
        at = pl.ds(pl.multiple_of(i * block, block), block)
        return pltpu.make_async_copy(e.at[at], e_kept.at[at], sem.at[i])

    for i in range(n):
        rows_copy(i).start()
    signs_copy.wait()
    s16[...] = s32[...].astype(jnp.bfloat16)

    def step(i, carry):
        rows_copy(i).wait()
        at = pl.ds(pl.multiple_of(i * block, block), block)
        sk = dot(e_kept[at, :], s16[...]) * in_scale
        sketch[at, :] = sk
        rounded_t[:, at] = sk.astype(jnp.bfloat16).T
        return carry

    lax.fori_loop(0, n, step, 0)
    outs = [
        pltpu.make_async_copy(sketch, sketch_out, out_sem.at[0]),
        pltpu.make_async_copy(rounded_t, rounded_out, out_sem.at[1]),
    ]
    for copy in outs:
        copy.start()
    high, low = split(sketch[...])
    acc[...] = dot(rounded_t[...], low)
    acc[...] = (dot(rounded_t[...], high) + (acc[...] + acc[...].T)) * gram_scale
    half = k // 2
    own = info[10] & 1
    gram_kept[...] = acc[pl.ds(pl.multiple_of(own * half, half), half), :]
    gram_sent[...] = acc[pl.ds(pl.multiple_of((1 - own) * half, half), half), :]
    size = k // groups
    for piece in range(8):
        at = pl.ds(pl.multiple_of(info[piece] * width, width), width)
        value = dot(rounded_t[...], e_kept[:, at]) * scale
        for g in range(groups):
            to = pl.multiple_of((info[8 + piece // 4] ^ g) * size, size)
            pieces[piece, pl.ds(to, size), :] = value[g * size : (g + 1) * size]
        if piece < 4:
            to = sent.at[pl.ds(piece * k, k)]
        else:
            to = (kept if piece < 6 else first).at[pl.ds(piece % 2 * k, k)]
        outs.append(pltpu.make_async_copy(pieces.at[piece], to, out_sem.at[2 + piece]))
        outs[-1].start()
    for copy in outs:
        copy.wait()


def front_call(info, e, signs, rows_all, groups, width):
    rows, d = e.shape
    k = signs.shape[1]
    copies = 4
    return pl.pallas_call(
        functools.partial(
            front_kernel, 1.0 / math.sqrt(d), 1.0 / rows_all, 1.0 / math.sqrt(rows_all), groups, width
        ),
        in_specs=[SMEM_SPEC, ANY_SPEC, ANY_SPEC],
        out_specs=[ANY_SPEC] * 2 + [VMEM_SPEC] * 2 + [ANY_SPEC] * 3,
        out_shape=[
            jax.ShapeDtypeStruct((rows, k), jnp.float32),
            jax.ShapeDtypeStruct((k, rows), jnp.bfloat16),
            jax.ShapeDtypeStruct((k // 2, k), jnp.float32),
            jax.ShapeDtypeStruct((k // 2, k), jnp.float32),
            jax.ShapeDtypeStruct((4 * k, width), jnp.float32),
            jax.ShapeDtypeStruct((2 * k, width), jnp.float32),
            jax.ShapeDtypeStruct((2 * k, width), jnp.float32),
        ],
        scratch_shapes=[
            pltpu.VMEM((rows, d), e.dtype),
            pltpu.VMEM((rows, k), jnp.float32),
            pltpu.VMEM((k, rows), jnp.bfloat16),
            pltpu.VMEM((d, k), jnp.int32),
            pltpu.VMEM((d, k), jnp.bfloat16),
            pltpu.VMEM((k, k), jnp.float32),
            pltpu.VMEM((8, k, width), jnp.float32),
            pltpu.SemaphoreType.DMA((copies + 1,)),
            pltpu.SemaphoreType.DMA((10,)),
        ],
        compiler_params=pltpu.CompilerParams(vmem_limit_bytes=56 * MIB),
        cost_estimate=pl.CostEstimate(flops=3 * rows * d * k, bytes_accessed=rows * d * 2 + d * k * 4, transcendentals=0),
        name="front",
    )(info, e, pltpu.with_memory_space_constraint(signs, pltpu.HBM))


def cross_kernel(scale, groups, info, e, rounded_t, sent, kept, first):
    step = pl.program_id(0)
    value = dot(rounded_t[...], e[...]) * scale
    size = value.shape[0] // groups
    order = info[8 + step // 4]

    def put(out):
        for g in range(groups):
            to = pl.multiple_of((order ^ g) * size, size)
            out[pl.ds(to, size), :] = value[g * size : (g + 1) * size]

    pl.when(step < 4)(lambda: put(sent))
    pl.when(step // 2 == 2)(lambda: put(kept))
    pl.when(step // 2 == 3)(lambda: put(first))


def cross_call(info, e, rounded_t, rows_all, groups, width):
    rows = e.shape[0]
    k = rounded_t.shape[0]
    return pl.pallas_call(
        functools.partial(cross_kernel, 1.0 / math.sqrt(rows_all), groups),
        grid_spec=pltpu.PrefetchScalarGridSpec(
            num_scalar_prefetch=1,
            grid=(8,),
            in_specs=[
                pl.BlockSpec((rows, width), lambda i, info: (0, info[i])),
                pl.BlockSpec((k, rows), lambda i, info: (0, 0), pipeline_mode=pl.Buffered(1)),
            ],
            out_specs=[
                pl.BlockSpec((k, width), lambda i, info, o=o, n=n: (jnp.clip(i - o, 0, n - 1), 0))
                for o, n in ((0, 4), (4, 2), (6, 2))
            ],
        ),
        out_shape=[jax.ShapeDtypeStruct((n * k, width), jnp.float32) for n in (4, 2, 2)],
        compiler_params=pltpu.CompilerParams(vmem_limit_bytes=16 * MIB),
        cost_estimate=pl.CostEstimate(flops=16 * rows * k * width, bytes_accessed=rows * width * 16, transcendentals=0),
        name="cross",
    )(info, pltpu.with_memory_space_constraint(e, pltpu.HBM), rounded_t)


def factor_kernel(part, info, *refs):
    triangle, high, low, work = refs[-4:]
    half, k = triangle.shape
    b = 64
    if part == 0:
        kept, got = refs[:2]
        own = info[10] & 1
        work[pl.ds(pl.multiple_of(own * half, half), half), :k] = kept[...]
        work[pl.ds(pl.multiple_of((1 - own) * half, half), half), :k] = got[...]
        rows_k = lax.broadcasted_iota(jnp.int32, (k, k), 0)
        cols_k = lax.broadcasted_iota(jnp.int32, (k, k), 1)
        work[:, k:] = jnp.where(rows_k == cols_k, 1.0, 0.0)
    else:
        work[...] = refs[0][...]
    lane = lax.broadcasted_iota(jnp.int32, (8, 2 * b), 1)
    sub = lax.broadcasted_iota(jnp.int32, (8, 2 * b), 0)

    def over_lanes(a, at):
        return jnp.broadcast_to(a[:, at : at + 1], (8, 2 * b))

    for n in range(part * (half // b), (part + 1) * (half // b)):
        put = slice(n * b - part * half, (n + 1) * b - part * half)
        first = (n % 2) * b
        pair = (n // 2) * 2 * b
        own_lanes = (lane >= first) & (lane < first + b)
        w = []
        for v in range(b // 8):
            a = work[n * b + 8 * v : n * b + 8 * v + 8, pair : pair + 2 * b]
            ident = jnp.where(lane == (b - first) + 8 * v + sub, 1.0, 0.0)
            w.append(jnp.where(own_lanes, a, ident))
        inv = []
        for q in range(b // 8):
            at = first + 8 * q
            row = [jnp.broadcast_to(w[q][i : i + 1, :], (8, 2 * b)) for i in range(8)]
            s = {(i, j): over_lanes(row[i], at + j) for i in range(8) for j in range(i, 8)}
            factor = {}
            scaled = []
            for j in range(8):
                r = 1.0 / s[j, j]
                for i in range(j + 1, 8):
                    factor[i, j] = s[j, i] * r
                    for m in range(i, 8):
                        s[i, m] = s[i, m] - factor[i, j] * s[j, m]
                    row[i] = row[i] - factor[i, j] * row[j]
                scaled.append(row[j] * r)
            new, pivots = row[0], s[0, 0]
            for i in range(1, 8):
                new = jnp.where(sub == i, row[i], new)
                pivots = jnp.where(sub == i, s[i, i], pivots)
            for v in range(q + 1, b // 8):
                col = [over_lanes(w[v], at + j) for j in range(8)]
                for j in range(8):
                    for m in range(j + 1, 8):
                        col[m] = col[m] - col[j] * factor[m, j]
                t = [col[j] * scaled[j] for j in range(8)]
                w[v] = w[v] - (((t[0] + t[1]) + (t[2] + t[3])) + ((t[4] + t[5]) + (t[6] + t[7])))
            moved = pltpu.roll(new * (1.0 / jnp.sqrt(pivots)), b, 1)
            inv.append(jnp.where(own_lanes, moved, 0.0))
        inv = jnp.concatenate(inv, axis=0)
        y = lax.dot_general(
            inv, work[pair : pair + 2 * b, :], (((1,), (0,)), ((), ())),
            precision=lax.Precision.HIGHEST, preferred_element_type=jnp.float32,
        )
        r_rows, i_rows = y[:, :k], y[:, k:]
        at = lax.broadcasted_iota(jnp.int32, (b, k), 0) + n * b
        to = lax.broadcasted_iota(jnp.int32, (b, k), 1)
        triangle[put, :] = jnp.where(to >= at, r_rows, 0.0)
        i_rows = jnp.where(to <= at, i_rows, 0.0)
        i_high, i_low = split(i_rows)
        high[put, :] = i_high
        low[put, :] = i_low
        if (n + 1) * b < k:
            later = jnp.where(to >= (n + 1) * b, r_rows, 0.0)
            work[...] -= lax.dot_general(
                later, y, (((0,), (0,)), ((), ())),
                precision=lax.Precision.HIGHEST, preferred_element_type=jnp.float32,
            )


def factor_call(part, info, *inputs):
    k = inputs[0].shape[0] * (2 - part)
    return pl.pallas_call(
        functools.partial(factor_kernel, part),
        in_specs=[SMEM_SPEC] + [VMEM_SPEC] * len(inputs),
        out_specs=[VMEM_SPEC] * 4,
        out_shape=[
            jax.ShapeDtypeStruct((k // 2, k), jnp.float32),
            jax.ShapeDtypeStruct((k // 2, k), jnp.bfloat16),
            jax.ShapeDtypeStruct((k // 2, k), jnp.bfloat16),
            jax.ShapeDtypeStruct((k, 2 * k), jnp.float32),
        ],
        compiler_params=pltpu.CompilerParams(vmem_limit_bytes=16 * MIB),
        cost_estimate=pl.CostEstimate(flops=5 * 10**9, bytes_accessed=k * k * 8, transcendentals=0),
        name="factor",
    )(info, *inputs)


def basis_kernel(sketch, high, low, out):
    s_high, s_low = split(sketch[...])
    right = ((1,), (1,))
    out[...] = (
        dot(s_high, high[...], right) + (dot(s_high, low[...], right) + dot(s_low, high[...], right))
    ).astype(out.dtype)


def basis_call(sketch, high, low):
    rows, k = sketch.shape
    block = rows // 4
    return pl.pallas_call(
        basis_kernel,
        grid=(rows // block,),
        in_specs=[pl.BlockSpec((block, k), lambda i: (i, 0))] + [pl.BlockSpec((k, k), lambda i: (0, 0))] * 2,
        out_specs=pl.BlockSpec((block, k), lambda i: (i, 0)),
        out_shape=jax.ShapeDtypeStruct((rows, k), jnp.bfloat16),
        compiler_params=pltpu.CompilerParams(vmem_limit_bytes=16 * MIB),
        cost_estimate=pl.CostEstimate(flops=6 * rows * k * k, bytes_accessed=rows * k * 6, transcendentals=0),
        name="basis",
    )(sketch, high, low)


def project_kernel(groups, width, info, high, low, *refs):
    *blocks, out, value, sem = refs
    blocks = blocks[-4:]
    k = high.shape[0]
    size = k // groups
    copies = []
    for n in range(8):
        block, order = blocks[n // 2], info[8 + n // 4]
        c_high, c_low = split(
            jnp.concatenate(
                [
                    block[pl.ds(pl.multiple_of((n % 2) * k + (order ^ g) * size, size), size), :]
                    for g in range(groups)
                ],
                axis=0,
            )
        )
        value[n] = dot(high[...], c_high) + (dot(high[...], c_low) + dot(low[...], c_high))
        at = pl.ds(pl.multiple_of(info[n] * width, width), width)
        copies.append(pltpu.make_async_copy(value.at[n], out.at[:, at], sem.at[n]))
        copies[-1].start()
    for copy in copies:
        copy.wait()


def project_call(info, high, low, blocks, groups, d, before):
    k, width = high.shape[0], blocks[0].shape[1]
    extra = [] if before is None else [before]
    return pl.pallas_call(
        functools.partial(project_kernel, groups, width),
        in_specs=[SMEM_SPEC, VMEM_SPEC, VMEM_SPEC] + [ANY_SPEC] * len(extra) + [VMEM_SPEC] * 4,
        out_specs=ANY_SPEC,
        out_shape=jax.ShapeDtypeStruct((k, d), jnp.float32),
        input_output_aliases={3: 0} if extra else {},
        scratch_shapes=[pltpu.VMEM((8, k, width), jnp.float32), pltpu.SemaphoreType.DMA((8,))],
        compiler_params=pltpu.CompilerParams(vmem_limit_bytes=16 * MIB),
        cost_estimate=pl.CostEstimate(flops=6 * k * k * width * 8, bytes_accessed=k * width * 32, transcendentals=0),
        name="project",
    )(info, *pinned(high, low), *extra, *pinned(*blocks))


def solution(mesh):
    n_devices = math.prod(mesh.shape.values())
    orders = orders_of(n_devices)
    steps = len(orders[0])
    groups = 1 << (steps - 2)
    pairs = [(i, i ^ 1) for i in range(n_devices)]
    swaps = [[(i, i ^ (1 << orders[i & 1][s])) for i in range(n_devices)] for s in range(steps)]

    def with_pair(a):
        return lax.ppermute(a, AXES, pairs)

    def swap(a, s):
        return lax.ppermute(a, AXES, swaps[s])

    def join(*arrays):
        return arrays[0] if len(arrays) == 1 else jnp.concatenate(arrays, axis=0)

    def shards(e, signs):
        rows_all = e.shape[0] * n_devices
        d = e.shape[1]
        k = signs.shape[1]
        width = d // (8 * CHUNKS)
        me = lax.axis_index(AXES).astype(jnp.int32)
        own = me & 1
        place = [bits_of(me, o[:2]) for o in orders]
        rest = [bits_of(me, o[2:]) for o in orders]
        mine = lambda pair: jnp.where(own == 0, pair[0], pair[1])
        other = lambda pair: jnp.where(own == 0, pair[1], pair[0])

        def info_of(chunk):
            at = [(chunk * 2 + 1 - own) * 4 + (other(place) ^ n) for n in range(4)]
            at += [(chunk * 2 + own) * 4 + (mine(place) ^ n) for n in range(4)]
            return jnp.stack(at + [other(rest), mine(rest), me])

        infos = [info_of(chunk) for chunk in range(CHUNKS)]
        last = [me]

        def in_turn(a):
            a, _ = lax.optimization_barrier((a, last[0]))
            last[0] = a
            return a

        sketch, rounded_t, gram_sent, gram, sent, kept, first = front_call(infos[0], e, signs, rows_all, groups, width)
        got, gram_got = with_pair(sent), with_pair(gram_sent)
        gram = gram + gram_got
        stay, go = [kept + got[: 2 * k], None], [in_turn(join(first + got[2 * k :], gram)), None]
        part = {0: swap(go[0], 0)}
        sent, kept, first = cross_call(infos[1], e, in_turn(rounded_t), rows_all, groups, width)
        got = with_pair(in_turn(sent))
        stay[1], go[1] = kept + got[: 2 * k], first + got[2 * k :]

        def halve(chunk, s):
            nonlocal gram
            r = part[chunk]
            n = stay[chunk].shape[0]
            a = stay[chunk] + r[:n]
            if chunk == 0:
                gram = gram + r[n:]
            if s == steps - 1:
                stay[chunk] = in_turn(a)
                return
            stay[chunk] = a[: n // 2]
            send = a[n // 2 :]
            part[chunk] = swap(in_turn(join(send, gram) if chunk == 0 else send), s + 1)

        def double(chunk, s):
            part[chunk] = swap(stay[chunk], s)

        def joined(chunk):
            stay[chunk] = in_turn(join(stay[chunk], part[chunk]))

        S = steps
        halve(0, 0)
        part[1] = swap(in_turn(go[1]), 0)
        for s in range(1, S):
            halve(0, s)
        double(0, S - 1)
        gram_got = with_pair(gram)
        down = list(range(S - 1, 0, -1))
        for i in range(max(S, len(down))):
            if i < S:
                halve(1, i)
            if i < len(down):
                joined(0)
                double(0, down[i] - 1)
        double(1, S - 1)
        triangle_a, high_a, low_a, work = factor_call(0, infos[0], in_turn(gram), gram_got)
        for s in down[:-1]:
            joined(1)
            double(1, s - 1)
        far = [None, None]
        far[0] = in_turn(part[0])
        from_pair = [[with_pair(stay[0]), with_pair(far[0])], None]
        joined(1)
        double(1, 0)
        pair_stay = with_pair(stay[1])
        triangle_b, high_b, low_b, _ = factor_call(1, infos[0], in_turn(work))
        triangle = join(triangle_a, triangle_b)
        high, low = in_turn(join(high_a, high_b)), join(low_a, low_b)
        basis = in_turn(basis_call(sketch, high, low))
        projected = in_turn(project_call(infos[0], high, low, [*from_pair[0], stay[0], far[0]], groups, d, None))
        far[1], projected = lax.optimization_barrier((part[1], projected))
        blocks = [pair_stay, with_pair(far[1]), stay[1], far[1]]
        projected = project_call(infos[1], high, low, blocks, groups, d, projected)
        return triangle, basis, projected

    return jax.shard_map(
        shards,
        mesh=mesh,
        in_specs=(P(AXES, None), P()),
        out_specs=(P(), P(AXES, None), P()),
        check_vma=False,
    )
```

```python
import functools
import math

import jax
import jax.numpy as jnp
from jax import lax
from jax.experimental import pallas as pl
from jax.experimental.pallas import tpu as pltpu
from jax.sharding import PartitionSpec as P

AXES = ("gx", "gy")
CHUNKS = 2
MIB = 1 << 20


def dot(a, b, dims=((1,), (0,))):
    return lax.dot_general(a, b, (dims, ((), ())), preferred_element_type=jnp.float32)


def split(a):
    high = a.astype(jnp.bfloat16)
    return high, (a - high.astype(jnp.float32)).astype(jnp.bfloat16)


def orders_of(n_devices):
    bits = list(range(1, n_devices.bit_length() - 1))
    swapped = bits[:]
    for i in range(0, len(bits) - 1, 2):
        swapped[i], swapped[i + 1] = bits[i + 1], bits[i]
    return bits, swapped


def bits_of(me, order):
    value = jnp.int32(0)
    for b in order:
        value = value * 2 + ((me >> b) & 1)
    return value

VMEM_SPEC = pl.BlockSpec(memory_space=pltpu.VMEM)
SMEM_SPEC = pl.BlockSpec(memory_space=pltpu.SMEM)
ANY_SPEC = pl.BlockSpec(memory_space=pl.ANY)


def pinned(*arrays):
    return [pltpu.with_memory_space_constraint(a, pltpu.VMEM) for a in arrays]


def front_kernel(in_scale, gram_scale, scale, groups, width, info, e, signs, sketch_out, gram_sent, gram_kept, *refs):
    e_kept, sketch, rounded_t, s32, s16, acc, pieces, sem, out_sem = refs[-9:]
    chunk_outs = refs[:-9]
    rows = e.shape[0]
    k = rounded_t.shape[0]
    n = sem.shape[0] - 1
    block = rows // n
    signs_copy = pltpu.make_async_copy(signs, s32, sem.at[n])
    signs_copy.start()

    def rows_copy(i):
        at = pl.ds(pl.multiple_of(i * block, block), block)
        return pltpu.make_async_copy(e.at[at], e_kept.at[at], sem.at[i])

    for i in range(n):
        rows_copy(i).start()
    signs_copy.wait()
    s16[...] = s32[...].astype(jnp.bfloat16)

    def step(i, carry):
        rows_copy(i).wait()
        at = pl.ds(pl.multiple_of(i * block, block), block)
        sk = dot(e_kept[at, :], s16[...]) * in_scale
        sketch[at, :] = sk
        rounded_t[:, at] = sk.astype(jnp.bfloat16).T
        return carry

    lax.fori_loop(0, n, step, 0)
    outs = [pltpu.make_async_copy(sketch, sketch_out, out_sem.at[0])]
    outs[0].start()
    high, low = split(sketch[...])
    acc[...] = dot(rounded_t[...], low)
    acc[...] = (dot(rounded_t[...], high) + (acc[...] + acc[...].T)) * gram_scale
    half = k // 2
    own = info[10] & 1
    size = half // groups
    for g in range(groups):
        for to, region, order in ((gram_kept, own, info[9]), (gram_sent, 1 - own, info[8])):
            at = pl.multiple_of(region * half + g * size, size)
            to[pl.ds(pl.multiple_of((order ^ g) * size, size), size), :] = acc[pl.ds(at, size), :]
    size = k // groups
    for chunk in range(len(chunk_outs) // 3):
        sent, kept, first = chunk_outs[3 * chunk : 3 * chunk + 3]
        for piece in range(8):
            at = pl.ds(pl.multiple_of((info[piece] + 8 * chunk) * width, width), width)
            value = dot(rounded_t[...], e_kept[:, at]) * scale
            slot = 8 * chunk + piece
            for g in range(groups):
                to = pl.multiple_of((info[8 + piece // 4] ^ g) * size, size)
                pieces[slot, pl.ds(to, size), :] = value[g * size : (g + 1) * size]
            if piece < 4:
                to = sent.at[pl.ds(piece * k, k)]
            else:
                to = (kept if piece < 6 else first).at[pl.ds(piece % 2 * k, k)]
            outs.append(pltpu.make_async_copy(pieces.at[slot], to, out_sem.at[1 + slot]))
            outs[-1].start()
    for copy in outs:
        copy.wait()


def front_call(info, e, signs, rows_all, groups, width, chunks):
    rows, d = e.shape
    k = signs.shape[1]
    copies = 4
    return pl.pallas_call(
        functools.partial(
            front_kernel, 1.0 / math.sqrt(d), 1.0 / rows_all, 1.0 / math.sqrt(rows_all), groups, width
        ),
        in_specs=[SMEM_SPEC, ANY_SPEC, ANY_SPEC],
        out_specs=[ANY_SPEC] + [VMEM_SPEC] * 2 + [ANY_SPEC] * (3 * chunks),
        out_shape=[
            jax.ShapeDtypeStruct((rows, k), jnp.float32),
            jax.ShapeDtypeStruct((k // 2, k), jnp.float32),
            jax.ShapeDtypeStruct((k // 2, k), jnp.float32),
        ]
        + [jax.ShapeDtypeStruct((n * k, width), jnp.float32) for n in (4, 2, 2)] * chunks,
        scratch_shapes=[
            pltpu.VMEM((rows, d), e.dtype),
            pltpu.VMEM((rows, k), jnp.float32),
            pltpu.VMEM((k, rows), jnp.bfloat16),
            pltpu.VMEM((d, k), jnp.int32),
            pltpu.VMEM((d, k), jnp.bfloat16),
            pltpu.VMEM((k, k), jnp.float32),
            pltpu.VMEM((8 * chunks, k, width), jnp.float32),
            pltpu.SemaphoreType.DMA((copies + 1,)),
            pltpu.SemaphoreType.DMA((1 + 8 * chunks,)),
        ],
        compiler_params=pltpu.CompilerParams(vmem_limit_bytes=56 * MIB),
        cost_estimate=pl.CostEstimate(flops=4 * rows * d * k, bytes_accessed=rows * d * 2 + d * k * 4, transcendentals=0),
        name="front",
    )(info, e, pltpu.with_memory_space_constraint(signs, pltpu.HBM))


def factor_kernel(part, groups, info, *refs):
    triangle, high, low, work = refs[-4:]
    half, k = triangle.shape
    b = 64
    if part == 0:
        kept, got = refs[:2]
        own = info[10] & 1
        size = half // groups
        for g in range(groups):
            for rows, region, order in ((kept, own, info[9]), (got, 1 - own, info[8])):
                at = pl.ds(pl.multiple_of((order ^ g) * size, size), size)
                work[pl.ds(pl.multiple_of(region * half + g * size, size), size), :k] = rows[at, :]
        rows_k = lax.broadcasted_iota(jnp.int32, (k, k), 0)
        cols_k = lax.broadcasted_iota(jnp.int32, (k, k), 1)
        work[:, k:] = jnp.where(rows_k == cols_k, 1.0, 0.0)
    else:
        work[...] = refs[0][...]
    lane = lax.broadcasted_iota(jnp.int32, (8, 2 * b), 1)
    sub = lax.broadcasted_iota(jnp.int32, (8, 2 * b), 0)

    def over_lanes(a, at):
        return jnp.broadcast_to(a[:, at : at + 1], (8, 2 * b))

    for n in range(part * (half // b), (part + 1) * (half // b)):
        put = slice(n * b - part * half, (n + 1) * b - part * half)
        first = (n % 2) * b
        pair = (n // 2) * 2 * b
        own_lanes = (lane >= first) & (lane < first + b)
        w = []
        for v in range(b // 8):
            a = work[n * b + 8 * v : n * b + 8 * v + 8, pair : pair + 2 * b]
            ident = jnp.where(lane == (b - first) + 8 * v + sub, 1.0, 0.0)
            w.append(jnp.where(own_lanes, a, ident))
        inv = []
        for q in range(b // 8):
            at = first + 8 * q
            row = [jnp.broadcast_to(w[q][i : i + 1, :], (8, 2 * b)) for i in range(8)]
            s = {(i, j): over_lanes(row[i], at + j) for i in range(8) for j in range(i, 8)}
            factor = {}
            scaled = []
            for j in range(8):
                r = 1.0 / s[j, j]
                for i in range(j + 1, 8):
                    factor[i, j] = s[j, i] * r
                    for m in range(i, 8):
                        s[i, m] = s[i, m] - factor[i, j] * s[j, m]
                    row[i] = row[i] - factor[i, j] * row[j]
                scaled.append(row[j] * r)
            new, pivots = row[0], s[0, 0]
            for i in range(1, 8):
                new = jnp.where(sub == i, row[i], new)
                pivots = jnp.where(sub == i, s[i, i], pivots)
            for v in range(q + 1, b // 8):
                col = [over_lanes(w[v], at + j) for j in range(8)]
                for j in range(8):
                    for m in range(j + 1, 8):
                        col[m] = col[m] - col[j] * factor[m, j]
                t = [col[j] * scaled[j] for j in range(8)]
                w[v] = w[v] - (((t[0] + t[1]) + (t[2] + t[3])) + ((t[4] + t[5]) + (t[6] + t[7])))
            moved = pltpu.roll(new * (1.0 / jnp.sqrt(pivots)), b, 1)
            inv.append(jnp.where(own_lanes, moved, 0.0))
        inv = jnp.concatenate(inv, axis=0)
        y = lax.dot_general(
            inv, work[pair : pair + 2 * b, :], (((1,), (0,)), ((), ())),
            precision=lax.Precision.HIGHEST, preferred_element_type=jnp.float32,
        )
        r_rows, i_rows = y[:, :k], y[:, k:]
        at = lax.broadcasted_iota(jnp.int32, (b, k), 0) + n * b
        to = lax.broadcasted_iota(jnp.int32, (b, k), 1)
        triangle[put, :] = jnp.where(to >= at, r_rows, 0.0)
        i_rows = jnp.where(to <= at, i_rows, 0.0)
        i_high, i_low = split(i_rows)
        high[put, :] = i_high
        low[put, :] = i_low
        if (n + 1) * b < k:
            later = jnp.where(to >= (n + 1) * b, r_rows, 0.0)
            work[...] -= lax.dot_general(
                later, y, (((0,), (0,)), ((), ())),
                precision=lax.Precision.HIGHEST, preferred_element_type=jnp.float32,
            )


def factor_call(part, groups, info, *inputs):
    k = inputs[0].shape[0] * (2 - part)
    return pl.pallas_call(
        functools.partial(factor_kernel, part, groups),
        in_specs=[SMEM_SPEC] + [VMEM_SPEC] * len(inputs),
        out_specs=[VMEM_SPEC] * 4,
        out_shape=[
            jax.ShapeDtypeStruct((k // 2, k), jnp.float32),
            jax.ShapeDtypeStruct((k // 2, k), jnp.bfloat16),
            jax.ShapeDtypeStruct((k // 2, k), jnp.bfloat16),
            jax.ShapeDtypeStruct((k, 2 * k), jnp.float32),
        ],
        compiler_params=pltpu.CompilerParams(vmem_limit_bytes=16 * MIB),
        cost_estimate=pl.CostEstimate(flops=5 * 10**9, bytes_accessed=k * k * 8, transcendentals=0),
        name="factor",
    )(info, *inputs)


def basis_kernel(sketch, high, low, out):
    s_high, s_low = split(sketch[...])
    right = ((1,), (1,))
    out[...] = (
        dot(s_high, high[...], right) + (dot(s_high, low[...], right) + dot(s_low, high[...], right))
    ).astype(out.dtype)


def basis_call(sketch, high, low):
    rows, k = sketch.shape
    block = rows // 4
    return pl.pallas_call(
        basis_kernel,
        grid=(rows // block,),
        in_specs=[pl.BlockSpec((block, k), lambda i: (i, 0))] + [pl.BlockSpec((k, k), lambda i: (0, 0))] * 2,
        out_specs=pl.BlockSpec((block, k), lambda i: (i, 0)),
        out_shape=jax.ShapeDtypeStruct((rows, k), jnp.bfloat16),
        compiler_params=pltpu.CompilerParams(vmem_limit_bytes=16 * MIB),
        cost_estimate=pl.CostEstimate(flops=6 * rows * k * k, bytes_accessed=rows * k * 6, transcendentals=0),
        name="basis",
    )(sketch, high, low)


def project_kernel(groups, width, chunk, info, high, low, *refs):
    *blocks, out, value, sem = refs
    blocks = blocks[-4:]
    k = high.shape[0]
    size = k // groups
    copies = []
    for n in range(8):
        block, order = blocks[n // 2], info[8 + n // 4]
        c_high, c_low = split(
            jnp.concatenate(
                [
                    block[pl.ds(pl.multiple_of((n % 2) * k + (order ^ g) * size, size), size), :]
                    for g in range(groups)
                ],
                axis=0,
            )
        )
        value[n] = dot(high[...], c_high) + (dot(high[...], c_low) + dot(low[...], c_high))
        at = pl.ds(pl.multiple_of((info[n] + 8 * chunk) * width, width), width)
        copies.append(pltpu.make_async_copy(value.at[n], out.at[:, at], sem.at[n]))
        copies[-1].start()
    for copy in copies:
        copy.wait()


def project_call(chunk, info, high, low, blocks, groups, d, before):
    k, width = high.shape[0], blocks[0].shape[1]
    extra = [] if before is None else [before]
    return pl.pallas_call(
        functools.partial(project_kernel, groups, width, chunk),
        in_specs=[SMEM_SPEC, VMEM_SPEC, VMEM_SPEC] + [ANY_SPEC] * len(extra) + [VMEM_SPEC] * 4,
        out_specs=ANY_SPEC,
        out_shape=jax.ShapeDtypeStruct((k, d), jnp.float32),
        input_output_aliases={3: 0} if extra else {},
        scratch_shapes=[pltpu.VMEM((8, k, width), jnp.float32), pltpu.SemaphoreType.DMA((8,))],
        compiler_params=pltpu.CompilerParams(vmem_limit_bytes=16 * MIB),
        cost_estimate=pl.CostEstimate(flops=6 * k * k * width * 8, bytes_accessed=k * width * 32, transcendentals=0),
        name="project",
    )(info, *pinned(high, low), *extra, *pinned(*blocks))


def solution(mesh):
    n_devices = math.prod(mesh.shape.values())
    orders = orders_of(n_devices)
    rest_bits = len(orders[0]) - 2
    groups = 1 << rest_bits

    def permutation(mask_of):
        return [(i, i ^ mask_of(i)) for i in range(n_devices)]

    def rest_mask(i, g):
        return sum(1 << b for t, b in enumerate(orders[i & 1][2:]) if g >> (rest_bits - 1 - t) & 1)

    pairs = permutation(lambda i: 1)
    swaps = [permutation(lambda i, s=s: 1 << orders[i & 1][s]) for s in range(2)]
    across = [permutation(lambda i, g=g: rest_mask(i, g)) for g in range(groups)]

    def with_pair(a):
        return lax.ppermute(a, AXES, pairs)

    def swap(a, s):
        return lax.ppermute(a, AXES, swaps[s])

    def join(*arrays):
        return arrays[0] if len(arrays) == 1 else jnp.concatenate(arrays, axis=0)

    def shards(e, signs):
        rows_all = e.shape[0] * n_devices
        d = e.shape[1]
        k = signs.shape[1]
        width = d // (8 * CHUNKS)
        me = lax.axis_index(AXES).astype(jnp.int32)
        own = me & 1
        place = [bits_of(me, o[:2]) for o in orders]
        rest = [bits_of(me, o[2:]) for o in orders]
        mine = lambda pair: jnp.where(own == 0, pair[0], pair[1])
        other = lambda pair: jnp.where(own == 0, pair[1], pair[0])
        info = jnp.stack(
            [(1 - own) * 4 + (other(place) ^ n) for n in range(4)]
            + [own * 4 + (mine(place) ^ n) for n in range(4)]
            + [other(rest), mine(rest), me]
        )
        last = [me]

        def in_turn(*arrays):
            *arrays, _ = lax.optimization_barrier((*arrays, last[0]))
            last[0] = arrays[-1]
            return arrays if len(arrays) > 1 else arrays[0]

        held, coming = [None] * CHUNKS, [None] * CHUNKS
        grams = None

        def first_sum(chunk, kept, first, got, *more):
            send, got = in_turn(join(first + got[2 * k :], *more), got)
            coming[chunk] = swap(send, 0)
            held[chunk] = (kept, got[: 2 * k])

        def second_sum(chunk):
            nonlocal grams
            kept, got = held[chunk]
            r = coming[chunk]
            more = []
            if chunk == 0:
                grams = grams + r[2 * k :]
                more = [grams]
            send, r = in_turn(join((kept[k:] + got[k:]) + r[k : 2 * k], *more), r)
            coming[chunk] = swap(send, 1)
            held[chunk] = (kept[:k], got[:k], r[:k])

        def scatter(chunk):
            nonlocal grams
            kept, got, before = held[chunk]
            r = coming[chunk]
            a = ((kept + got) + before) + r[:k]
            size = k // groups
            parts = [a[g * size : (g + 1) * size] for g in range(groups)]
            if chunk == 0:
                grams = grams + r[k:]
                half = size // 2
                parts = [join(p, grams[g * half : (g + 1) * half]) for g, p in enumerate(parts)]
            parts = in_turn(*parts)
            held[chunk] = parts[0]
            coming[chunk] = [lax.ppermute(parts[g], AXES, across[g]) for g in range(1, groups)]

        def gather(chunk):
            a = held[chunk]
            for r in coming[chunk]:
                a = a + r
            a = in_turn(a)
            held[chunk] = a
            coming[chunk] = [lax.ppermute(a, AXES, across[g]) for g in range(1, groups)]

        def second_gather(chunk):
            nonlocal grams
            size = k // groups
            parts = [held[chunk], *coming[chunk]]
            if chunk == 0:
                grams = join(*[p[size:] for p in parts])
            a = in_turn(join(*[p[:size] for p in parts]))
            held[chunk] = a
            coming[chunk] = swap(a, 1)

        def first_gather(chunk):
            a = in_turn(join(held[chunk], coming[chunk]))
            held[chunk] = a
            coming[chunk] = swap(a, 0)

        sketch, gram_sent, gram, *products = front_call(info, e, signs, rows_all, groups, width, CHUNKS)
        got = [with_pair(products[0]), None]
        grams = gram + with_pair(gram_sent)
        got[1] = with_pair(products[3])
        first_sum(0, *products[1:3], got[0], grams)
        second_sum(0)
        first_sum(1, *products[4:6], got[1])
        scatter(0)
        second_sum(1)
        gather(0)
        scatter(1)
        second_gather(0)
        gram_got = with_pair(grams)
        gather(1)
        first_gather(0)
        triangle_a, high_a, low_a, work = factor_call(0, groups, info, in_turn(grams), gram_got)
        second_gather(1)
        far = in_turn(coming[0])
        pair_blocks = [with_pair(held[0]), with_pair(far)]
        first_gather(1)
        pair_held = with_pair(held[1])
        triangle_b, high_b, low_b, _ = factor_call(1, groups, info, in_turn(work))
        triangle = join(triangle_a, triangle_b)
        high, low = in_turn(join(high_a, high_b)), join(low_a, low_b)
        basis = in_turn(basis_call(sketch, high, low))
        far1 = in_turn(coming[1])
        pair_far = with_pair(far1)
        projected = project_call(0, info, high, low, [*pair_blocks, held[0], far], groups, d, None)
        projected = project_call(1, info, high, low, [pair_held, pair_far, held[1], far1], groups, d, projected)
        return triangle, basis, projected

    return jax.shard_map(
        shards,
        mesh=mesh,
        in_specs=(P(AXES, None), P()),
        out_specs=(P(), P(AXES, None), P()),
        check_vma=False,
    )
```

```python
import functools
import math

import jax
import jax.numpy as jnp
from jax import lax
from jax.experimental import pallas as pl
from jax.experimental.pallas import tpu as pltpu
from jax.sharding import PartitionSpec as P

AXES = ("gx", "gy")
MIB = 1 << 20
LINE_FIRST = 0.375


def dot(a, b, dims=((1,), (0,))):
    return lax.dot_general(a, b, (dims, ((), ())), preferred_element_type=jnp.float32)


def split(a):
    high = a.astype(jnp.bfloat16)
    return high, (a - high.astype(jnp.float32)).astype(jnp.bfloat16)


VMEM_SPEC = pl.BlockSpec(memory_space=pltpu.VMEM)
SMEM_SPEC = pl.BlockSpec(memory_space=pltpu.SMEM)
ANY_SPEC = pl.BlockSpec(memory_space=pl.ANY)


def pinned(*arrays):
    return [pltpu.with_memory_space_constraint(a, pltpu.VMEM) for a in arrays]


PLANE = 4


def row_classes(k, line):
    unit = 8 * line
    second = max(1, round(k * LINE_FIRST / unit)) * unit
    return k - second, second


def front_kernel(
    in_scale, gram_scale, scale, line,
    info, e, signs, sketch_out, gram_sent, gram_kept, sent1, sent2, kept1, kept2,
    e_kept, sketch, rounded_t, s32, s16, acc, class1, class2, sem, out_sem,
):
    rows, d = e.shape
    k = rounded_t.shape[0]
    n = sem.shape[0] - 1
    block = rows // n
    signs_copy = pltpu.make_async_copy(signs, s32, sem.at[n])
    signs_copy.start()

    def rows_copy(i):
        at = pl.ds(pl.multiple_of(i * block, block), block)
        return pltpu.make_async_copy(e.at[at], e_kept.at[at], sem.at[i])

    for i in range(n):
        rows_copy(i).start()
    signs_copy.wait()
    s16[...] = s32[...].astype(jnp.bfloat16)

    def step(i, carry):
        rows_copy(i).wait()
        at = pl.ds(pl.multiple_of(i * block, block), block)
        sk = dot(e_kept[at, :], s16[...]) * in_scale
        sketch[at, :] = sk
        rounded_t[:, at] = sk.astype(jnp.bfloat16).T
        return carry

    lax.fori_loop(0, n, step, 0)
    outs = [pltpu.make_async_copy(sketch, sketch_out, out_sem.at[0])]
    outs[0].start()
    high, low = split(sketch[...])
    acc[...] = dot(rounded_t[...], low)
    acc[...] = (dot(rounded_t[...], high) + (acc[...] + acc[...].T)) * gram_scale
    own, in_plane, in_line = info[0], info[1], info[2]
    half = k // 2
    size = half // line
    for g in range(line):
        to = pl.ds(pl.multiple_of((in_line ^ g) * size, size), size)
        for out, region in ((gram_kept, own), (gram_sent, 1 - own)):
            out[to, :] = acc[pl.ds(pl.multiple_of(region * half + g * size, size), size), :]
    rows1, rows2 = row_classes(k, line)
    size1, size2 = rows1 // line, rows2 // line
    width = d // (2 * PLANE)
    for r, region in enumerate((1 - own, own)):
        for p in range(PLANE):
            at = pl.ds(pl.multiple_of((region * PLANE + (in_plane ^ p)) * width, width), width)
            value = dot(rounded_t[...], e_kept[:, at]) * scale
            for g in range(line):
                to = in_line ^ g
                for h in range(2):
                    part = value[:, h * width // 2 : (h + 1) * width // 2]
                    to1 = pl.multiple_of(p * 2 * rows1 + (2 * to + h) * size1, 8)
                    class1[r, pl.ds(to1, size1), :] = part[g * size1 : (g + 1) * size1]
                    to2 = pl.multiple_of(((to * PLANE + (in_plane ^ p)) * 2 + h) * size2, 8)
                    class2[r, pl.ds(to2, size2), :] = part[rows1 + g * size2 : rows1 + (g + 1) * size2]
            at = pl.ds(p * 2 * rows1, 2 * rows1)
            outs.append(pltpu.make_async_copy(class1.at[r, at], (sent1, kept1)[r].at[at], out_sem.at[1 + r * PLANE + p]))
            outs[-1].start()
        outs.append(pltpu.make_async_copy(class2.at[r], (sent2, kept2)[r], out_sem.at[1 + 2 * PLANE + r]))
        outs[-1].start()
    for copy in outs:
        copy.wait()


def front_call(info, e, signs, rows_all, line):
    rows, d = e.shape
    k = signs.shape[1]
    copies = 4
    rows1, rows2 = row_classes(k, line)
    width = d // (4 * PLANE)
    classes = [(2 * PLANE * rows1, width), (2 * PLANE * rows2, width)]
    f32 = lambda *shape: jax.ShapeDtypeStruct(shape, jnp.float32)
    return pl.pallas_call(
        functools.partial(front_kernel, 1.0 / math.sqrt(d), 1.0 / rows_all, 1.0 / math.sqrt(rows_all), line),
        in_specs=[SMEM_SPEC, ANY_SPEC, ANY_SPEC],
        out_specs=[ANY_SPEC] + [VMEM_SPEC] * 2 + [ANY_SPEC] * 4,
        out_shape=[f32(rows, k), f32(k // 2, k), f32(k // 2, k)] + [f32(*c) for c in classes] * 2,
        scratch_shapes=[
            pltpu.VMEM((rows, d), e.dtype),
            pltpu.VMEM((rows, k), jnp.float32),
            pltpu.VMEM((k, rows), jnp.bfloat16),
            pltpu.VMEM((d, k), jnp.int32),
            pltpu.VMEM((d, k), jnp.bfloat16),
            pltpu.VMEM((k, k), jnp.float32),
            pltpu.VMEM((2, *classes[0]), jnp.float32),
            pltpu.VMEM((2, *classes[1]), jnp.float32),
            pltpu.SemaphoreType.DMA((copies + 1,)),
            pltpu.SemaphoreType.DMA((3 + 2 * PLANE,)),
        ],
        compiler_params=pltpu.CompilerParams(vmem_limit_bytes=56 * MIB),
        cost_estimate=pl.CostEstimate(flops=4 * rows * d * k, bytes_accessed=rows * d * 2 + d * k * 4, transcendentals=0),
        name="front",
    )(info, e, pltpu.with_memory_space_constraint(signs, pltpu.HBM))


def factor_kernel(line, info, kept, got, triangle, high, low, work):
    k = triangle.shape[0]
    half = k // 2
    b = 64
    own, in_line = info[0], info[2]
    size = half // line
    for g in range(line):
        at = pl.ds(pl.multiple_of((in_line ^ g) * size, size), size)
        for rows, region in ((kept, own), (got, 1 - own)):
            work[pl.ds(pl.multiple_of(region * half + g * size, size), size), :k] = rows[at, :]
    rows_k = lax.broadcasted_iota(jnp.int32, (k, k), 0)
    cols_k = lax.broadcasted_iota(jnp.int32, (k, k), 1)
    work[:, k:] = jnp.where(rows_k == cols_k, 1.0, 0.0)
    lane = lax.broadcasted_iota(jnp.int32, (8, 2 * b), 1)
    sub = lax.broadcasted_iota(jnp.int32, (8, 2 * b), 0)

    def over_lanes(a, at):
        return jnp.broadcast_to(a[:, at : at + 1], (8, 2 * b))

    for n in range(k // b):
        put = slice(n * b, (n + 1) * b)
        first = (n % 2) * b
        pair = (n // 2) * 2 * b
        own_lanes = (lane >= first) & (lane < first + b)
        w = []
        for v in range(b // 8):
            a = work[n * b + 8 * v : n * b + 8 * v + 8, pair : pair + 2 * b]
            ident = jnp.where(lane == (b - first) + 8 * v + sub, 1.0, 0.0)
            w.append(jnp.where(own_lanes, a, ident))
        inv = []
        for q in range(b // 8):
            at = first + 8 * q
            row = [jnp.broadcast_to(w[q][i : i + 1, :], (8, 2 * b)) for i in range(8)]
            s = {(i, j): over_lanes(row[i], at + j) for i in range(8) for j in range(i, 8)}
            factor = {}
            scaled = []
            for j in range(8):
                r = 1.0 / s[j, j]
                for i in range(j + 1, 8):
                    factor[i, j] = s[j, i] * r
                    for m in range(i, 8):
                        s[i, m] = s[i, m] - factor[i, j] * s[j, m]
                    row[i] = row[i] - factor[i, j] * row[j]
                scaled.append(row[j] * r)
            new, pivots = row[0], s[0, 0]
            for i in range(1, 8):
                new = jnp.where(sub == i, row[i], new)
                pivots = jnp.where(sub == i, s[i, i], pivots)
            for v in range(q + 1, b // 8):
                col = [over_lanes(w[v], at + j) for j in range(8)]
                for j in range(8):
                    for m in range(j + 1, 8):
                        col[m] = col[m] - col[j] * factor[m, j]
                t = [col[j] * scaled[j] for j in range(8)]
                w[v] = w[v] - (((t[0] + t[1]) + (t[2] + t[3])) + ((t[4] + t[5]) + (t[6] + t[7])))
            moved = pltpu.roll(new * (1.0 / jnp.sqrt(pivots)), b, 1)
            inv.append(jnp.where(own_lanes, moved, 0.0))
        inv = jnp.concatenate(inv, axis=0)
        y = lax.dot_general(
            inv, work[pair : pair + 2 * b, :], (((1,), (0,)), ((), ())),
            precision=lax.Precision.HIGHEST, preferred_element_type=jnp.float32,
        )
        r_rows, i_rows = y[:, :k], y[:, k:]
        at = lax.broadcasted_iota(jnp.int32, (b, k), 0) + n * b
        to = lax.broadcasted_iota(jnp.int32, (b, k), 1)
        triangle[put, :] = jnp.where(to >= at, r_rows, 0.0)
        i_rows = jnp.where(to <= at, i_rows, 0.0)
        i_high, i_low = split(i_rows)
        high[put, :] = i_high
        low[put, :] = i_low
        if (n + 1) * b < k:
            later = jnp.where(to >= (n + 1) * b, r_rows, 0.0)
            work[...] -= lax.dot_general(
                later, y, (((0,), (0,)), ((), ())),
                precision=lax.Precision.HIGHEST, preferred_element_type=jnp.float32,
            )


def factor_call(line, info, kept, got):
    k = kept.shape[1]
    return pl.pallas_call(
        functools.partial(factor_kernel, line),
        in_specs=[SMEM_SPEC, VMEM_SPEC, VMEM_SPEC],
        out_specs=[VMEM_SPEC] * 3,
        out_shape=[
            jax.ShapeDtypeStruct((k, k), jnp.float32),
            jax.ShapeDtypeStruct((k, k), jnp.bfloat16),
            jax.ShapeDtypeStruct((k, k), jnp.bfloat16),
        ],
        scratch_shapes=[pltpu.VMEM((k, 2 * k), jnp.float32)],
        compiler_params=pltpu.CompilerParams(vmem_limit_bytes=16 * MIB),
        cost_estimate=pl.CostEstimate(flops=10**10, bytes_accessed=k * k * 8, transcendentals=0),
        name="factor",
    )(info, kept, got)


def basis_kernel(sketch, high, low, out):
    s_high, s_low = split(sketch[...])
    right = ((1,), (1,))
    out[...] = (
        dot(s_high, high[...], right) + (dot(s_high, low[...], right) + dot(s_low, high[...], right))
    ).astype(out.dtype)


def basis_call(sketch, high, low):
    rows, k = sketch.shape
    block = rows // 4
    return pl.pallas_call(
        basis_kernel,
        grid=(rows // block,),
        in_specs=[pl.BlockSpec((block, k), lambda i: (i, 0))] + [pl.BlockSpec((k, k), lambda i: (0, 0))] * 2,
        out_specs=pl.BlockSpec((block, k), lambda i: (i, 0)),
        out_shape=jax.ShapeDtypeStruct((rows, k), jnp.bfloat16),
        compiler_params=pltpu.CompilerParams(vmem_limit_bytes=16 * MIB),
        cost_estimate=pl.CostEstimate(flops=6 * rows * k * k, bytes_accessed=rows * k * 6, transcendentals=0),
        name="basis",
    )(sketch, high, low)


def project_kernel(line, is_own, info, high, low, *refs):
    *blocks, out, whole, value, sem = refs
    class1, class2 = blocks[-(PLANE + line) : -line], blocks[-line:]
    k = high.shape[0]
    rows1, rows2 = row_classes(k, line)
    size1, size2 = rows1 // line, rows2 // line
    own, in_plane, in_line = info[0], info[1], info[2]
    region = own if is_own else 1 - own
    width = value.shape[2]
    copies = []
    for p in range(PLANE):
        for g in range(line):
            to = in_line ^ g
            for h in range(2):
                cols = slice(h * width // 2, (h + 1) * width // 2)
                to1 = pl.ds(pl.multiple_of(to * size1, 8), size1)
                whole[p, to1, cols] = class1[p][(2 * g + h) * size1 : (2 * g + h + 1) * size1, :]
                to2 = pl.ds(pl.multiple_of(rows1 + to * size2, 8), size2)
                at2 = pl.ds(pl.multiple_of(((in_plane ^ p) * 2 + h) * size2, 8), size2)
                whole[p, to2, cols] = class2[g][at2, :]
        c_high, c_low = split(whole[p])
        value[p] = dot(high[...], c_high) + (dot(high[...], c_low) + dot(low[...], c_high))
        at = pl.ds(pl.multiple_of((region * PLANE + (in_plane ^ p)) * width, width), width)
        copies.append(pltpu.make_async_copy(value.at[p], out.at[:, at], sem.at[p]))
        copies[-1].start()
    for copy in copies:
        copy.wait()


def project_call(line, is_own, info, high, low, blocks, d, before):
    k = high.shape[0]
    width = d // (2 * PLANE)
    extra = [] if before is None else [before]
    return pl.pallas_call(
        functools.partial(project_kernel, line, is_own),
        in_specs=[SMEM_SPEC, VMEM_SPEC, VMEM_SPEC] + [ANY_SPEC] * len(extra) + [VMEM_SPEC] * len(blocks),
        out_specs=ANY_SPEC,
        out_shape=jax.ShapeDtypeStruct((k, d), jnp.float32),
        input_output_aliases={3: 0} if extra else {},
        scratch_shapes=[
            pltpu.VMEM((PLANE, k, width), jnp.float32),
            pltpu.VMEM((PLANE, k, width), jnp.float32),
            pltpu.SemaphoreType.DMA((PLANE,)),
        ],
        compiler_params=pltpu.CompilerParams(vmem_limit_bytes=16 * MIB),
        cost_estimate=pl.CostEstimate(flops=3 * k * k * d, bytes_accessed=k * d * 4, transcendentals=0),
        name="project",
    )(info, *pinned(high, low), *extra, *pinned(*blocks))


def solution(mesh):
    n_devices = math.prod(mesh.shape.values())
    line = n_devices // (2 * PLANE)

    def over(mask):
        pairs = [(i, i ^ mask) for i in range(n_devices)]
        return lambda a: lax.ppermute(a, AXES, pairs)

    with_pair = over(1)
    over_plane = [over(2 * g) for g in range(PLANE)]
    over_line = [over(2 * PLANE * g) for g in range(line)]

    def parts_of(a, n):
        size = a.shape[0] // n
        return [a[i * size : (i + 1) * size] for i in range(n)]

    def join(*arrays):
        return jnp.concatenate(arrays, axis=0)

    def shards(e, signs):
        rows_all = e.shape[0] * n_devices
        d = e.shape[1]
        k = signs.shape[1]
        rows1, rows2 = row_classes(k, line)
        me = lax.axis_index(AXES).astype(jnp.int32)
        info = jnp.stack([me & 1, (me >> 1) & (PLANE - 1), me // (2 * PLANE)])
        last = [me]

        def in_turn(*arrays):
            *arrays, _ = lax.optimization_barrier((*arrays, last[0]))
            last[0] = arrays[-1]
            return arrays if len(arrays) > 1 else arrays[0]

        sketch, gram_sent, gram, sent1, sent2, kept1, kept2 = front_call(info, e, signs, rows_all, line)
        got2, gram_got, got1 = with_pair(sent2), with_pair(gram_sent), with_pair(sent1)
        grams = parts_of(gram + gram_got, line)
        parts2 = [join(a + b, g) for a, b, g in zip(parts_of(kept2, line), parts_of(got2, line), grams)]
        parts2 = in_turn(*parts2)
        from_line = [over_line[g](parts2[g]) for g in range(1, line)]
        parts1 = in_turn(*[a + b for a, b in zip(parts_of(kept1, PLANE), parts_of(got1, PLANE))])
        from_plane = [over_plane[g](parts1[g]) for g in range(1, PLANE)]
        a2 = in_turn(sum(from_line, parts2[0]))
        whole2 = [over_plane[g](a2) for g in range(1, PLANE)]
        parts1 = in_turn(*parts_of(sum(from_plane, parts1[0]), line))
        from_line = [over_line[g](parts1[g]) for g in range(1, line)]
        a2 = (a2 + whole2[0]) + (whole2[1] + whole2[2])
        n2 = a2.shape[0] - gram.shape[0] // line
        a1 = in_turn(join(sum(from_line, parts1[0]), a2[n2:]))
        n1 = a1.shape[0] - gram.shape[0] // line
        from_line = [over_line[g](a1) for g in range(1, line)]
        a2 = in_turn(a2[:n2])
        class2 = [a2] + [over_line[g](a2) for g in range(1, line)]
        gathered = [a1, *from_line]
        a1 = in_turn(join(*[a[:n1] for a in gathered]))
        class1 = [a1] + [over_plane[g](a1) for g in range(1, PLANE)]
        gram = in_turn(join(*[a[n1:] for a in gathered]))
        triangle, high, low = factor_call(line, info, gram, with_pair(gram))
        high = in_turn(high)
        basis = in_turn(basis_call(sketch, high, low))
        ours = in_turn(*class1, *class2)
        theirs = [with_pair(a) for a in ours]
        projected = project_call(line, True, info, high, low, ours, d, None)
        projected = project_call(line, False, info, high, low, theirs, d, projected)
        return triangle, basis, projected

    return jax.shard_map(
        shards,
        mesh=mesh,
        in_specs=(P(AXES, None), P()),
        out_specs=(P(), P(AXES, None), P()),
        check_vma=False,
    )
```

```python
import functools
import math

import jax
import jax.numpy as jnp
from jax import lax
from jax.experimental import pallas as pl
from jax.experimental.pallas import tpu as pltpu
from jax.sharding import PartitionSpec as P

AXES = ("gx", "gy")
MIB = 1 << 20
LINE_FIRST = 0.25


def dot(a, b, dims=((1,), (0,))):
    return lax.dot_general(a, b, (dims, ((), ())), preferred_element_type=jnp.float32)


def split(a):
    high = a.astype(jnp.bfloat16)
    return high, (a - high.astype(jnp.float32)).astype(jnp.bfloat16)


VMEM_SPEC = pl.BlockSpec(memory_space=pltpu.VMEM)
SMEM_SPEC = pl.BlockSpec(memory_space=pltpu.SMEM)
ANY_SPEC = pl.BlockSpec(memory_space=pl.ANY)


def pinned(*arrays):
    return [pltpu.with_memory_space_constraint(a, pltpu.VMEM) for a in arrays]


PLANE = 4


def row_classes(k, line):
    unit = 8 * line
    second = max(1, round(k * LINE_FIRST / unit)) * unit
    return k - second, second


def front_kernel(
    in_scale, gram_scale, scale, line,
    info, e, signs, sketch_out, gram_sent, gram_kept, sent1, sent2, kept1, kept2,
    e_kept, sketch, rounded_t, s32, s16, acc, class1, class2, sem, out_sem,
):
    rows, d = e.shape
    k = rounded_t.shape[0]
    n = sem.shape[0] - 1
    block = rows // n
    signs_copy = pltpu.make_async_copy(signs, s32, sem.at[n])
    signs_copy.start()

    def rows_copy(i):
        at = pl.ds(pl.multiple_of(i * block, block), block)
        return pltpu.make_async_copy(e.at[at], e_kept.at[at], sem.at[i])

    for i in range(n):
        rows_copy(i).start()
    signs_copy.wait()
    s16[...] = s32[...].astype(jnp.bfloat16)

    def step(i, carry):
        rows_copy(i).wait()
        at = pl.ds(pl.multiple_of(i * block, block), block)
        sk = dot(e_kept[at, :], s16[...]) * in_scale
        sketch[at, :] = sk
        rounded_t[:, at] = sk.astype(jnp.bfloat16).T
        return carry

    lax.fori_loop(0, n, step, 0)
    outs = [pltpu.make_async_copy(sketch, sketch_out, out_sem.at[0])]
    outs[0].start()
    high, low = split(sketch[...])
    acc[...] = dot(rounded_t[...], low)
    acc[...] = (dot(rounded_t[...], high) + (acc[...] + acc[...].T)) * gram_scale
    own, in_plane, in_line = info[0], info[1], info[2]
    half = k // 2
    size = half // line
    for g in range(line):
        to = pl.ds(pl.multiple_of((in_line ^ g) * size, size), size)
        for out, region in ((gram_kept, own), (gram_sent, 1 - own)):
            out[to, :] = acc[pl.ds(pl.multiple_of(region * half + g * size, size), size), :]
    rows1, rows2 = row_classes(k, line)
    size1, size2 = rows1 // line, rows2 // line
    width = d // (2 * PLANE)
    for r, region in enumerate((1 - own, own)):
        for p in range(PLANE):
            at = pl.ds(pl.multiple_of((region * PLANE + (in_plane ^ p)) * width, width), width)
            value = dot(rounded_t[...], e_kept[:, at]) * scale
            for g in range(line):
                to = in_line ^ g
                for h in range(2):
                    part = value[:, h * width // 2 : (h + 1) * width // 2]
                    to1 = pl.multiple_of(p * 2 * rows1 + (2 * to + h) * size1, 8)
                    (class1, kept1)[r][pl.ds(to1, size1), :] = part[g * size1 : (g + 1) * size1]
                    to2 = pl.multiple_of(((to * PLANE + (in_plane ^ p)) * 2 + h) * size2, 8)
                    (class2, kept2)[r][pl.ds(to2, size2), :] = part[rows1 + g * size2 : rows1 + (g + 1) * size2]
            if r == 0:
                at = pl.ds(p * 2 * rows1, 2 * rows1)
                outs.append(pltpu.make_async_copy(class1.at[at], sent1.at[at], out_sem.at[1 + p]))
                outs[-1].start()
        if r == 0:
            outs.append(pltpu.make_async_copy(class2, sent2, out_sem.at[1 + PLANE]))
            outs[-1].start()
    for copy in outs:
        copy.wait()


def front_call(info, e, signs, rows_all, line):
    rows, d = e.shape
    k = signs.shape[1]
    copies = 4
    rows1, rows2 = row_classes(k, line)
    width = d // (4 * PLANE)
    classes = [(2 * PLANE * rows1, width), (2 * PLANE * rows2, width)]
    f32 = lambda *shape: jax.ShapeDtypeStruct(shape, jnp.float32)
    return pl.pallas_call(
        functools.partial(front_kernel, 1.0 / math.sqrt(d), 1.0 / rows_all, 1.0 / math.sqrt(rows_all), line),
        in_specs=[SMEM_SPEC, ANY_SPEC, ANY_SPEC],
        out_specs=[ANY_SPEC] + [VMEM_SPEC] * 2 + [ANY_SPEC] * 2 + [VMEM_SPEC] * 2,
        out_shape=[f32(rows, k)]
        + [pltpu.VMEM((k // 2, k), jnp.float32)] * 2
        + [f32(*c) for c in classes]
        + [pltpu.VMEM(c, jnp.float32) for c in classes],
        scratch_shapes=[
            pltpu.VMEM((rows, d), e.dtype),
            pltpu.VMEM((rows, k), jnp.float32),
            pltpu.VMEM((k, rows), jnp.bfloat16),
            pltpu.VMEM((d, k), jnp.int32),
            pltpu.VMEM((d, k), jnp.bfloat16),
            pltpu.VMEM((k, k), jnp.float32),
            pltpu.VMEM(classes[0], jnp.float32),
            pltpu.VMEM(classes[1], jnp.float32),
            pltpu.SemaphoreType.DMA((copies + 1,)),
            pltpu.SemaphoreType.DMA((2 + PLANE,)),
        ],
        compiler_params=pltpu.CompilerParams(vmem_limit_bytes=48 * MIB),
        cost_estimate=pl.CostEstimate(flops=4 * rows * d * k, bytes_accessed=rows * d * 2 + d * k * 4, transcendentals=0),
        name="front",
    )(info, e, pltpu.with_memory_space_constraint(signs, pltpu.HBM))


def factor_kernel(line, info, kept, got, triangle, high, low, work):
    k = triangle.shape[0]
    half = k // 2
    b = 64
    own, in_line = info[0], info[2]
    size = half // line
    for g in range(line):
        at = pl.ds(pl.multiple_of((in_line ^ g) * size, size), size)
        for rows, region in ((kept, own), (got, 1 - own)):
            work[pl.ds(pl.multiple_of(region * half + g * size, size), size), :k] = rows[at, :]
    rows_k = lax.broadcasted_iota(jnp.int32, (k, k), 0)
    cols_k = lax.broadcasted_iota(jnp.int32, (k, k), 1)
    work[:, k:] = jnp.where(rows_k == cols_k, 1.0, 0.0)
    lane = lax.broadcasted_iota(jnp.int32, (8, 2 * b), 1)
    sub = lax.broadcasted_iota(jnp.int32, (8, 2 * b), 0)

    def over_lanes(a, at):
        return jnp.broadcast_to(a[:, at : at + 1], (8, 2 * b))

    for n in range(k // b):
        put = slice(n * b, (n + 1) * b)
        first = (n % 2) * b
        pair = (n // 2) * 2 * b
        own_lanes = (lane >= first) & (lane < first + b)
        w = []
        for v in range(b // 8):
            a = work[n * b + 8 * v : n * b + 8 * v + 8, pair : pair + 2 * b]
            ident = jnp.where(lane == (b - first) + 8 * v + sub, 1.0, 0.0)
            w.append(jnp.where(own_lanes, a, ident))
        inv = []
        for q in range(b // 8):
            at = first + 8 * q
            row = [jnp.broadcast_to(w[q][i : i + 1, :], (8, 2 * b)) for i in range(8)]
            s = {(i, j): over_lanes(row[i], at + j) for i in range(8) for j in range(i, 8)}
            factor = {}
            scaled = []
            for j in range(8):
                r = 1.0 / s[j, j]
                for i in range(j + 1, 8):
                    factor[i, j] = s[j, i] * r
                    for m in range(i, 8):
                        s[i, m] = s[i, m] - factor[i, j] * s[j, m]
                    row[i] = row[i] - factor[i, j] * row[j]
                scaled.append(row[j] * r)
            new, pivots = row[0], s[0, 0]
            for i in range(1, 8):
                new = jnp.where(sub == i, row[i], new)
                pivots = jnp.where(sub == i, s[i, i], pivots)
            for v in range(q + 1, b // 8):
                col = [over_lanes(w[v], at + j) for j in range(8)]
                for j in range(8):
                    for m in range(j + 1, 8):
                        col[m] = col[m] - col[j] * factor[m, j]
                t = [col[j] * scaled[j] for j in range(8)]
                w[v] = w[v] - (((t[0] + t[1]) + (t[2] + t[3])) + ((t[4] + t[5]) + (t[6] + t[7])))
            moved = pltpu.roll(new * (1.0 / jnp.sqrt(pivots)), b, 1)
            inv.append(jnp.where(own_lanes, moved, 0.0))
        inv = jnp.concatenate(inv, axis=0)
        y = lax.dot_general(
            inv, work[pair : pair + 2 * b, :], (((1,), (0,)), ((), ())),
            precision=lax.Precision.HIGHEST, preferred_element_type=jnp.float32,
        )
        r_rows, i_rows = y[:, :k], y[:, k:]
        at = lax.broadcasted_iota(jnp.int32, (b, k), 0) + n * b
        to = lax.broadcasted_iota(jnp.int32, (b, k), 1)
        triangle[put, :] = jnp.where(to >= at, r_rows, 0.0)
        i_rows = jnp.where(to <= at, i_rows, 0.0)
        i_high, i_low = split(i_rows)
        high[put, :] = i_high
        low[put, :] = i_low
        if (n + 1) * b < k:
            later = jnp.where(to >= (n + 1) * b, r_rows, 0.0)
            work[...] -= lax.dot_general(
                later, y, (((0,), (0,)), ((), ())),
                precision=lax.Precision.HIGHEST, preferred_element_type=jnp.float32,
            )


def factor_call(line, info, kept, got):
    k = kept.shape[1]
    return pl.pallas_call(
        functools.partial(factor_kernel, line),
        in_specs=[SMEM_SPEC, VMEM_SPEC, VMEM_SPEC],
        out_specs=[VMEM_SPEC] * 3,
        out_shape=[
            jax.ShapeDtypeStruct((k, k), jnp.float32),
            jax.ShapeDtypeStruct((k, k), jnp.bfloat16),
            jax.ShapeDtypeStruct((k, k), jnp.bfloat16),
        ],
        scratch_shapes=[pltpu.VMEM((k, 2 * k), jnp.float32)],
        compiler_params=pltpu.CompilerParams(vmem_limit_bytes=16 * MIB),
        cost_estimate=pl.CostEstimate(flops=10**10, bytes_accessed=k * k * 8, transcendentals=0),
        name="factor",
    )(info, kept, got)


def basis_kernel(sketch, high, low, out):
    s_high, s_low = split(sketch[...])
    right = ((1,), (1,))
    out[...] = (
        dot(s_high, high[...], right) + (dot(s_high, low[...], right) + dot(s_low, high[...], right))
    ).astype(out.dtype)


def basis_call(sketch, high, low):
    rows, k = sketch.shape
    block = rows // 4
    return pl.pallas_call(
        basis_kernel,
        grid=(rows // block,),
        in_specs=[pl.BlockSpec((block, k), lambda i: (i, 0))] + [pl.BlockSpec((k, k), lambda i: (0, 0))] * 2,
        out_specs=pl.BlockSpec((block, k), lambda i: (i, 0)),
        out_shape=jax.ShapeDtypeStruct((rows, k), jnp.bfloat16),
        compiler_params=pltpu.CompilerParams(vmem_limit_bytes=16 * MIB),
        cost_estimate=pl.CostEstimate(flops=6 * rows * k * k, bytes_accessed=rows * k * 6, transcendentals=0),
        name="basis",
    )(sketch, high, low)


def project_kernel(line, is_own, info, high, low, *refs):
    *blocks, out, whole, value, sem = refs
    class1, class2 = blocks[-PLANE - 1 : -1], blocks[-1]
    k = high.shape[0]
    rows1, rows2 = row_classes(k, line)
    size1, size2 = rows1 // line, rows2 // line
    own, in_plane, in_line = info[0], info[1], info[2]
    region = own if is_own else 1 - own
    width = value.shape[2]
    copies = []
    for p in range(PLANE):
        for g in range(line):
            to = in_line ^ g
            for h in range(2):
                cols = slice(h * width // 2, (h + 1) * width // 2)
                to1 = pl.ds(pl.multiple_of(to * size1, 8), size1)
                whole[p, to1, cols] = class1[p][(2 * g + h) * size1 : (2 * g + h + 1) * size1, :]
                to2 = pl.ds(pl.multiple_of(rows1 + to * size2, 8), size2)
                at2 = pl.ds(pl.multiple_of(((g * PLANE + (in_plane ^ p)) * 2 + h) * size2, 8), size2)
                whole[p, to2, cols] = class2[at2, :]
        c_high, c_low = split(whole[p])
        value[p] = dot(high[...], c_high) + (dot(high[...], c_low) + dot(low[...], c_high))
        at = pl.ds(pl.multiple_of((region * PLANE + (in_plane ^ p)) * width, width), width)
        copies.append(pltpu.make_async_copy(value.at[p], out.at[:, at], sem.at[p]))
        copies[-1].start()
    for copy in copies:
        copy.wait()


def project_call(line, is_own, info, high, low, blocks, d, before):
    k = high.shape[0]
    width = d // (2 * PLANE)
    extra = [] if before is None else [before]
    return pl.pallas_call(
        functools.partial(project_kernel, line, is_own),
        in_specs=[SMEM_SPEC, VMEM_SPEC, VMEM_SPEC] + [ANY_SPEC] * len(extra) + [VMEM_SPEC] * len(blocks),
        out_specs=ANY_SPEC,
        out_shape=jax.ShapeDtypeStruct((k, d), jnp.float32),
        input_output_aliases={3: 0} if extra else {},
        scratch_shapes=[
            pltpu.VMEM((PLANE, k, width), jnp.float32),
            pltpu.VMEM((PLANE, k, width), jnp.float32),
            pltpu.SemaphoreType.DMA((PLANE,)),
        ],
        compiler_params=pltpu.CompilerParams(vmem_limit_bytes=16 * MIB),
        cost_estimate=pl.CostEstimate(flops=3 * k * k * d, bytes_accessed=k * d * 4, transcendentals=0),
        name="project",
    )(info, *pinned(high, low), *extra, *pinned(*blocks))


def solution(mesh):
    n_devices = math.prod(mesh.shape.values())
    line = n_devices // (2 * PLANE)

    def over(mask):
        pairs = [(i, i ^ mask) for i in range(n_devices)]
        return lambda a: lax.ppermute(a, AXES, pairs)

    with_pair = over(1)
    over_plane = [over(2 * g) for g in range(PLANE)]
    over_line = [over(2 * PLANE * g) for g in range(line)]

    def parts_of(a, n):
        size = a.shape[0] // n
        return [a[i * size : (i + 1) * size] for i in range(n)]

    def join(*arrays):
        return jnp.concatenate(arrays, axis=0)

    def shards(e, signs):
        rows_all = e.shape[0] * n_devices
        d = e.shape[1]
        k = signs.shape[1]
        rows1, rows2 = row_classes(k, line)
        me = lax.axis_index(AXES).astype(jnp.int32)
        info = jnp.stack([me & 1, (me >> 1) & (PLANE - 1), me // (2 * PLANE)])
        last = [me]

        def in_turn(*arrays):
            *arrays, _ = lax.optimization_barrier((*arrays, last[0]))
            last[0] = arrays[-1]
            return arrays if len(arrays) > 1 else arrays[0]

        sketch, gram_sent, gram, sent1, sent2, kept1, kept2 = front_call(info, e, signs, rows_all, line)
        got1, got2, gram_got = with_pair(sent1), with_pair(sent2), with_pair(gram_sent)
        parts1 = in_turn(*[a + b for a, b in zip(parts_of(kept1, PLANE), parts_of(got1, PLANE))])
        from_plane = [over_plane[g](parts1[g]) for g in range(1, PLANE)]
        grams = parts_of(gram + gram_got, line)
        parts2 = [join(a + b, g) for a, b, g in zip(parts_of(kept2, line), parts_of(got2, line), grams)]
        parts2 = in_turn(*parts2)
        from_line = [over_line[g](parts2[g]) for g in range(1, line)]
        a2 = sum(from_line, parts2[0])
        parts1 = in_turn(*parts_of(sum(from_plane, parts1[0]), line))
        from_line = [over_line[g](parts1[g]) for g in range(1, line)]
        a2 = in_turn(a2)
        whole2 = [over_plane[g](a2) for g in range(1, PLANE)]
        a2 = (a2 + whole2[0]) + (whole2[1] + whole2[2])
        n2 = a2.shape[0] - gram.shape[0] // line
        a1 = in_turn(join(sum(from_line, parts1[0]), a2[n2:]))
        n1 = a1.shape[0] - gram.shape[0] // line
        gathered = [a1] + [over_line[g](a1) for g in range(1, line)]
        a2 = in_turn(a2[:n2])
        near = over_line[1](a2)
        a1 = in_turn(join(*[a[:n1] for a in gathered]))
        class1 = [a1] + [over_plane[g](a1) for g in range(1, PLANE)]
        gram = in_turn(join(*[a[n1:] for a in gathered]))
        gram_got = with_pair(gram)
        gram_got, a2_later = in_turn(gram_got, a2)
        class2 = [a2, near] + [over_line[g](a2_later) for g in range(2, line)]
        triangle, high, low = factor_call(line, info, in_turn(gram), gram_got)
        high = in_turn(high)
        *class1, class2 = in_turn(*class1, join(*class2))
        theirs = [with_pair(a) for a in (*class1, class2)]
        basis = in_turn(basis_call(in_turn(sketch), high, low))
        projected = project_call(line, True, info, high, low, [*class1, class2], d, None)
        projected = project_call(line, False, info, high, low, theirs, d, projected)
        return triangle, basis, projected

    return jax.shard_map(
        shards,
        mesh=mesh,
        in_specs=(P(AXES, None), P()),
        out_specs=(P(), P(AXES, None), P()),
        check_vma=False,
    )
```

```python
import functools
import math

import jax
import jax.numpy as jnp
from jax import lax
from jax.experimental import pallas as pl
from jax.experimental.pallas import tpu as pltpu
from jax.sharding import PartitionSpec as P

AXES = ("gx", "gy")
MIB = 1 << 20
LINE_FIRST = 0.25


def dot(a, b, dims=((1,), (0,))):
    return lax.dot_general(a, b, (dims, ((), ())), preferred_element_type=jnp.float32)


def split(a):
    high = a.astype(jnp.bfloat16)
    return high, (a - high.astype(jnp.float32)).astype(jnp.bfloat16)


VMEM_SPEC = pl.BlockSpec(memory_space=pltpu.VMEM)
SMEM_SPEC = pl.BlockSpec(memory_space=pltpu.SMEM)
ANY_SPEC = pl.BlockSpec(memory_space=pl.ANY)


def pinned(*arrays):
    return [pltpu.with_memory_space_constraint(a, pltpu.VMEM) for a in arrays]


PLANE = 4


def row_classes(k, line):
    unit = 8 * line
    second = max(1, round(k * LINE_FIRST / unit)) * unit
    return k - second, second


def put_products(scale, line, info, region, rounded_t, columns, width, class1, class2, done=None):
    in_plane, in_line = info[1], info[2]
    rows1, rows2 = row_classes(rounded_t.shape[0], line)
    size1, size2 = rows1 // line, rows2 // line
    for p in range(PLANE):
        value = dot(rounded_t[...], columns(p)) * scale
        for g in range(line):
            to = in_line ^ g
            for h in range(2):
                part = value[:, h * width // 2 : (h + 1) * width // 2]
                to1 = pl.multiple_of(p * 2 * rows1 + (2 * to + h) * size1, 8)
                class1[pl.ds(to1, size1), :] = part[g * size1 : (g + 1) * size1]
                to2 = pl.multiple_of(((to * PLANE + (in_plane ^ p)) * 2 + h) * size2, 8)
                class2[pl.ds(to2, size2), :] = part[rows1 + g * size2 : rows1 + (g + 1) * size2]
        if done is not None:
            done(p, 2 * rows1)


def front_kernel(
    in_scale, gram_scale, scale, line,
    info, e, signs, sketch_out, rounded_t, gram_sent, gram_kept, sent1, sent2,
    e_kept, sketch, s32, s16, acc, class1, class2, sem, out_sem,
):
    rows, d = e.shape
    k = rounded_t.shape[0]
    n = sem.shape[0] - 1
    block = rows // n
    signs_copy = pltpu.make_async_copy(signs, s32, sem.at[n])
    signs_copy.start()

    def rows_copy(i):
        at = pl.ds(pl.multiple_of(i * block, block), block)
        return pltpu.make_async_copy(e.at[at], e_kept.at[at], sem.at[i])

    for i in range(n):
        rows_copy(i).start()
    signs_copy.wait()
    s16[...] = s32[...].astype(jnp.bfloat16)

    def step(i, carry):
        rows_copy(i).wait()
        at = pl.ds(pl.multiple_of(i * block, block), block)
        sk = dot(e_kept[at, :], s16[...]) * in_scale
        sketch[at, :] = sk
        rounded_t[:, at] = sk.astype(jnp.bfloat16).T
        return carry

    lax.fori_loop(0, n, step, 0)
    outs = [pltpu.make_async_copy(sketch, sketch_out, out_sem.at[0])]
    outs[0].start()
    high, low = split(sketch[...])
    acc[...] = dot(rounded_t[...], low)
    acc[...] = (dot(rounded_t[...], high) + (acc[...] + acc[...].T)) * gram_scale
    own, in_plane, in_line = info[0], info[1], info[2]
    half = k // 2
    size = half // line
    for g in range(line):
        to = pl.ds(pl.multiple_of((in_line ^ g) * size, size), size)
        for out, region in ((gram_kept, own), (gram_sent, 1 - own)):
            out[to, :] = acc[pl.ds(pl.multiple_of(region * half + g * size, size), size), :]
    width = d // (2 * PLANE)

    def columns(p):
        return e_kept[:, pl.ds(pl.multiple_of(((1 - own) * PLANE + (in_plane ^ p)) * width, width), width)]

    def done(p, size):
        at = pl.ds(p * size, size)
        outs.append(pltpu.make_async_copy(class1.at[at], sent1.at[at], out_sem.at[1 + p]))
        outs[-1].start()

    put_products(scale, line, info, 1 - own, rounded_t, columns, width, class1, class2, done)
    outs.append(pltpu.make_async_copy(class2, sent2, out_sem.at[1 + PLANE]))
    outs[-1].start()
    for copy in outs:
        copy.wait()


def classes_of(k, d, line):
    return [(2 * PLANE * rows, d // (4 * PLANE)) for rows in row_classes(k, line)]


def front_call(info, e, signs, rows_all, line):
    rows, d = e.shape
    k = signs.shape[1]
    copies = 4
    classes = classes_of(k, d, line)
    f32 = lambda *shape: jax.ShapeDtypeStruct(shape, jnp.float32)
    return pl.pallas_call(
        functools.partial(front_kernel, 1.0 / math.sqrt(d), 1.0 / rows_all, 1.0 / math.sqrt(rows_all), line),
        in_specs=[SMEM_SPEC, ANY_SPEC, ANY_SPEC],
        out_specs=[ANY_SPEC] + [VMEM_SPEC] * 3 + [ANY_SPEC] * 2,
        out_shape=[f32(rows, k), pltpu.VMEM((k, rows), jnp.bfloat16)]
        + [pltpu.VMEM((k // 2, k), jnp.float32)] * 2
        + [f32(*c) for c in classes],
        scratch_shapes=[
            pltpu.VMEM((rows, d), e.dtype),
            pltpu.VMEM((rows, k), jnp.float32),
            pltpu.VMEM((d, k), jnp.int32),
            pltpu.VMEM((d, k), jnp.bfloat16),
            pltpu.VMEM((k, k), jnp.float32),
            pltpu.VMEM(classes[0], jnp.float32),
            pltpu.VMEM(classes[1], jnp.float32),
            pltpu.SemaphoreType.DMA((copies + 1,)),
            pltpu.SemaphoreType.DMA((2 + PLANE,)),
        ],
        compiler_params=pltpu.CompilerParams(vmem_limit_bytes=48 * MIB),
        cost_estimate=pl.CostEstimate(flops=3 * rows * d * k, bytes_accessed=rows * d * 2 + d * k * 4, transcendentals=0),
        name="front",
    )(info, e, pltpu.with_memory_space_constraint(signs, pltpu.HBM))


def cross_kernel(scale, line, info, e, rounded_t, kept1, kept2, blocks, sem):
    own, in_plane = info[0], info[1]
    width = blocks.shape[2]

    def copy(p):
        at = pl.ds(pl.multiple_of((own * PLANE + (in_plane ^ p)) * width, width), width)
        return pltpu.make_async_copy(e.at[:, at], blocks.at[p], sem.at[p])

    for p in range(PLANE):
        copy(p).start()

    def columns(p):
        copy(p).wait()
        return blocks[p]

    put_products(scale, line, info, own, rounded_t, columns, width, kept1, kept2)


def cross_call(info, e, rounded_t, rows_all, line):
    rows, d = e.shape
    k = rounded_t.shape[0]
    width = d // (2 * PLANE)
    return pl.pallas_call(
        functools.partial(cross_kernel, 1.0 / math.sqrt(rows_all), line),
        in_specs=[SMEM_SPEC, ANY_SPEC, VMEM_SPEC],
        out_specs=[VMEM_SPEC] * 2,
        out_shape=[pltpu.VMEM(c, jnp.float32) for c in classes_of(k, d, line)],
        scratch_shapes=[pltpu.VMEM((PLANE, rows, width), e.dtype), pltpu.SemaphoreType.DMA((PLANE,))],
        compiler_params=pltpu.CompilerParams(vmem_limit_bytes=24 * MIB),
        cost_estimate=pl.CostEstimate(flops=rows * d * k, bytes_accessed=rows * d, transcendentals=0),
        name="cross",
    )(info, pltpu.with_memory_space_constraint(e, pltpu.HBM), *pinned(rounded_t))


def factor_kernel(line, info, kept, got, triangle, inverse, work):
    k = triangle.shape[0]
    half = k // 2
    b = 64
    own, in_line = info[0], info[2]
    size = half // line
    for g in range(line):
        at = pl.ds(pl.multiple_of((in_line ^ g) * size, size), size)
        for rows, region in ((kept, own), (got, 1 - own)):
            work[pl.ds(pl.multiple_of(region * half + g * size, size), size), :k] = rows[at, :]
    rows_k = lax.broadcasted_iota(jnp.int32, (k, k), 0)
    cols_k = lax.broadcasted_iota(jnp.int32, (k, k), 1)
    work[:, k:] = jnp.where(rows_k == cols_k, 1.0, 0.0)
    lane = lax.broadcasted_iota(jnp.int32, (8, 2 * b), 1)
    sub = lax.broadcasted_iota(jnp.int32, (8, 2 * b), 0)

    def over_lanes(a, at):
        return jnp.broadcast_to(a[:, at : at + 1], (8, 2 * b))

    for n in range(k // b):
        first = (n % 2) * b
        pair = (n // 2) * 2 * b
        own_lanes = (lane >= first) & (lane < first + b)
        w = []
        for v in range(b // 8):
            a = work[n * b + 8 * v : n * b + 8 * v + 8, pair : pair + 2 * b]
            ident = jnp.where(lane == (b - first) + 8 * v + sub, 1.0, 0.0)
            w.append(jnp.where(own_lanes, a, ident))
        inv = []
        for q in range(b // 8):
            at = first + 8 * q
            row = [jnp.broadcast_to(w[q][i : i + 1, :], (8, 2 * b)) for i in range(8)]
            s = {(i, j): over_lanes(row[i], at + j) for i in range(8) for j in range(i, 8)}
            factor = {}
            scaled = []
            for j in range(8):
                r = 1.0 / s[j, j]
                for i in range(j + 1, 8):
                    factor[i, j] = s[j, i] * r
                    for m in range(i, 8):
                        s[i, m] = s[i, m] - factor[i, j] * s[j, m]
                    row[i] = row[i] - factor[i, j] * row[j]
                scaled.append(row[j] * r)
            new, pivots = row[0], s[0, 0]
            for i in range(1, 8):
                new = jnp.where(sub == i, row[i], new)
                pivots = jnp.where(sub == i, s[i, i], pivots)
            for v in range(q + 1, b // 8):
                col = [over_lanes(w[v], at + j) for j in range(8)]
                for j in range(8):
                    for m in range(j + 1, 8):
                        col[m] = col[m] - col[j] * factor[m, j]
                t = [col[j] * scaled[j] for j in range(8)]
                w[v] = w[v] - (((t[0] + t[1]) + (t[2] + t[3])) + ((t[4] + t[5]) + (t[6] + t[7])))
            moved = pltpu.roll(new * (1.0 / jnp.sqrt(pivots)), b, 1)
            inv.append(jnp.where(own_lanes, moved, 0.0))
        inv = jnp.concatenate(inv, axis=0)
        end = k + pair + 2 * b
        y = lax.dot_general(
            inv, work[pair : pair + 2 * b, pair:end], (((1,), (0,)), ((), ())),
            precision=lax.Precision.HIGHEST, preferred_element_type=jnp.float32,
        )
        r_rows, i_rows = y[:, : k - pair], y[:, k - pair :]
        at = lax.broadcasted_iota(jnp.int32, r_rows.shape, 0) + n * b
        to = lax.broadcasted_iota(jnp.int32, r_rows.shape, 1) + pair
        put = slice(n * b, (n + 1) * b)
        if pair:
            triangle[put, :pair] = jnp.zeros((b, pair), jnp.float32)
        triangle[put, pair:] = jnp.where(to >= at, r_rows, 0.0)
        i_at = lax.broadcasted_iota(jnp.int32, i_rows.shape, 0) + n * b
        i_to = lax.broadcasted_iota(jnp.int32, i_rows.shape, 1)
        for row, part in zip((n * b, k + n * b), split(jnp.where(i_to <= i_at, i_rows, 0.0))):
            inverse[row : row + b, : pair + 2 * b] = part
            if pair + 2 * b < k:
                inverse[row : row + b, pair + 2 * b :] = jnp.zeros((b, k - pair - 2 * b), part.dtype)
        if (n + 1) * b < k:
            rest = (n + 1) // 2 * 2 * b
            later = jnp.where(to >= (n + 1) * b, r_rows, 0.0)[:, rest - pair :]
            work[rest:, rest:end] -= lax.dot_general(
                later, y[:, rest - pair :], (((0,), (0,)), ((), ())),
                precision=lax.Precision.HIGHEST, preferred_element_type=jnp.float32,
            )


def factor_call(line, info, kept, got):
    k = kept.shape[1]
    return pl.pallas_call(
        functools.partial(factor_kernel, line),
        in_specs=[SMEM_SPEC, VMEM_SPEC, VMEM_SPEC],
        out_specs=[VMEM_SPEC] * 2,
        out_shape=[
            jax.ShapeDtypeStruct((k, k), jnp.float32),
            jax.ShapeDtypeStruct((2 * k, k), jnp.bfloat16),
        ],
        scratch_shapes=[pltpu.VMEM((k, 2 * k), jnp.float32)],
        compiler_params=pltpu.CompilerParams(vmem_limit_bytes=16 * MIB),
        cost_estimate=pl.CostEstimate(flops=10**10, bytes_accessed=k * k * 8, transcendentals=0),
        name="factor",
    )(info, kept, got)


def basis_kernel(sketch, inverse, out):
    k = sketch.shape[1]
    s_high, s_low = split(sketch[...])
    right = ((1,), (1,))
    both = dot(s_high, inverse[...], right)
    out[...] = (both[:, :k] + (both[:, k:] + dot(s_low, inverse[:k, :], right))).astype(out.dtype)


def basis_call(sketch, inverse):
    rows, k = sketch.shape
    block = rows // 4
    return pl.pallas_call(
        basis_kernel,
        grid=(rows // block,),
        in_specs=[pl.BlockSpec((block, k), lambda i: (i, 0)), pl.BlockSpec((2 * k, k), lambda i: (0, 0))],
        out_specs=pl.BlockSpec((block, k), lambda i: (i, 0)),
        out_shape=jax.ShapeDtypeStruct((rows, k), jnp.bfloat16),
        compiler_params=pltpu.CompilerParams(vmem_limit_bytes=16 * MIB),
        cost_estimate=pl.CostEstimate(flops=6 * rows * k * k, bytes_accessed=rows * k * 6, transcendentals=0),
        name="basis",
    )(sketch, inverse)


def project_kernel(line, is_own, info, inverse, *refs):
    *blocks, out, whole, value, sem = refs
    class1, class2 = blocks[-PLANE - 1 : -1], blocks[-1]
    k = inverse.shape[1]
    rows1, rows2 = row_classes(k, line)
    size1, size2 = rows1 // line, rows2 // line
    own, in_plane, in_line = info[0], info[1], info[2]
    region = own if is_own else 1 - own
    width = value.shape[2]
    copies = []
    for p in range(PLANE):
        for g in range(line):
            to = in_line ^ g
            for h in range(2):
                cols = slice(h * width // 2, (h + 1) * width // 2)
                to1 = pl.ds(pl.multiple_of(to * size1, 8), size1)
                whole[p, to1, cols] = class1[p][(2 * g + h) * size1 : (2 * g + h + 1) * size1, :]
                to2 = pl.ds(pl.multiple_of(rows1 + to * size2, 8), size2)
                at2 = pl.ds(pl.multiple_of(((g * PLANE + (in_plane ^ p)) * 2 + h) * size2, 8), size2)
                whole[p, to2, cols] = class2[at2, :]
        c_high, c_low = split(whole[p])
        both = dot(inverse[...], c_high)
        value[p] = both[:k] + (both[k:] + dot(inverse[:k, :], c_low))
        at = pl.ds(pl.multiple_of((region * PLANE + (in_plane ^ p)) * width, width), width)
        copies.append(pltpu.make_async_copy(value.at[p], out.at[:, at], sem.at[p]))
        copies[-1].start()
    for copy in copies:
        copy.wait()


def project_call(line, is_own, info, inverse, blocks, d, before):
    k = inverse.shape[1]
    width = d // (2 * PLANE)
    extra = [] if before is None else [before]
    return pl.pallas_call(
        functools.partial(project_kernel, line, is_own),
        in_specs=[SMEM_SPEC, VMEM_SPEC] + [ANY_SPEC] * len(extra) + [VMEM_SPEC] * len(blocks),
        out_specs=ANY_SPEC,
        out_shape=jax.ShapeDtypeStruct((k, d), jnp.float32),
        input_output_aliases={2: 0} if extra else {},
        scratch_shapes=[
            pltpu.VMEM((PLANE, k, width), jnp.float32),
            pltpu.VMEM((PLANE, k, width), jnp.float32),
            pltpu.SemaphoreType.DMA((PLANE,)),
        ],
        compiler_params=pltpu.CompilerParams(vmem_limit_bytes=16 * MIB),
        cost_estimate=pl.CostEstimate(flops=3 * k * k * d, bytes_accessed=k * d * 4, transcendentals=0),
        name="project",
    )(info, *pinned(inverse), *extra, *pinned(*blocks))


def solution(mesh):
    n_devices = math.prod(mesh.shape.values())
    line = n_devices // (2 * PLANE)

    def over(mask):
        pairs = [(i, i ^ mask) for i in range(n_devices)]
        return lambda a: lax.ppermute(a, AXES, pairs)

    with_pair = over(1)
    over_plane = [over(2 * g) for g in range(PLANE)]
    over_line = [over(2 * PLANE * g) for g in range(line)]

    def parts_of(a, n):
        size = a.shape[0] // n
        return [a[i * size : (i + 1) * size] for i in range(n)]

    def join(*arrays):
        return jnp.concatenate(arrays, axis=0)

    def shards(e, signs):
        rows_all = e.shape[0] * n_devices
        d = e.shape[1]
        k = signs.shape[1]
        rows1, rows2 = row_classes(k, line)
        me = lax.axis_index(AXES).astype(jnp.int32)
        info = jnp.stack([me & 1, (me >> 1) & (PLANE - 1), me // (2 * PLANE)])
        last = [me]

        def in_turn(*arrays):
            *arrays, _ = lax.optimization_barrier((*arrays, last[0]))
            last[0] = arrays[-1]
            return arrays if len(arrays) > 1 else arrays[0]

        sketch, rounded_t, gram_sent, gram, sent1, sent2 = front_call(info, e, signs, rows_all, line)
        got1, got2, gram_got = with_pair(sent1), with_pair(sent2), with_pair(gram_sent)
        kept1, kept2 = cross_call(info, e, rounded_t, rows_all, line)
        parts1 = in_turn(*[a + b for a, b in zip(parts_of(kept1, PLANE), parts_of(got1, PLANE))])
        from_plane = [over_plane[g](parts1[g]) for g in range(1, PLANE)]
        grams = parts_of(gram + gram_got, line)
        parts2 = [join(a + b, g) for a, b, g in zip(parts_of(kept2, line), parts_of(got2, line), grams)]
        parts2 = in_turn(*parts2)
        from_line = [over_line[g](parts2[g]) for g in range(1, line)]
        a2 = sum(from_line, parts2[0])
        parts1 = in_turn(*parts_of(sum(from_plane, parts1[0]), line))
        from_line = [over_line[g](parts1[g]) for g in range(1, line)]
        a2 = in_turn(a2)
        whole2 = [over_plane[g](a2) for g in range(1, PLANE)]
        a2 = (a2 + whole2[0]) + (whole2[1] + whole2[2])
        n2 = a2.shape[0] - gram.shape[0] // line
        a1 = in_turn(join(sum(from_line, parts1[0]), a2[n2:]))
        n1 = a1.shape[0] - gram.shape[0] // line
        gathered = [a1] + [over_line[g](a1) for g in range(1, line)]
        class2 = in_turn(a2[:n2])
        class2 = join(class2, over_line[1](class2))
        *gathered, class2 = in_turn(*gathered, class2)
        a1 = in_turn(join(*[a[:n1] for a in gathered]))
        class1 = [over_plane[g](a1) for g in range(1, PLANE)]
        gram = in_turn(join(*[a[n1:] for a in gathered]))
        gram_got, class2 = in_turn(with_pair(gram), class2)
        for bit in range(1, line.bit_length() - 1):
            class2 = join(class2, over_line[1 << bit](class2))
        triangle, inverse = factor_call(line, info, in_turn(gram), gram_got)
        inverse, class2 = in_turn(inverse, class2)
        theirs = [with_pair(a1), with_pair(class2)]
        basis = in_turn(basis_call(in_turn(sketch), inverse))
        class1 = in_turn(*class1)
        theirs = [theirs[0], *[with_pair(a) for a in class1], theirs[1]]
        projected = project_call(line, True, info, inverse, [a1, *class1, class2], d, None)
        projected = project_call(line, False, info, inverse, theirs, d, projected)
        return triangle, basis, projected

    return jax.shard_map(
        shards,
        mesh=mesh,
        in_specs=(P(AXES, None), P()),
        out_specs=(P(), P(AXES, None), P()),
        check_vma=False,
    )
```

```python
import functools
import math

import jax
import jax.numpy as jnp
from jax import lax
from jax.experimental import pallas as pl
from jax.experimental.pallas import tpu as pltpu
from jax.sharding import PartitionSpec as P

AXES = ("gx", "gy")
MIB = 1 << 20
LINE_FIRST = 0.25


def dot(a, b, dims=((1,), (0,))):
    return lax.dot_general(a, b, (dims, ((), ())), preferred_element_type=jnp.float32)


def split(a):
    high = a.astype(jnp.bfloat16)
    return high, (a - high.astype(jnp.float32)).astype(jnp.bfloat16)


VMEM_SPEC = pl.BlockSpec(memory_space=pltpu.VMEM)
SMEM_SPEC = pl.BlockSpec(memory_space=pltpu.SMEM)
ANY_SPEC = pl.BlockSpec(memory_space=pl.ANY)


def pinned(*arrays):
    return [pltpu.with_memory_space_constraint(a, pltpu.VMEM) for a in arrays]


PLANE = 4


def row_classes(k, line):
    unit = 8 * line
    second = max(1, round(k * LINE_FIRST / unit)) * unit
    return k - second, second


def front_kernel(
    in_scale, gram_scale, scale, line,
    info, e, signs, sketch_out, gram_sent, gram_kept, sent1, sent2, kept1, kept2,
    e_kept, sketch, rounded_t, s32, s16, acc, class1, class2, sem, out_sem,
):
    rows, d = e.shape
    k = rounded_t.shape[0]
    n = sem.shape[0] - 1
    block = rows // n
    signs_copy = pltpu.make_async_copy(signs, s32, sem.at[n])
    signs_copy.start()

    def rows_copy(i):
        at = pl.ds(pl.multiple_of(i * block, block), block)
        return pltpu.make_async_copy(e.at[at], e_kept.at[at], sem.at[i])

    for i in range(n):
        rows_copy(i).start()
    signs_copy.wait()
    s16[...] = s32[...].astype(jnp.bfloat16)

    def step(i, carry):
        rows_copy(i).wait()
        at = pl.ds(pl.multiple_of(i * block, block), block)
        sk = dot(e_kept[at, :], s16[...]) * in_scale
        sketch[at, :] = sk
        rounded_t[:, at] = sk.astype(jnp.bfloat16).T
        return carry

    lax.fori_loop(0, n, step, 0)
    outs = [pltpu.make_async_copy(sketch, sketch_out, out_sem.at[0])]
    outs[0].start()
    high, low = split(sketch[...])
    acc[...] = dot(rounded_t[...], low)
    acc[...] = (dot(rounded_t[...], high) + (acc[...] + acc[...].T)) * gram_scale
    own, in_plane, in_line = info[0], info[1], info[2]
    half = k // 2
    size = half // line
    for g in range(line):
        to = pl.ds(pl.multiple_of((in_line ^ g) * size, size), size)
        for out, region in ((gram_kept, own), (gram_sent, 1 - own)):
            out[to, :] = acc[pl.ds(pl.multiple_of(region * half + g * size, size), size), :]
    rows1, rows2 = row_classes(k, line)
    size1, size2 = rows1 // line, rows2 // line
    width = d // (2 * PLANE)
    for r, region in enumerate((1 - own, own)):
        for p in range(PLANE):
            at = pl.ds(pl.multiple_of((region * PLANE + (in_plane ^ p)) * width, width), width)
            value = dot(rounded_t[...], e_kept[:, at]) * scale
            for g in range(line):
                to = in_line ^ g
                for h in range(2):
                    part = value[:, h * width // 2 : (h + 1) * width // 2]
                    to1 = pl.multiple_of(p * 2 * rows1 + (2 * to + h) * size1, 8)
                    (class1, kept1)[r][pl.ds(to1, size1), :] = part[g * size1 : (g + 1) * size1]
                    to2 = pl.multiple_of(((to * PLANE + (in_plane ^ p)) * 2 + h) * size2, 8)
                    (class2, kept2)[r][pl.ds(to2, size2), :] = part[rows1 + g * size2 : rows1 + (g + 1) * size2]
            if r == 0:
                at = pl.ds(p * 2 * rows1, 2 * rows1)
                outs.append(pltpu.make_async_copy(class1.at[at], sent1.at[at], out_sem.at[1 + p]))
                outs[-1].start()
        if r == 0:
            outs.append(pltpu.make_async_copy(class2, sent2, out_sem.at[1 + PLANE]))
            outs[-1].start()
    for copy in outs:
        copy.wait()


def front_call(info, e, signs, rows_all, line):
    rows, d = e.shape
    k = signs.shape[1]
    copies = 4
    rows1, rows2 = row_classes(k, line)
    width = d // (4 * PLANE)
    classes = [(2 * PLANE * rows1, width), (2 * PLANE * rows2, width)]
    f32 = lambda *shape: jax.ShapeDtypeStruct(shape, jnp.float32)
    return pl.pallas_call(
        functools.partial(front_kernel, 1.0 / math.sqrt(d), 1.0 / rows_all, 1.0 / math.sqrt(rows_all), line),
        in_specs=[SMEM_SPEC, ANY_SPEC, ANY_SPEC],
        out_specs=[ANY_SPEC] + [VMEM_SPEC] * 2 + [ANY_SPEC] * 2 + [VMEM_SPEC] * 2,
        out_shape=[f32(rows, k)]
        + [pltpu.VMEM((k // 2, k), jnp.float32)] * 2
        + [f32(*c) for c in classes]
        + [pltpu.VMEM(c, jnp.float32) for c in classes],
        scratch_shapes=[
            pltpu.VMEM((rows, d), e.dtype),
            pltpu.VMEM((rows, k), jnp.float32),
            pltpu.VMEM((k, rows), jnp.bfloat16),
            pltpu.VMEM((d, k), jnp.int32),
            pltpu.VMEM((d, k), jnp.bfloat16),
            pltpu.VMEM((k, k), jnp.float32),
            pltpu.VMEM(classes[0], jnp.float32),
            pltpu.VMEM(classes[1], jnp.float32),
            pltpu.SemaphoreType.DMA((copies + 1,)),
            pltpu.SemaphoreType.DMA((2 + PLANE,)),
        ],
        compiler_params=pltpu.CompilerParams(vmem_limit_bytes=48 * MIB),
        cost_estimate=pl.CostEstimate(flops=4 * rows * d * k, bytes_accessed=rows * d * 2 + d * k * 4, transcendentals=0),
        name="front",
    )(info, e, pltpu.with_memory_space_constraint(signs, pltpu.HBM))


def factor_kernel(line, info, kept, got, triangle, inverse, work):
    k = triangle.shape[0]
    half = k // 2
    b = 64
    own, in_line = info[0], info[2]
    size = half // line
    for g in range(line):
        at = pl.ds(pl.multiple_of((in_line ^ g) * size, size), size)
        for rows, region in ((kept, own), (got, 1 - own)):
            work[pl.ds(pl.multiple_of(region * half + g * size, size), size), :k] = rows[at, :]
    rows_k = lax.broadcasted_iota(jnp.int32, (k, k), 0)
    cols_k = lax.broadcasted_iota(jnp.int32, (k, k), 1)
    work[:, k:] = jnp.where(rows_k == cols_k, 1.0, 0.0)
    lane = lax.broadcasted_iota(jnp.int32, (8, 2 * b), 1)
    sub = lax.broadcasted_iota(jnp.int32, (8, 2 * b), 0)

    def over_lanes(a, at):
        return jnp.broadcast_to(a[:, at : at + 1], (8, 2 * b))

    for n in range(k // b):
        first = (n % 2) * b
        pair = (n // 2) * 2 * b
        own_lanes = (lane >= first) & (lane < first + b)
        w = []
        for v in range(b // 8):
            a = work[n * b + 8 * v : n * b + 8 * v + 8, pair : pair + 2 * b]
            ident = jnp.where(lane == (b - first) + 8 * v + sub, 1.0, 0.0)
            w.append(jnp.where(own_lanes, a, ident))
        inv = []
        for q in range(b // 8):
            at = first + 8 * q
            row = [jnp.broadcast_to(w[q][i : i + 1, :], (8, 2 * b)) for i in range(8)]
            s = {(i, j): over_lanes(row[i], at + j) for i in range(8) for j in range(i, 8)}
            factor = {}
            scaled = []
            for j in range(8):
                r = 1.0 / s[j, j]
                for i in range(j + 1, 8):
                    factor[i, j] = s[j, i] * r
                    for m in range(i, 8):
                        s[i, m] = s[i, m] - factor[i, j] * s[j, m]
                    row[i] = row[i] - factor[i, j] * row[j]
                scaled.append(row[j] * r)
            new, pivots = row[0], s[0, 0]
            for i in range(1, 8):
                new = jnp.where(sub == i, row[i], new)
                pivots = jnp.where(sub == i, s[i, i], pivots)
            for v in range(q + 1, b // 8):
                col = [over_lanes(w[v], at + j) for j in range(8)]
                for j in range(8):
                    for m in range(j + 1, 8):
                        col[m] = col[m] - col[j] * factor[m, j]
                t = [col[j] * scaled[j] for j in range(8)]
                w[v] = w[v] - (((t[0] + t[1]) + (t[2] + t[3])) + ((t[4] + t[5]) + (t[6] + t[7])))
            moved = pltpu.roll(new * (1.0 / jnp.sqrt(pivots)), b, 1)
            inv.append(jnp.where(own_lanes, moved, 0.0))
        inv = jnp.concatenate(inv, axis=0)
        end = k + pair + 2 * b
        y = lax.dot_general(
            inv, work[pair : pair + 2 * b, pair:end], (((1,), (0,)), ((), ())),
            precision=lax.Precision.HIGHEST, preferred_element_type=jnp.float32,
        )
        r_rows, i_rows = y[:, : k - pair], y[:, k - pair :]
        at = lax.broadcasted_iota(jnp.int32, r_rows.shape, 0) + n * b
        to = lax.broadcasted_iota(jnp.int32, r_rows.shape, 1) + pair
        put = slice(n * b, (n + 1) * b)
        if pair:
            triangle[put, :pair] = jnp.zeros((b, pair), jnp.float32)
        triangle[put, pair:] = jnp.where(to >= at, r_rows, 0.0)
        i_at = lax.broadcasted_iota(jnp.int32, i_rows.shape, 0) + n * b
        i_to = lax.broadcasted_iota(jnp.int32, i_rows.shape, 1)
        for row, part in zip((n * b, k + n * b), split(jnp.where(i_to <= i_at, i_rows, 0.0))):
            inverse[row : row + b, : pair + 2 * b] = part
            if pair + 2 * b < k:
                inverse[row : row + b, pair + 2 * b :] = jnp.zeros((b, k - pair - 2 * b), part.dtype)
        if (n + 1) * b < k:
            rest = (n + 1) // 2 * 2 * b
            later = jnp.where(to >= (n + 1) * b, r_rows, 0.0)[:, rest - pair :]
            work[rest:, rest:end] -= lax.dot_general(
                later, y[:, rest - pair :], (((0,), (0,)), ((), ())),
                precision=lax.Precision.HIGHEST, preferred_element_type=jnp.float32,
            )


def factor_call(line, info, kept, got):
    k = kept.shape[1]
    return pl.pallas_call(
        functools.partial(factor_kernel, line),
        in_specs=[SMEM_SPEC, VMEM_SPEC, VMEM_SPEC],
        out_specs=[VMEM_SPEC] * 2,
        out_shape=[
            jax.ShapeDtypeStruct((k, k), jnp.float32),
            jax.ShapeDtypeStruct((2 * k, k), jnp.bfloat16),
        ],
        scratch_shapes=[pltpu.VMEM((k, 2 * k), jnp.float32)],
        compiler_params=pltpu.CompilerParams(vmem_limit_bytes=16 * MIB),
        cost_estimate=pl.CostEstimate(flops=10**10, bytes_accessed=k * k * 8, transcendentals=0),
        name="factor",
    )(info, kept, got)


def basis_kernel(sketch, inverse, out):
    k = sketch.shape[1]
    s_high, s_low = split(sketch[...])
    right = ((1,), (1,))
    both = dot(s_high, inverse[...], right)
    out[...] = (both[:, :k] + (both[:, k:] + dot(s_low, inverse[:k, :], right))).astype(out.dtype)


def basis_call(sketch, inverse):
    rows, k = sketch.shape
    block = rows // 4
    return pl.pallas_call(
        basis_kernel,
        grid=(rows // block,),
        in_specs=[pl.BlockSpec((block, k), lambda i: (i, 0)), pl.BlockSpec((2 * k, k), lambda i: (0, 0))],
        out_specs=pl.BlockSpec((block, k), lambda i: (i, 0)),
        out_shape=jax.ShapeDtypeStruct((rows, k), jnp.bfloat16),
        compiler_params=pltpu.CompilerParams(vmem_limit_bytes=16 * MIB),
        cost_estimate=pl.CostEstimate(flops=6 * rows * k * k, bytes_accessed=rows * k * 6, transcendentals=0),
        name="basis",
    )(sketch, inverse)


def project_kernel(line, is_own, info, inverse, *refs):
    *blocks, out, whole, value, sem = refs
    class1, class2 = blocks[-PLANE - 1 : -1], blocks[-1]
    k = inverse.shape[1]
    rows1, rows2 = row_classes(k, line)
    size1, size2 = rows1 // line, rows2 // line
    own, in_plane, in_line = info[0], info[1], info[2]
    region = own if is_own else 1 - own
    width = value.shape[2]
    copies = []
    for p in range(PLANE):
        for g in range(line):
            to = in_line ^ g
            for h in range(2):
                cols = slice(h * width // 2, (h + 1) * width // 2)
                to1 = pl.ds(pl.multiple_of(to * size1, 8), size1)
                whole[p, to1, cols] = class1[p][(2 * g + h) * size1 : (2 * g + h + 1) * size1, :]
                to2 = pl.ds(pl.multiple_of(rows1 + to * size2, 8), size2)
                at2 = pl.ds(pl.multiple_of(((g * PLANE + (in_plane ^ p)) * 2 + h) * size2, 8), size2)
                whole[p, to2, cols] = class2[at2, :]
        c_high, c_low = split(whole[p])
        both = dot(inverse[...], c_high)
        value[p] = both[:k] + (both[k:] + dot(inverse[:k, :], c_low))
        at = pl.ds(pl.multiple_of((region * PLANE + (in_plane ^ p)) * width, width), width)
        copies.append(pltpu.make_async_copy(value.at[p], out.at[:, at], sem.at[p]))
        copies[-1].start()
    for copy in copies:
        copy.wait()


def project_call(line, is_own, info, inverse, blocks, d, before):
    k = inverse.shape[1]
    width = d // (2 * PLANE)
    extra = [] if before is None else [before]
    return pl.pallas_call(
        functools.partial(project_kernel, line, is_own),
        in_specs=[SMEM_SPEC, VMEM_SPEC] + [ANY_SPEC] * len(extra) + [VMEM_SPEC] * len(blocks),
        out_specs=ANY_SPEC,
        out_shape=jax.ShapeDtypeStruct((k, d), jnp.float32),
        input_output_aliases={2: 0} if extra else {},
        scratch_shapes=[
            pltpu.VMEM((PLANE, k, width), jnp.float32),
            pltpu.VMEM((PLANE, k, width), jnp.float32),
            pltpu.SemaphoreType.DMA((PLANE,)),
        ],
        compiler_params=pltpu.CompilerParams(vmem_limit_bytes=16 * MIB),
        cost_estimate=pl.CostEstimate(flops=3 * k * k * d, bytes_accessed=k * d * 4, transcendentals=0),
        name="project",
    )(info, *pinned(inverse), *extra, *pinned(*blocks))


def solution(mesh):
    n_devices = math.prod(mesh.shape.values())
    line = n_devices // (2 * PLANE)

    def over(mask):
        pairs = [(i, i ^ mask) for i in range(n_devices)]
        return lambda a: lax.ppermute(a, AXES, pairs)

    with_pair = over(1)
    over_plane = [over(2 * g) for g in range(PLANE)]
    over_line = [over(2 * PLANE * g) for g in range(line)]

    def parts_of(a, n):
        size = a.shape[0] // n
        return [a[i * size : (i + 1) * size] for i in range(n)]

    def join(*arrays):
        return jnp.concatenate(arrays, axis=0)

    def shards(e, signs):
        rows_all = e.shape[0] * n_devices
        d = e.shape[1]
        k = signs.shape[1]
        rows1, rows2 = row_classes(k, line)
        me = lax.axis_index(AXES).astype(jnp.int32)
        info = jnp.stack([me & 1, (me >> 1) & (PLANE - 1), me // (2 * PLANE)])
        last = [me]

        def in_turn(*arrays):
            *arrays, _ = lax.optimization_barrier((*arrays, last[0]))
            last[0] = arrays[-1]
            return arrays if len(arrays) > 1 else arrays[0]

        sketch, gram_sent, gram, sent1, sent2, kept1, kept2 = front_call(info, e, signs, rows_all, line)
        got1, got2, gram_got = with_pair(sent1), with_pair(sent2), with_pair(gram_sent)
        parts1 = in_turn(*[a + b for a, b in zip(parts_of(kept1, PLANE), parts_of(got1, PLANE))])
        from_plane = [over_plane[g](parts1[g]) for g in range(1, PLANE)]
        grams = parts_of(gram + gram_got, line)
        parts2 = [join(a + b, g) for a, b, g in zip(parts_of(kept2, line), parts_of(got2, line), grams)]
        parts2 = in_turn(*parts2)
        from_line = [over_line[g](parts2[g]) for g in range(1, line)]
        parts1 = in_turn(*parts_of(sum(from_plane, parts1[0]), line))
        a2 = sum(from_line, parts2[0])
        from_line = [over_line[g](parts1[g]) for g in range(1, line)]
        a2 = in_turn(a2)
        whole2 = [over_plane[g](a2) for g in range(1, PLANE)]
        a2 = (a2 + whole2[0]) + (whole2[1] + whole2[2])
        n2 = a2.shape[0] - gram.shape[0] // line
        a1 = join(sum(from_line, parts1[0]), a2[n2:])
        near, a1, a2 = in_turn(join(a1, a2[:n2]), a1, a2[:n2])
        near = over_line[1](near)
        gathered = [a1, near[: a1.shape[0]]] + [over_line[g](a1) for g in range(2, line)]
        class2 = join(a2, near[a1.shape[0] :])
        n1 = a1.shape[0] - gram.shape[0] // line
        a1 = in_turn(join(*[a[:n1] for a in gathered]))
        class1 = [over_plane[g](a1) for g in range(1, PLANE)]
        gram = in_turn(join(*[a[n1:] for a in gathered]))
        gram_got, class2 = in_turn(with_pair(gram), class2)
        for bit in range(1, line.bit_length() - 1):
            class2 = join(class2, over_line[1 << bit](class2))
        triangle, inverse = factor_call(line, info, in_turn(gram), gram_got)
        inverse = in_turn(inverse)
        basis = in_turn(basis_call(in_turn(sketch), inverse))
        *class1, class2 = in_turn(*class1, class2)
        theirs = [with_pair(a) for a in (a1, *class1, class2)]
        projected = project_call(line, True, info, inverse, [a1, *class1, class2], d, None)
        projected = project_call(line, False, info, inverse, theirs, d, projected)
        return triangle, basis, projected

    return jax.shard_map(
        shards,
        mesh=mesh,
        in_specs=(P(AXES, None), P()),
        out_specs=(P(), P(AXES, None), P()),
        check_vma=False,
    )
```

```python
import functools
import math

import jax
import jax.numpy as jnp
from jax import lax
from jax.experimental import pallas as pl
from jax.experimental.pallas import tpu as pltpu
from jax.sharding import PartitionSpec as P

AXES = ("gx", "gy")
MIB = 1 << 20
LINE_FIRST = 0.25


def dot(a, b, dims=((1,), (0,))):
    return lax.dot_general(a, b, (dims, ((), ())), preferred_element_type=jnp.float32)


def split(a):
    high = a.astype(jnp.bfloat16)
    return high, (a - high.astype(jnp.float32)).astype(jnp.bfloat16)


VMEM_SPEC = pl.BlockSpec(memory_space=pltpu.VMEM)
SMEM_SPEC = pl.BlockSpec(memory_space=pltpu.SMEM)
ANY_SPEC = pl.BlockSpec(memory_space=pl.ANY)


def pinned(*arrays):
    return [pltpu.with_memory_space_constraint(a, pltpu.VMEM) for a in arrays]


PLANE = 4


def row_classes(k, line):
    unit = 8 * line
    second = max(1, round(k * LINE_FIRST / unit)) * unit
    return k - second, second


def front_kernel(
    in_scale, gram_scale, scale, line,
    info, e, signs, sketch_out, gram_sent, gram_kept, sent1, sent2, kept1, kept2,
    e_kept, sketch, rounded_t, s32, s16, acc, class1, class2, sem, out_sem,
):
    rows, d = e.shape
    k = rounded_t.shape[0]
    n = sem.shape[0] - 1
    block = rows // n
    signs_copy = pltpu.make_async_copy(signs, s32, sem.at[n])
    signs_copy.start()

    def rows_copy(i):
        at = pl.ds(pl.multiple_of(i * block, block), block)
        return pltpu.make_async_copy(e.at[at], e_kept.at[at], sem.at[i])

    for i in range(n):
        rows_copy(i).start()
    signs_copy.wait()
    s16[...] = s32[...].astype(jnp.bfloat16)

    def step(i, carry):
        rows_copy(i).wait()
        at = pl.ds(pl.multiple_of(i * block, block), block)
        sk = dot(e_kept[at, :], s16[...]) * in_scale
        sketch[at, :] = sk
        rounded_t[:, at] = sk.astype(jnp.bfloat16).T
        return carry

    lax.fori_loop(0, n, step, 0)
    outs = [pltpu.make_async_copy(sketch, sketch_out, out_sem.at[0])]
    outs[0].start()
    high, low = split(sketch[...])
    acc[...] = dot(rounded_t[...], low)
    acc[...] = (dot(rounded_t[...], high) + (acc[...] + acc[...].T)) * gram_scale
    own, in_plane, in_line = info[0], info[1], info[2]
    half = k // 2
    size = half // line
    for g in range(line):
        to = pl.ds(pl.multiple_of((in_line ^ g) * size, size), size)
        for out, region in ((gram_kept, own), (gram_sent, 1 - own)):
            out[to, :] = acc[pl.ds(pl.multiple_of(region * half + g * size, size), size), :]
    rows1, rows2 = row_classes(k, line)
    size1, size2 = rows1 // line, rows2 // line
    width = d // (2 * PLANE)
    for r, region in enumerate((1 - own, own)):
        for p in range(PLANE):
            at = pl.ds(pl.multiple_of((region * PLANE + (in_plane ^ p)) * width, width), width)
            value = dot(rounded_t[...], e_kept[:, at]) * scale
            for g in range(line):
                to = in_line ^ g
                for h in range(2):
                    part = value[:, h * width // 2 : (h + 1) * width // 2]
                    to1 = pl.multiple_of(p * 2 * rows1 + (2 * to + h) * size1, 8)
                    (class1, kept1)[r][pl.ds(to1, size1), :] = part[g * size1 : (g + 1) * size1]
                    to2 = pl.multiple_of(((to * PLANE + (in_plane ^ p)) * 2 + h) * size2, 8)
                    (class2, kept2)[r][pl.ds(to2, size2), :] = part[rows1 + g * size2 : rows1 + (g + 1) * size2]
            if r == 0:
                at = pl.ds(p * 2 * rows1, 2 * rows1)
                outs.append(pltpu.make_async_copy(class1.at[at], sent1.at[at], out_sem.at[1 + p]))
                outs[-1].start()
        if r == 0:
            outs.append(pltpu.make_async_copy(class2, sent2, out_sem.at[1 + PLANE]))
            outs[-1].start()
    for copy in outs:
        copy.wait()


def front_call(info, e, signs, rows_all, line):
    rows, d = e.shape
    k = signs.shape[1]
    copies = 4
    rows1, rows2 = row_classes(k, line)
    width = d // (4 * PLANE)
    classes = [(2 * PLANE * rows1, width), (2 * PLANE * rows2, width)]
    f32 = lambda *shape: jax.ShapeDtypeStruct(shape, jnp.float32)
    return pl.pallas_call(
        functools.partial(front_kernel, 1.0 / math.sqrt(d), 1.0 / rows_all, 1.0 / math.sqrt(rows_all), line),
        in_specs=[SMEM_SPEC, ANY_SPEC, ANY_SPEC],
        out_specs=[ANY_SPEC] + [VMEM_SPEC] * 2 + [ANY_SPEC] * 2 + [VMEM_SPEC] * 2,
        out_shape=[f32(rows, k)]
        + [pltpu.VMEM((k // 2, k), jnp.float32)] * 2
        + [f32(*c) for c in classes]
        + [pltpu.VMEM(c, jnp.float32) for c in classes],
        scratch_shapes=[
            pltpu.VMEM((rows, d), e.dtype),
            pltpu.VMEM((rows, k), jnp.float32),
            pltpu.VMEM((k, rows), jnp.bfloat16),
            pltpu.VMEM((d, k), jnp.int32),
            pltpu.VMEM((d, k), jnp.bfloat16),
            pltpu.VMEM((k, k), jnp.float32),
            pltpu.VMEM(classes[0], jnp.float32),
            pltpu.VMEM(classes[1], jnp.float32),
            pltpu.SemaphoreType.DMA((copies + 1,)),
            pltpu.SemaphoreType.DMA((2 + PLANE,)),
        ],
        compiler_params=pltpu.CompilerParams(vmem_limit_bytes=48 * MIB),
        cost_estimate=pl.CostEstimate(flops=4 * rows * d * k, bytes_accessed=rows * d * 2 + d * k * 4, transcendentals=0),
        name="front",
    )(info, e, pltpu.with_memory_space_constraint(signs, pltpu.HBM))


def factor_kernel(line, info, kept, got, triangle, inverse, work):
    k = triangle.shape[0]
    half = k // 2
    b = 64
    own, in_line = info[0], info[2]
    size = half // line
    for g in range(line):
        at = pl.ds(pl.multiple_of((in_line ^ g) * size, size), size)
        for rows, region in ((kept, own), (got, 1 - own)):
            work[pl.ds(pl.multiple_of(region * half + g * size, size), size), :k] = rows[at, :]
    rows_k = lax.broadcasted_iota(jnp.int32, (k, k), 0)
    cols_k = lax.broadcasted_iota(jnp.int32, (k, k), 1)
    work[:, k:] = jnp.where(rows_k == cols_k, 1.0, 0.0)
    lane = lax.broadcasted_iota(jnp.int32, (8, 2 * b), 1)
    sub = lax.broadcasted_iota(jnp.int32, (8, 2 * b), 0)

    def over_lanes(a, at):
        return jnp.broadcast_to(a[:, at : at + 1], (8, 2 * b))

    for n in range(k // b):
        first = (n % 2) * b
        pair = (n // 2) * 2 * b
        own_lanes = (lane >= first) & (lane < first + b)
        w = []
        for v in range(b // 8):
            a = work[n * b + 8 * v : n * b + 8 * v + 8, pair : pair + 2 * b]
            ident = jnp.where(lane == (b - first) + 8 * v + sub, 1.0, 0.0)
            w.append(jnp.where(own_lanes, a, ident))
        inv = []
        for q in range(b // 8):
            at = first + 8 * q
            row = [jnp.broadcast_to(w[q][i : i + 1, :], (8, 2 * b)) for i in range(8)]
            s = {(i, j): over_lanes(row[i], at + j) for i in range(8) for j in range(i, 8)}
            factor = {}
            scaled = []
            for j in range(8):
                r = 1.0 / s[j, j]
                for i in range(j + 1, 8):
                    factor[i, j] = s[j, i] * r
                    for m in range(i, 8):
                        s[i, m] = s[i, m] - factor[i, j] * s[j, m]
                    row[i] = row[i] - factor[i, j] * row[j]
                scaled.append(row[j] * r)
            new, pivots = row[0], s[0, 0]
            for i in range(1, 8):
                new = jnp.where(sub == i, row[i], new)
                pivots = jnp.where(sub == i, s[i, i], pivots)
            for v in range(q + 1, b // 8):
                col = [over_lanes(w[v], at + j) for j in range(8)]
                for j in range(8):
                    for m in range(j + 1, 8):
                        col[m] = col[m] - col[j] * factor[m, j]
                t = [col[j] * scaled[j] for j in range(8)]
                w[v] = w[v] - (((t[0] + t[1]) + (t[2] + t[3])) + ((t[4] + t[5]) + (t[6] + t[7])))
            moved = pltpu.roll(new * (1.0 / jnp.sqrt(pivots)), b, 1)
            inv.append(jnp.where(own_lanes, moved, 0.0))
        inv = jnp.concatenate(inv, axis=0)
        end = k + pair + 2 * b
        y = lax.dot_general(
            inv, work[pair : pair + 2 * b, pair:end], (((1,), (0,)), ((), ())),
            precision=lax.Precision.HIGHEST, preferred_element_type=jnp.float32,
        )
        r_rows, i_rows = y[:, : k - pair], y[:, k - pair :]
        at = lax.broadcasted_iota(jnp.int32, r_rows.shape, 0) + n * b
        to = lax.broadcasted_iota(jnp.int32, r_rows.shape, 1) + pair
        put = slice(n * b, (n + 1) * b)
        if pair:
            triangle[put, :pair] = jnp.zeros((b, pair), jnp.float32)
        triangle[put, pair:] = jnp.where(to >= at, r_rows, 0.0)
        i_at = lax.broadcasted_iota(jnp.int32, i_rows.shape, 0) + n * b
        i_to = lax.broadcasted_iota(jnp.int32, i_rows.shape, 1)
        for row, part in zip((n * b, k + n * b), split(jnp.where(i_to <= i_at, i_rows, 0.0))):
            inverse[row : row + b, : pair + 2 * b] = part
            if pair + 2 * b < k:
                inverse[row : row + b, pair + 2 * b :] = jnp.zeros((b, k - pair - 2 * b), part.dtype)
        if (n + 1) * b < k:
            rest = (n + 1) // 2 * 2 * b
            later = jnp.where(to >= (n + 1) * b, r_rows, 0.0)[:, rest - pair :]
            work[rest:, rest:end] -= lax.dot_general(
                later, y[:, rest - pair :], (((0,), (0,)), ((), ())),
                precision=lax.Precision.HIGHEST, preferred_element_type=jnp.float32,
            )


def factor_call(line, info, kept, got):
    k = kept.shape[1]
    return pl.pallas_call(
        functools.partial(factor_kernel, line),
        in_specs=[SMEM_SPEC, VMEM_SPEC, VMEM_SPEC],
        out_specs=[VMEM_SPEC] * 2,
        out_shape=[
            jax.ShapeDtypeStruct((k, k), jnp.float32),
            jax.ShapeDtypeStruct((2 * k, k), jnp.bfloat16),
        ],
        scratch_shapes=[pltpu.VMEM((k, 2 * k), jnp.float32)],
        compiler_params=pltpu.CompilerParams(vmem_limit_bytes=16 * MIB),
        cost_estimate=pl.CostEstimate(flops=10**10, bytes_accessed=k * k * 8, transcendentals=0),
        name="factor",
    )(info, kept, got)


def basis_kernel(sketch, inverse, out):
    k = sketch.shape[1]
    s_high, s_low = split(sketch[...])
    right = ((1,), (1,))
    both = dot(s_high, inverse[...], right)
    out[...] = (both[:, :k] + (both[:, k:] + dot(s_low, inverse[:k, :], right))).astype(out.dtype)


def basis_call(sketch, inverse):
    rows, k = sketch.shape
    block = rows // 4
    return pl.pallas_call(
        basis_kernel,
        grid=(rows // block,),
        in_specs=[pl.BlockSpec((block, k), lambda i: (i, 0)), pl.BlockSpec((2 * k, k), lambda i: (0, 0))],
        out_specs=pl.BlockSpec((block, k), lambda i: (i, 0)),
        out_shape=jax.ShapeDtypeStruct((rows, k), jnp.bfloat16),
        compiler_params=pltpu.CompilerParams(vmem_limit_bytes=16 * MIB),
        cost_estimate=pl.CostEstimate(flops=6 * rows * k * k, bytes_accessed=rows * k * 6, transcendentals=0),
        name="basis",
    )(sketch, inverse)


def project_kernel(line, is_own, info, inverse, *refs):
    *blocks, out, whole, value, sem = refs
    class1, class2 = blocks[-PLANE - 1 : -1], blocks[-1]
    k = inverse.shape[1]
    rows1, rows2 = row_classes(k, line)
    size1, size2 = rows1 // line, rows2 // line
    own, in_plane, in_line = info[0], info[1], info[2]
    region = own if is_own else 1 - own
    width = value.shape[2]
    copies = []
    for p in range(PLANE):
        for g in range(line):
            to = in_line ^ g
            for h in range(2):
                cols = slice(h * width // 2, (h + 1) * width // 2)
                to1 = pl.ds(pl.multiple_of(to * size1, 8), size1)
                whole[p, to1, cols] = class1[p][(2 * g + h) * size1 : (2 * g + h + 1) * size1, :]
                to2 = pl.ds(pl.multiple_of(rows1 + to * size2, 8), size2)
                at2 = pl.ds(pl.multiple_of(((g * PLANE + (in_plane ^ p)) * 2 + h) * size2, 8), size2)
                whole[p, to2, cols] = class2[at2, :]
        c_high, c_low = split(whole[p])
        both = dot(inverse[...], c_high)
        value[p] = both[:k] + (both[k:] + dot(inverse[:k, :], c_low))
        at = pl.ds(pl.multiple_of((region * PLANE + (in_plane ^ p)) * width, width), width)
        copies.append(pltpu.make_async_copy(value.at[p], out.at[:, at], sem.at[p]))
        copies[-1].start()
    for copy in copies:
        copy.wait()


def project_call(line, is_own, info, inverse, blocks, d, before):
    k = inverse.shape[1]
    width = d // (2 * PLANE)
    extra = [] if before is None else [before]
    return pl.pallas_call(
        functools.partial(project_kernel, line, is_own),
        in_specs=[SMEM_SPEC, VMEM_SPEC] + [ANY_SPEC] * len(extra) + [VMEM_SPEC] * len(blocks),
        out_specs=ANY_SPEC,
        out_shape=jax.ShapeDtypeStruct((k, d), jnp.float32),
        input_output_aliases={2: 0} if extra else {},
        scratch_shapes=[
            pltpu.VMEM((PLANE, k, width), jnp.float32),
            pltpu.VMEM((PLANE, k, width), jnp.float32),
            pltpu.SemaphoreType.DMA((PLANE,)),
        ],
        compiler_params=pltpu.CompilerParams(vmem_limit_bytes=16 * MIB),
        cost_estimate=pl.CostEstimate(flops=3 * k * k * d, bytes_accessed=k * d * 4, transcendentals=0),
        name="project",
    )(info, *pinned(inverse), *extra, *pinned(*blocks))


def solution(mesh):
    n_devices = math.prod(mesh.shape.values())
    line = n_devices // (2 * PLANE)

    def over(mask):
        pairs = [(i, i ^ mask) for i in range(n_devices)]
        return lambda a: lax.ppermute(a, AXES, pairs)

    with_pair = over(1)
    over_plane = [over(2 * g) for g in range(PLANE)]
    over_line = [over(2 * PLANE * g) for g in range(line)]

    def parts_of(a, n):
        size = a.shape[0] // n
        return [a[i * size : (i + 1) * size] for i in range(n)]

    def join(*arrays):
        return jnp.concatenate(arrays, axis=0)

    def shards(e, signs):
        rows_all = e.shape[0] * n_devices
        d = e.shape[1]
        k = signs.shape[1]
        rows1, rows2 = row_classes(k, line)
        me = lax.axis_index(AXES).astype(jnp.int32)
        info = jnp.stack([me & 1, (me >> 1) & (PLANE - 1), me // (2 * PLANE)])
        last = [me]

        def in_turn(*arrays):
            *arrays, _ = lax.optimization_barrier((*arrays, last[0]))
            last[0] = arrays[-1]
            return arrays if len(arrays) > 1 else arrays[0]

        sketch, gram_sent, gram, sent1, sent2, kept1, kept2 = front_call(info, e, signs, rows_all, line)
        got1, got2, gram_got = with_pair(sent1), with_pair(sent2), with_pair(gram_sent)
        parts1 = in_turn(*[a + b for a, b in zip(parts_of(kept1, PLANE), parts_of(got1, PLANE))])
        from_plane = [over_plane[g](parts1[g]) for g in range(1, PLANE)]
        grams = parts_of(gram + gram_got, line)
        parts2 = [join(a + b, g) for a, b, g in zip(parts_of(kept2, line), parts_of(got2, line), grams)]
        parts2 = in_turn(*parts2)
        from_line = [over_line[g](parts2[g]) for g in range(1, line)]
        parts1 = in_turn(*parts_of(sum(from_plane, parts1[0]), line))
        a2 = sum(from_line, parts2[0])
        from_line = [over_line[g](parts1[g]) for g in range(1, line)]
        a2 = in_turn(a2)
        whole2 = [over_plane[g](a2) for g in range(1, PLANE)]
        a2 = (a2 + whole2[0]) + (whole2[1] + whole2[2])
        n2 = a2.shape[0] - gram.shape[0] // line
        a1 = in_turn(join(sum(from_line, parts1[0]), a2[n2:]))
        gathered = [a1] + [over_line[g](a1) for g in range(1, line)]
        n1 = a1.shape[0] - gram.shape[0] // line
        a1 = in_turn(join(*[a[:n1] for a in gathered]))
        class1 = [over_plane[g](a1) for g in range(1, PLANE)]
        gram = in_turn(join(*[a[n1:] for a in gathered]))
        gram_got = with_pair(gram)
        class2 = in_turn(a2[:n2])
        class2 = join(class2, over_line[1](class2))
        gram_got, class2 = in_turn(gram_got, class2)
        for bit in range(1, line.bit_length() - 1):
            class2 = join(class2, over_line[1 << bit](class2))
        a1 = in_turn(a1)
        their1 = with_pair(a1)
        triangle, inverse = factor_call(line, info, in_turn(gram), gram_got)
        their1, inverse = in_turn(their1, inverse)
        basis = in_turn(basis_call(in_turn(sketch), inverse))
        class2 = in_turn(class2)
        their2 = with_pair(class2)
        class1 = in_turn(*class1)
        theirs = [their1, *[with_pair(a) for a in class1], their2]
        projected = project_call(line, True, info, inverse, [a1, *class1, class2], d, None)
        projected = project_call(line, False, info, inverse, theirs, d, projected)
        return triangle, basis, projected

    return jax.shard_map(
        shards,
        mesh=mesh,
        in_specs=(P(AXES, None), P()),
        out_specs=(P(), P(AXES, None), P()),
        check_vma=False,
    )
```

```python
import functools
import math

import jax
import jax.numpy as jnp
from jax import lax
from jax.experimental import pallas as pl
from jax.experimental.pallas import tpu as pltpu
from jax.sharding import PartitionSpec as P

AXES = ("gx", "gy")
MIB = 1 << 20
LINE_FIRST = 0.25


def dot(a, b, dims=((1,), (0,))):
    return lax.dot_general(a, b, (dims, ((), ())), preferred_element_type=jnp.float32)


def split(a):
    high = a.astype(jnp.bfloat16)
    return high, (a - high.astype(jnp.float32)).astype(jnp.bfloat16)


VMEM_SPEC = pl.BlockSpec(memory_space=pltpu.VMEM)
SMEM_SPEC = pl.BlockSpec(memory_space=pltpu.SMEM)
ANY_SPEC = pl.BlockSpec(memory_space=pl.ANY)


def pinned(*arrays):
    return [pltpu.with_memory_space_constraint(a, pltpu.VMEM) for a in arrays]


PLANE = 4


def row_classes(k, line):
    unit = 8 * line
    second = max(1, round(k * LINE_FIRST / unit)) * unit
    return k - second, second


def front_kernel(
    in_scale, gram_scale, scale, line,
    info, e, signs, sketch_out, gram_sent, gram_kept, sent2, kept1, kept2, *refs,
):
    sent1 = refs[:PLANE]
    e_kept, sketch, rounded_t, s32, s16, acc, class1, class2, sem, out_sem = refs[PLANE:]
    rows, d = e.shape
    k = rounded_t.shape[0]
    n = sem.shape[0] - 1
    block = rows // n
    signs_copy = pltpu.make_async_copy(signs, s32, sem.at[n])
    signs_copy.start()

    def rows_copy(i):
        at = pl.ds(pl.multiple_of(i * block, block), block)
        return pltpu.make_async_copy(e.at[at], e_kept.at[at], sem.at[i])

    for i in range(n):
        rows_copy(i).start()
    signs_copy.wait()
    s16[...] = s32[...].astype(jnp.bfloat16)

    def step(i, carry):
        rows_copy(i).wait()
        at = pl.ds(pl.multiple_of(i * block, block), block)
        sk = dot(e_kept[at, :], s16[...]) * in_scale
        sketch[at, :] = sk
        rounded_t[:, at] = sk.astype(jnp.bfloat16).T
        return carry

    lax.fori_loop(0, n, step, 0)
    outs = [pltpu.make_async_copy(sketch, sketch_out, out_sem.at[0])]
    outs[0].start()
    high, low = split(sketch[...])
    acc[...] = dot(rounded_t[...], low)
    acc[...] = (dot(rounded_t[...], high) + (acc[...] + acc[...].T)) * gram_scale
    own, in_plane, in_line = info[0], info[1], info[2]
    half = k // 2
    size = half // line
    for g in range(line):
        to = pl.ds(pl.multiple_of((in_line ^ g) * size, size), size)
        for out, region in ((gram_kept, own), (gram_sent, 1 - own)):
            out[to, :] = acc[pl.ds(pl.multiple_of(region * half + g * size, size), size), :]
    rows1, rows2 = row_classes(k, line)
    size1, size2 = rows1 // line, rows2 // line
    width = d // (2 * PLANE)
    for r, region in enumerate((1 - own, own)):
        for p in range(PLANE):
            at = pl.ds(pl.multiple_of((region * PLANE + (in_plane ^ p)) * width, width), width)
            value = dot(rounded_t[...], e_kept[:, at]) * scale
            for g in range(line):
                to = in_line ^ g
                for h in range(2):
                    part = value[:, h * width // 2 : (h + 1) * width // 2]
                    to1 = pl.multiple_of(p * 2 * rows1 + (2 * to + h) * size1, 8)
                    (class1, kept1)[r][pl.ds(to1, size1), :] = part[g * size1 : (g + 1) * size1]
                    to2 = pl.multiple_of(((to * PLANE + (in_plane ^ p)) * 2 + h) * size2, 8)
                    (class2, kept2)[r][pl.ds(to2, size2), :] = part[rows1 + g * size2 : rows1 + (g + 1) * size2]
            if r == 0:
                at = pl.ds(p * 2 * rows1, 2 * rows1)
                outs.append(pltpu.make_async_copy(class1.at[at], sent1[p], out_sem.at[1 + p]))
                outs[-1].start()
        if r == 0:
            outs.append(pltpu.make_async_copy(class2, sent2, out_sem.at[1 + PLANE]))
            outs[-1].start()
    for copy in outs:
        copy.wait()


def front_call(info, e, signs, rows_all, line):
    rows, d = e.shape
    k = signs.shape[1]
    copies = 4
    rows1, rows2 = row_classes(k, line)
    width = d // (4 * PLANE)
    classes = [(2 * PLANE * rows1, width), (2 * PLANE * rows2, width)]
    f32 = lambda *shape: jax.ShapeDtypeStruct(shape, jnp.float32)
    return pl.pallas_call(
        functools.partial(front_kernel, 1.0 / math.sqrt(d), 1.0 / rows_all, 1.0 / math.sqrt(rows_all), line),
        in_specs=[SMEM_SPEC, ANY_SPEC, ANY_SPEC],
        out_specs=[ANY_SPEC] + [VMEM_SPEC] * 2 + [ANY_SPEC] + [VMEM_SPEC] * 2 + [ANY_SPEC] * PLANE,
        out_shape=[f32(rows, k)]
        + [pltpu.VMEM((k // 2, k), jnp.float32)] * 2
        + [f32(*classes[1])]
        + [pltpu.VMEM(c, jnp.float32) for c in classes]
        + [f32(2 * rows1, width)] * PLANE,
        scratch_shapes=[
            pltpu.VMEM((rows, d), e.dtype),
            pltpu.VMEM((rows, k), jnp.float32),
            pltpu.VMEM((k, rows), jnp.bfloat16),
            pltpu.VMEM((d, k), jnp.int32),
            pltpu.VMEM((d, k), jnp.bfloat16),
            pltpu.VMEM((k, k), jnp.float32),
            pltpu.VMEM(classes[0], jnp.float32),
            pltpu.VMEM(classes[1], jnp.float32),
            pltpu.SemaphoreType.DMA((copies + 1,)),
            pltpu.SemaphoreType.DMA((2 + PLANE,)),
        ],
        compiler_params=pltpu.CompilerParams(vmem_limit_bytes=48 * MIB),
        cost_estimate=pl.CostEstimate(flops=4 * rows * d * k, bytes_accessed=rows * d * 2 + d * k * 4, transcendentals=0),
        name="front",
    )(info, e, pltpu.with_memory_space_constraint(signs, pltpu.HBM))


def factor_kernel(line, info, kept, got, triangle, inverse, work):
    k = triangle.shape[0]
    half = k // 2
    b = 64
    own, in_line = info[0], info[2]
    size = half // line
    for g in range(line):
        at = pl.ds(pl.multiple_of((in_line ^ g) * size, size), size)
        for rows, region in ((kept, own), (got, 1 - own)):
            work[pl.ds(pl.multiple_of(region * half + g * size, size), size), :k] = rows[at, :]
    rows_k = lax.broadcasted_iota(jnp.int32, (k, k), 0)
    cols_k = lax.broadcasted_iota(jnp.int32, (k, k), 1)
    work[:, k:] = jnp.where(rows_k == cols_k, 1.0, 0.0)
    lane = lax.broadcasted_iota(jnp.int32, (8, 2 * b), 1)
    sub = lax.broadcasted_iota(jnp.int32, (8, 2 * b), 0)

    def over_lanes(a, at):
        return jnp.broadcast_to(a[:, at : at + 1], (8, 2 * b))

    for n in range(k // b):
        first = (n % 2) * b
        pair = (n // 2) * 2 * b
        own_lanes = (lane >= first) & (lane < first + b)
        w = []
        for v in range(b // 8):
            a = work[n * b + 8 * v : n * b + 8 * v + 8, pair : pair + 2 * b]
            ident = jnp.where(lane == (b - first) + 8 * v + sub, 1.0, 0.0)
            w.append(jnp.where(own_lanes, a, ident))
        inv = []
        for q in range(b // 8):
            at = first + 8 * q
            row = [jnp.broadcast_to(w[q][i : i + 1, :], (8, 2 * b)) for i in range(8)]
            s = {(i, j): over_lanes(row[i], at + j) for i in range(8) for j in range(i, 8)}
            factor = {}
            scaled = []
            for j in range(8):
                r = 1.0 / s[j, j]
                for i in range(j + 1, 8):
                    factor[i, j] = s[j, i] * r
                    for m in range(i, 8):
                        s[i, m] = s[i, m] - factor[i, j] * s[j, m]
                    row[i] = row[i] - factor[i, j] * row[j]
                scaled.append(row[j] * r)
            new, pivots = row[0], s[0, 0]
            for i in range(1, 8):
                new = jnp.where(sub == i, row[i], new)
                pivots = jnp.where(sub == i, s[i, i], pivots)
            for v in range(q + 1, b // 8):
                col = [over_lanes(w[v], at + j) for j in range(8)]
                for j in range(8):
                    for m in range(j + 1, 8):
                        col[m] = col[m] - col[j] * factor[m, j]
                t = [col[j] * scaled[j] for j in range(8)]
                w[v] = w[v] - (((t[0] + t[1]) + (t[2] + t[3])) + ((t[4] + t[5]) + (t[6] + t[7])))
            moved = pltpu.roll(new * (1.0 / jnp.sqrt(pivots)), b, 1)
            inv.append(jnp.where(own_lanes, moved, 0.0))
        inv = jnp.concatenate(inv, axis=0)
        end = k + pair + 2 * b
        y = lax.dot_general(
            inv, work[pair : pair + 2 * b, pair:end], (((1,), (0,)), ((), ())),
            precision=lax.Precision.HIGHEST, preferred_element_type=jnp.float32,
        )
        r_rows, i_rows = y[:, : k - pair], y[:, k - pair :]
        at = lax.broadcasted_iota(jnp.int32, r_rows.shape, 0) + n * b
        to = lax.broadcasted_iota(jnp.int32, r_rows.shape, 1) + pair
        put = slice(n * b, (n + 1) * b)
        if pair:
            triangle[put, :pair] = jnp.zeros((b, pair), jnp.float32)
        triangle[put, pair:] = jnp.where(to >= at, r_rows, 0.0)
        i_at = lax.broadcasted_iota(jnp.int32, i_rows.shape, 0) + n * b
        i_to = lax.broadcasted_iota(jnp.int32, i_rows.shape, 1)
        for row, part in zip((n * b, k + n * b), split(jnp.where(i_to <= i_at, i_rows, 0.0))):
            inverse[row : row + b, : pair + 2 * b] = part
            if pair + 2 * b < k:
                inverse[row : row + b, pair + 2 * b :] = jnp.zeros((b, k - pair - 2 * b), part.dtype)
        if (n + 1) * b < k:
            rest = (n + 1) // 2 * 2 * b
            later = jnp.where(to >= (n + 1) * b, r_rows, 0.0)[:, rest - pair :]
            work[rest:, rest:end] -= lax.dot_general(
                later, y[:, rest - pair :], (((0,), (0,)), ((), ())),
                precision=lax.Precision.HIGHEST, preferred_element_type=jnp.float32,
            )


def factor_call(line, info, kept, got):
    k = kept.shape[1]
    return pl.pallas_call(
        functools.partial(factor_kernel, line),
        in_specs=[SMEM_SPEC, VMEM_SPEC, VMEM_SPEC],
        out_specs=[VMEM_SPEC] * 2,
        out_shape=[
            jax.ShapeDtypeStruct((k, k), jnp.float32),
            jax.ShapeDtypeStruct((2 * k, k), jnp.bfloat16),
        ],
        scratch_shapes=[pltpu.VMEM((k, 2 * k), jnp.float32)],
        compiler_params=pltpu.CompilerParams(vmem_limit_bytes=16 * MIB),
        cost_estimate=pl.CostEstimate(flops=10**10, bytes_accessed=k * k * 8, transcendentals=0),
        name="factor",
    )(info, kept, got)


def basis_kernel(sketch, inverse, out, value, sem):
    rows, k = sketch.shape
    n = sem.shape[0]
    right = ((1,), (1,))
    copies = []
    for i in range(n):
        at = pl.ds(i * (rows // n), rows // n)
        s_high, s_low = split(sketch[at, :])
        both = dot(s_high, inverse[...], right)
        value[at, :] = (both[:, :k] + (both[:, k:] + dot(s_low, inverse[:k, :], right))).astype(out.dtype)
        copies.append(pltpu.make_async_copy(value.at[at], out.at[at], sem.at[i]))
        copies[-1].start()
    for copy in copies:
        copy.wait()


def basis_call(sketch, inverse):
    rows, k = sketch.shape
    return pl.pallas_call(
        basis_kernel,
        in_specs=[VMEM_SPEC] * 2,
        out_specs=ANY_SPEC,
        out_shape=jax.ShapeDtypeStruct((rows, k), jnp.bfloat16),
        scratch_shapes=[pltpu.VMEM((rows, k), jnp.bfloat16), pltpu.SemaphoreType.DMA((4,))],
        compiler_params=pltpu.CompilerParams(vmem_limit_bytes=16 * MIB),
        cost_estimate=pl.CostEstimate(flops=6 * rows * k * k, bytes_accessed=rows * k * 6, transcendentals=0),
        name="basis",
    )(*pinned(sketch, inverse))


def project_kernel(line, is_own, info, inverse, *refs):
    *blocks, out, whole, value, sem = refs
    class1, class2 = blocks[-PLANE - 1 : -1], blocks[-1]
    k = inverse.shape[1]
    rows1, rows2 = row_classes(k, line)
    size1, size2 = rows1 // line, rows2 // line
    own, in_plane, in_line = info[0], info[1], info[2]
    region = own if is_own else 1 - own
    width = value.shape[2]
    copies = []
    for p in range(PLANE):
        for g in range(line):
            to = in_line ^ g
            for h in range(2):
                cols = slice(h * width // 2, (h + 1) * width // 2)
                to1 = pl.ds(pl.multiple_of(to * size1, 8), size1)
                whole[p, to1, cols] = class1[p][(2 * g + h) * size1 : (2 * g + h + 1) * size1, :]
                to2 = pl.ds(pl.multiple_of(rows1 + to * size2, 8), size2)
                at2 = pl.ds(pl.multiple_of(((g * PLANE + (in_plane ^ p)) * 2 + h) * size2, 8), size2)
                whole[p, to2, cols] = class2[at2, :]
        c_high, c_low = split(whole[p])
        both = dot(inverse[...], c_high)
        value[p] = both[:k] + (both[k:] + dot(inverse[:k, :], c_low))
        at = pl.ds(pl.multiple_of((region * PLANE + (in_plane ^ p)) * width, width), width)
        copies.append(pltpu.make_async_copy(value.at[p], out.at[:, at], sem.at[p]))
        copies[-1].start()
    for copy in copies:
        copy.wait()


def project_call(line, is_own, info, inverse, blocks, d, before):
    k = inverse.shape[1]
    width = d // (2 * PLANE)
    extra = [] if before is None else [before]
    return pl.pallas_call(
        functools.partial(project_kernel, line, is_own),
        in_specs=[SMEM_SPEC, VMEM_SPEC] + [ANY_SPEC] * len(extra) + [VMEM_SPEC] * len(blocks),
        out_specs=ANY_SPEC,
        out_shape=jax.ShapeDtypeStruct((k, d), jnp.float32),
        input_output_aliases={2: 0} if extra else {},
        scratch_shapes=[
            pltpu.VMEM((PLANE, k, width), jnp.float32),
            pltpu.VMEM((PLANE, k, width), jnp.float32),
            pltpu.SemaphoreType.DMA((PLANE,)),
        ],
        compiler_params=pltpu.CompilerParams(vmem_limit_bytes=16 * MIB),
        cost_estimate=pl.CostEstimate(flops=3 * k * k * d, bytes_accessed=k * d * 4, transcendentals=0),
        name="project",
    )(info, *pinned(inverse), *extra, *pinned(*blocks))


def solution(mesh):
    n_devices = math.prod(mesh.shape.values())
    line = n_devices // (2 * PLANE)

    def over(mask):
        pairs = [(i, i ^ mask) for i in range(n_devices)]
        return lambda a: lax.ppermute(a, AXES, pairs)

    with_pair = over(1)
    over_plane = [over(2 * g) for g in range(PLANE)]
    over_line = [over(2 * PLANE * g) for g in range(line)]

    def parts_of(a, n):
        size = a.shape[0] // n
        return [a[i * size : (i + 1) * size] for i in range(n)]

    def join(*arrays):
        return jnp.concatenate(arrays, axis=0)

    def shards(e, signs):
        rows_all = e.shape[0] * n_devices
        d = e.shape[1]
        k = signs.shape[1]
        rows1, rows2 = row_classes(k, line)
        me = lax.axis_index(AXES).astype(jnp.int32)
        info = jnp.stack([me & 1, (me >> 1) & (PLANE - 1), me // (2 * PLANE)])
        last = [me]

        def in_turn(*arrays):
            *arrays, _ = lax.optimization_barrier((*arrays, last[0]))
            last[0] = arrays[-1]
            return arrays if len(arrays) > 1 else arrays[0]

        sketch, gram_sent, gram, sent2, kept1, kept2, *sent1 = front_call(info, e, signs, rows_all, line)
        got1 = [with_pair(a) for a in sent1[1:]]
        gram_got, got2 = with_pair(gram_sent), with_pair(sent2)
        kept1 = parts_of(kept1, PLANE)
        from_plane = []
        for g in range(1, PLANE):
            if g > 1:
                got1[g - 1] = in_turn(got1[g - 1])
            from_plane.append(over_plane[g](in_turn(kept1[g] + got1[g - 1])))
        a1 = kept1[0] + with_pair(sent1[0])
        grams = parts_of(gram + gram_got, line)
        parts2 = [join(a + b, g) for a, b, g in zip(parts_of(kept2, line), parts_of(got2, line), grams)]
        parts2 = in_turn(*parts2)
        from_line = [over_line[g](parts2[g]) for g in range(1, line)]
        parts1 = in_turn(*parts_of(sum(from_plane, a1), line))
        a2 = sum(from_line, parts2[0])
        from_line = [over_line[g](parts1[g]) for g in range(1, line)]
        a2 = in_turn(a2)
        whole2 = [over_plane[g](a2) for g in range(1, PLANE)]
        a2 = (a2 + whole2[0]) + (whole2[1] + whole2[2])
        n2 = a2.shape[0] - gram.shape[0] // line
        a1 = in_turn(join(sum(from_line, parts1[0]), a2[n2:]))
        gathered = [a1] + [over_line[g](a1) for g in range(1, line)]
        n1 = a1.shape[0] - gram.shape[0] // line
        a1 = in_turn(join(*[a[:n1] for a in gathered]))
        class1 = [over_plane[g](a1) for g in range(1, PLANE)]
        gram = in_turn(join(*[a[n1:] for a in gathered]))
        gram_got = with_pair(gram)
        class2 = in_turn(a2[:n2])
        class2 = join(class2, over_line[1](class2))
        gram_got, class2 = in_turn(gram_got, class2)
        for bit in range(1, line.bit_length() - 1):
            class2 = join(class2, over_line[1 << bit](class2))
        a1 = in_turn(a1)
        their1 = with_pair(a1)
        triangle, inverse = factor_call(line, info, in_turn(gram), gram_got)
        their1, inverse = in_turn(their1, inverse)
        basis = in_turn(basis_call(in_turn(sketch), inverse))
        class2 = in_turn(class2)
        their2 = with_pair(class2)
        class1 = in_turn(*class1)
        theirs = [their1, *[with_pair(a) for a in class1], their2]
        projected = project_call(line, True, info, inverse, [a1, *class1, class2], d, None)
        projected = project_call(line, False, info, inverse, theirs, d, projected)
        return triangle, basis, projected

    return jax.shard_map(
        shards,
        mesh=mesh,
        in_specs=(P(AXES, None), P()),
        out_specs=(P(), P(AXES, None), P()),
        check_vma=False,
    )
```

```python
import functools
import math

import jax
import jax.numpy as jnp
from jax import lax
from jax.experimental import pallas as pl
from jax.experimental.pallas import tpu as pltpu
from jax.sharding import PartitionSpec as P

AXES = ("gx", "gy")
MIB = 1 << 20
LINE_FIRST = 0.25


def dot(a, b, dims=((1,), (0,))):
    return lax.dot_general(a, b, (dims, ((), ())), preferred_element_type=jnp.float32)


def split(a):
    high = a.astype(jnp.bfloat16)
    return high, (a - high.astype(jnp.float32)).astype(jnp.bfloat16)


VMEM_SPEC = pl.BlockSpec(memory_space=pltpu.VMEM)
ANY_SPEC = pl.BlockSpec(memory_space=pl.ANY)


def pinned(*arrays):
    return [pltpu.with_memory_space_constraint(a, pltpu.VMEM) for a in arrays]


PLANE = 4
FRONT_BLOCKS = (0, 1, 2, 4, 6, 8)


def place():
    index = lax.axis_index(AXES[0]) * lax.axis_size(AXES[1]) + lax.axis_index(AXES[1])
    return index & 1, (index >> 1) & (PLANE - 1), index // (2 * PLANE)


def row_classes(k, line):
    unit = 8 * line
    second = max(1, round(k * LINE_FIRST / unit)) * unit
    return k - second, second


def front_kernel(in_scale, gram_scale, scale, line, e, signs, sketch_out, sent2, kept1, kept2, *refs):
    sent1 = refs[:PLANE]
    e_kept, sketch, rounded_t, s32, s16, acc, class1, class2, sem, out_sem = refs[PLANE:]
    rows, d = e.shape
    k = rounded_t.shape[0]
    n = sem.shape[0] - 1
    signs_copy = pltpu.make_async_copy(signs, s32, sem.at[n])
    signs_copy.start()

    starts = [rows * i // 8 for i in FRONT_BLOCKS]
    blocks = [pl.ds(a, b - a) for a, b in zip(starts, starts[1:])]
    copies = [pltpu.make_async_copy(e.at[at], e_kept.at[at], sem.at[i]) for i, at in enumerate(blocks)]
    for copy in copies:
        copy.start()
    signs_copy.wait()
    s16[...] = s32[...].astype(jnp.bfloat16)

    for copy, at in zip(copies, blocks):
        copy.wait()
        sk = dot(e_kept[at, :], s16[...]) * in_scale
        sketch[at, :] = sk
        rounded_t[:, at] = sk.astype(jnp.bfloat16).T
    outs = [pltpu.make_async_copy(sketch, sketch_out, out_sem.at[0])]
    outs[0].start()
    high, low = split(sketch[...])
    acc[...] = dot(rounded_t[...], low)
    acc[...] = (dot(rounded_t[...], high) + (acc[...] + acc[...].T)) * gram_scale
    own, in_plane, in_line = place()
    rows1, rows2 = row_classes(k, line)
    size1, size2 = rows1 // line, rows2 // line
    half = k // 2
    size = half // line
    group = 2 * PLANE * size2 + size
    for g in range(line):
        to = pl.ds(pl.multiple_of((in_line ^ g) * group + 2 * PLANE * size2, 8), size)
        for out, region in ((kept2, own), (class2, 1 - own)):
            out[to, :] = acc[pl.ds(pl.multiple_of(region * half + g * size, size), size), :]
    width = d // (2 * PLANE)
    for r, region in enumerate((1 - own, own)):
        for p in range(PLANE):
            at = pl.ds(pl.multiple_of((region * PLANE + (in_plane ^ p)) * width, width), width)
            value = dot(rounded_t[...], e_kept[:, at]) * scale
            for g in range(line):
                to = in_line ^ g
                for h in range(2):
                    part = value[:, h * width // 2 : (h + 1) * width // 2]
                    to1 = pl.multiple_of(p * 2 * rows1 + (2 * to + h) * size1, 8)
                    (class1, kept1)[r][pl.ds(to1, size1), :] = part[g * size1 : (g + 1) * size1]
                    to2 = pl.multiple_of(to * group + ((in_plane ^ p) * 2 + h) * size2, 8)
                    (class2, kept2)[r][pl.ds(to2, size2), :] = part[rows1 + g * size2 : rows1 + (g + 1) * size2]
            if r == 0:
                at = pl.ds(p * 2 * rows1, 2 * rows1)
                outs.append(pltpu.make_async_copy(class1.at[at], sent1[p], out_sem.at[1 + p]))
                outs[-1].start()
        if r == 0:
            outs.append(pltpu.make_async_copy(class2, sent2, out_sem.at[1 + PLANE]))
            outs[-1].start()
    for copy in outs:
        copy.wait()


def front_call(e, signs, rows_all, line):
    rows, d = e.shape
    k = signs.shape[1]
    copies = len(FRONT_BLOCKS) - 1
    rows1, rows2 = row_classes(k, line)
    width = d // (4 * PLANE)
    classes = [(2 * PLANE * rows1, width), (2 * PLANE * rows2 + k // 2, width)]
    f32 = lambda *shape: jax.ShapeDtypeStruct(shape, jnp.float32)
    return pl.pallas_call(
        functools.partial(front_kernel, 1.0 / math.sqrt(d), 1.0 / rows_all, 1.0 / math.sqrt(rows_all), line),
        in_specs=[ANY_SPEC, ANY_SPEC],
        out_specs=[ANY_SPEC] * 2 + [VMEM_SPEC] * 2 + [ANY_SPEC] * PLANE,
        out_shape=[f32(rows, k), f32(*classes[1])]
        + [pltpu.VMEM(c, jnp.float32) for c in classes]
        + [f32(2 * rows1, width)] * PLANE,
        scratch_shapes=[
            pltpu.VMEM((rows, d), e.dtype),
            pltpu.VMEM((rows, k), jnp.float32),
            pltpu.VMEM((k, rows), jnp.bfloat16),
            pltpu.VMEM((d, k), jnp.int32),
            pltpu.VMEM((d, k), jnp.bfloat16),
            pltpu.VMEM((k, k), jnp.float32),
            pltpu.VMEM(classes[0], jnp.float32),
            pltpu.VMEM(classes[1], jnp.float32),
            pltpu.SemaphoreType.DMA((copies + 1,)),
            pltpu.SemaphoreType.DMA((2 + PLANE,)),
        ],
        compiler_params=pltpu.CompilerParams(vmem_limit_bytes=48 * MIB),
        cost_estimate=pl.CostEstimate(flops=4 * rows * d * k, bytes_accessed=rows * d * 2 + d * k * 4, transcendentals=0),
        name="front",
    )(e, pltpu.with_memory_space_constraint(signs, pltpu.HBM))


def factor_kernel(line, kept, got, triangle, inverse, work):
    k = triangle.shape[0]
    half = k // 2
    b = 64
    own, _, in_line = place()
    size = half // line
    for g in range(line):
        at = pl.ds(pl.multiple_of((in_line ^ g) * size, size), size)
        for rows, region in ((kept, own), (got, 1 - own)):
            work[pl.ds(pl.multiple_of(region * half + g * size, size), size), :k] = rows[at, :]
    rows_k = lax.broadcasted_iota(jnp.int32, (k, k), 0)
    cols_k = lax.broadcasted_iota(jnp.int32, (k, k), 1)
    work[:, k:] = jnp.where(rows_k == cols_k, 1.0, 0.0)
    lane = lax.broadcasted_iota(jnp.int32, (8, 2 * b), 1)
    sub = lax.broadcasted_iota(jnp.int32, (8, 2 * b), 0)

    def over_lanes(a, at):
        return jnp.broadcast_to(a[:, at : at + 1], (8, 2 * b))

    for n in range(k // b):
        first = (n % 2) * b
        pair = (n // 2) * 2 * b
        own_lanes = (lane >= first) & (lane < first + b)
        w = []
        for v in range(b // 8):
            a = work[n * b + 8 * v : n * b + 8 * v + 8, pair : pair + 2 * b]
            ident = jnp.where(lane == (b - first) + 8 * v + sub, 1.0, 0.0)
            w.append(jnp.where(own_lanes, a, ident))
        inv = []
        for q in range(b // 8):
            at = first + 8 * q
            row = [jnp.broadcast_to(w[q][i : i + 1, :], (8, 2 * b)) for i in range(8)]
            s = {(i, j): over_lanes(row[i], at + j) for i in range(8) for j in range(i, 8)}
            factor = {}
            scaled = []
            for j in range(8):
                r = 1.0 / s[j, j]
                for i in range(j + 1, 8):
                    factor[i, j] = s[j, i] * r
                    for m in range(i, 8):
                        s[i, m] = s[i, m] - factor[i, j] * s[j, m]
                    row[i] = row[i] - factor[i, j] * row[j]
                scaled.append(row[j] * r)
            new, pivots = row[0], s[0, 0]
            for i in range(1, 8):
                new = jnp.where(sub == i, row[i], new)
                pivots = jnp.where(sub == i, s[i, i], pivots)
            for v in range(q + 1, b // 8):
                col = [over_lanes(w[v], at + j) for j in range(8)]
                for j in range(8):
                    for m in range(j + 1, 8):
                        col[m] = col[m] - col[j] * factor[m, j]
                t = [col[j] * scaled[j] for j in range(8)]
                w[v] = w[v] - (((t[0] + t[1]) + (t[2] + t[3])) + ((t[4] + t[5]) + (t[6] + t[7])))
            moved = pltpu.roll(new * (1.0 / jnp.sqrt(pivots)), b, 1)
            inv.append(jnp.where(own_lanes, moved, 0.0))
        inv = jnp.concatenate(inv, axis=0)
        end = k + pair + 2 * b
        y = lax.dot_general(
            inv, work[pair : pair + 2 * b, pair:end], (((1,), (0,)), ((), ())),
            precision=lax.Precision.HIGHEST, preferred_element_type=jnp.float32,
        )
        r_rows, i_rows = y[:, : k - pair], y[:, k - pair :]
        at = lax.broadcasted_iota(jnp.int32, r_rows.shape, 0) + n * b
        to = lax.broadcasted_iota(jnp.int32, r_rows.shape, 1) + pair
        put = slice(n * b, (n + 1) * b)
        if pair:
            triangle[put, :pair] = jnp.zeros((b, pair), jnp.float32)
        triangle[put, pair:] = jnp.where(to >= at, r_rows, 0.0)
        i_at = lax.broadcasted_iota(jnp.int32, i_rows.shape, 0) + n * b
        i_to = lax.broadcasted_iota(jnp.int32, i_rows.shape, 1)
        for row, part in zip((n * b, k + n * b), split(jnp.where(i_to <= i_at, i_rows, 0.0))):
            inverse[row : row + b, : pair + 2 * b] = part
            if pair + 2 * b < k:
                inverse[row : row + b, pair + 2 * b :] = jnp.zeros((b, k - pair - 2 * b), part.dtype)
        if (n + 1) * b < k:
            rest = (n + 1) // 2 * 2 * b
            later = jnp.where(to >= (n + 1) * b, r_rows, 0.0)[:, rest - pair :]
            work[rest:, rest:end] -= lax.dot_general(
                later, y[:, rest - pair :], (((0,), (0,)), ((), ())),
                precision=lax.Precision.HIGHEST, preferred_element_type=jnp.float32,
            )


def factor_call(line, kept, got):
    k = kept.shape[1]
    return pl.pallas_call(
        functools.partial(factor_kernel, line),
        in_specs=[VMEM_SPEC] * 2,
        out_specs=[VMEM_SPEC] * 2,
        out_shape=[
            jax.ShapeDtypeStruct((k, k), jnp.float32),
            jax.ShapeDtypeStruct((2 * k, k), jnp.bfloat16),
        ],
        scratch_shapes=[pltpu.VMEM((k, 2 * k), jnp.float32)],
        compiler_params=pltpu.CompilerParams(vmem_limit_bytes=16 * MIB),
        cost_estimate=pl.CostEstimate(flops=10**10, bytes_accessed=k * k * 8, transcendentals=0),
        name="factor",
    )(kept, got)


def basis_kernel(sketch, inverse, out, value, sem):
    rows, k = sketch.shape
    n = sem.shape[0]
    right = ((1,), (1,))
    copies = []
    for i in range(n):
        at = pl.ds(i * (rows // n), rows // n)
        s_high, s_low = split(sketch[at, :])
        both = dot(s_high, inverse[...], right)
        value[at, :] = (both[:, :k] + (both[:, k:] + dot(s_low, inverse[:k, :], right))).astype(out.dtype)
        copies.append(pltpu.make_async_copy(value.at[at], out.at[at], sem.at[i]))
        copies[-1].start()
    for copy in copies:
        copy.wait()


def basis_call(sketch, inverse):
    rows, k = sketch.shape
    return pl.pallas_call(
        basis_kernel,
        in_specs=[VMEM_SPEC] * 2,
        out_specs=ANY_SPEC,
        out_shape=jax.ShapeDtypeStruct((rows, k), jnp.bfloat16),
        scratch_shapes=[pltpu.VMEM((rows, k), jnp.bfloat16), pltpu.SemaphoreType.DMA((4,))],
        compiler_params=pltpu.CompilerParams(vmem_limit_bytes=16 * MIB),
        cost_estimate=pl.CostEstimate(flops=6 * rows * k * k, bytes_accessed=rows * k * 6, transcendentals=0),
        name="basis",
    )(*pinned(sketch, inverse))


def project_kernel(line, is_own, inverse, *refs):
    *blocks, out, whole, value, sem = refs
    class1, class2 = blocks[-PLANE - 1 : -1], blocks[-1]
    k = inverse.shape[1]
    rows1, rows2 = row_classes(k, line)
    size1, size2 = rows1 // line, rows2 // line
    own, in_plane, in_line = place()
    region = own if is_own else 1 - own
    width = value.shape[2]
    copies = []
    for p in range(PLANE):
        for g in range(line):
            to = in_line ^ g
            for h in range(2):
                cols = slice(h * width // 2, (h + 1) * width // 2)
                to1 = pl.ds(pl.multiple_of(to * size1, 8), size1)
                whole[p, to1, cols] = class1[p][(2 * g + h) * size1 : (2 * g + h + 1) * size1, :]
                to2 = pl.ds(pl.multiple_of(rows1 + to * size2, 8), size2)
                at2 = pl.ds(pl.multiple_of(((g * PLANE + (in_plane ^ p)) * 2 + h) * size2, 8), size2)
                whole[p, to2, cols] = class2[at2, :]
        c_high, c_low = split(whole[p])
        both = dot(inverse[...], c_high)
        value[p] = both[:k] + (both[k:] + dot(inverse[:k, :], c_low))
        at = pl.ds(pl.multiple_of((region * PLANE + (in_plane ^ p)) * width, width), width)
        copies.append(pltpu.make_async_copy(value.at[p], out.at[:, at], sem.at[p]))
        copies[-1].start()
    for copy in copies:
        copy.wait()


def project_call(line, is_own, inverse, blocks, d, before):
    k = inverse.shape[1]
    width = d // (2 * PLANE)
    extra = [] if before is None else [before]
    return pl.pallas_call(
        functools.partial(project_kernel, line, is_own),
        in_specs=[VMEM_SPEC] + [ANY_SPEC] * len(extra) + [VMEM_SPEC] * len(blocks),
        out_specs=ANY_SPEC,
        out_shape=jax.ShapeDtypeStruct((k, d), jnp.float32),
        input_output_aliases={1: 0} if extra else {},
        scratch_shapes=[
            pltpu.VMEM((PLANE, k, width), jnp.float32),
            pltpu.VMEM((PLANE, k, width), jnp.float32),
            pltpu.SemaphoreType.DMA((PLANE,)),
        ],
        compiler_params=pltpu.CompilerParams(vmem_limit_bytes=16 * MIB),
        cost_estimate=pl.CostEstimate(flops=3 * k * k * d, bytes_accessed=k * d * 4, transcendentals=0),
        name="project",
    )(*pinned(inverse), *extra, *pinned(*blocks))


def solution(mesh):
    n_devices = math.prod(mesh.shape.values())
    line = n_devices // (2 * PLANE)

    def over(mask):
        pairs = [(i, i ^ mask) for i in range(n_devices)]
        return lambda a: lax.ppermute(a, AXES, pairs)

    with_pair = over(1)
    over_plane = [over(2 * g) for g in range(PLANE)]
    over_line = [over(2 * PLANE * g) for g in range(line)]

    def parts_of(a, n):
        size = a.shape[0] // n
        return [a[i * size : (i + 1) * size] for i in range(n)]

    def join(*arrays):
        return jnp.concatenate(arrays, axis=0)

    def shards(e, signs):
        rows_all = e.shape[0] * n_devices
        d = e.shape[1]
        k = signs.shape[1]
        rows1, rows2 = row_classes(k, line)
        last = []

        def in_turn(*arrays):
            arrays = lax.optimization_barrier((*arrays, *last[-1:]))[: len(arrays)]
            last.append(arrays[-1])
            return arrays if len(arrays) > 1 else arrays[0]

        sketch, sent2, kept1, kept2, *sent1 = front_call(e, signs, rows_all, line)
        got1 = [with_pair(a) for a in sent1[1:]]
        got2 = with_pair(sent2)
        kept1 = parts_of(kept1, PLANE)
        from_plane = []
        for g in range(1, PLANE):
            if g > 1:
                got1[g - 1] = in_turn(got1[g - 1])
            from_plane.append(over_plane[g](in_turn(kept1[g] + got1[g - 1])))
        a1 = kept1[0] + with_pair(sent1[0])
        parts2 = in_turn(*[a + b for a, b in zip(parts_of(kept2, line), parts_of(got2, line))])
        from_line = [over_line[g](parts2[g]) for g in range(1, line)]
        mine, near, *far = parts_of(sum(from_plane, a1), line)
        a2 = sum(from_line, parts2[0])
        mine, *far = in_turn(mine, *far)
        from_line = [over_line[g](a) for g, a in enumerate(far, 2)]
        a2 = in_turn(a2)
        whole2 = [over_plane[g](a2) for g in range(1, PLANE)]
        from_line = [over_line[1](in_turn(near)), *from_line]
        a2 = (a2 + whole2[0]) + (whole2[1] + whole2[2])
        n2 = a2.shape[0] - k // 2 // line
        a1 = in_turn(join(sum(from_line, mine), a2[n2:]))
        gathered = [a1] + [over_line[g](a1) for g in range(1, line)]
        n1 = a1.shape[0] - k // 2 // line
        a1 = in_turn(join(*[a[:n1] for a in gathered]))
        class1 = [over_plane[g](a1) for g in range(1, PLANE)]
        gram = in_turn(join(*[a[n1:] for a in gathered]))
        gram_got = with_pair(gram)
        class2 = in_turn(a2[:n2])
        class2 = join(class2, over_line[1](class2))
        gram_got, class2 = in_turn(gram_got, class2)
        for bit in range(1, line.bit_length() - 1):
            class2 = join(class2, over_line[1 << bit](class2))
        a1 = in_turn(a1)
        their1 = with_pair(a1)
        triangle, inverse = factor_call(line, in_turn(gram), gram_got)
        their1, inverse = in_turn(their1, inverse)
        basis = in_turn(basis_call(in_turn(sketch), inverse))
        class2 = in_turn(class2)
        their2 = with_pair(class2)
        class1 = in_turn(*class1)
        theirs = [their1, *[with_pair(a) for a in class1], their2]
        projected = project_call(line, True, inverse, [a1, *class1, class2], d, None)
        projected = project_call(line, False, inverse, theirs, d, projected)
        return triangle, basis, projected

    return jax.shard_map(
        shards,
        mesh=mesh,
        in_specs=(P(AXES, None), P()),
        out_specs=(P(), P(AXES, None), P()),
        check_vma=False,
    )
```

```python
import functools
import math

import jax
import jax.numpy as jnp
from jax import lax
from jax.experimental import pallas as pl
from jax.experimental.pallas import tpu as pltpu
from jax.sharding import PartitionSpec as P

AXES = ("gx", "gy")
MIB = 1 << 20
LINE_FIRST = 0.25


def dot(a, b, dims=((1,), (0,))):
    return lax.dot_general(a, b, (dims, ((), ())), preferred_element_type=jnp.float32)


def split(a):
    high = a.astype(jnp.bfloat16)
    return high, (a - high.astype(jnp.float32)).astype(jnp.bfloat16)


VMEM_SPEC = pl.BlockSpec(memory_space=pltpu.VMEM)
ANY_SPEC = pl.BlockSpec(memory_space=pl.ANY)


def pinned(*arrays):
    return [pltpu.with_memory_space_constraint(a, pltpu.VMEM) for a in arrays]


PLANE = 4


def place():
    index = lax.axis_index(AXES[0]) * lax.axis_size(AXES[1]) + lax.axis_index(AXES[1])
    return index & 1, (index >> 1) & (PLANE - 1), index // (2 * PLANE)


def row_classes(k, line):
    unit = 8 * line
    second = max(1, round(k * LINE_FIRST / unit)) * unit
    return k - second, second


def front_kernel(in_scale, gram_scale, scale, line, e, signs, sketch_out, sent2, kept1, kept2, *refs):
    sent1 = refs[:PLANE]
    e_kept, sketch, rounded_t, s32, s16, acc, class1, class2, sem, out_sem = refs[PLANE:]
    rows, d = e.shape
    k = rounded_t.shape[0]
    n = sem.shape[0] - 1
    block = rows // n
    signs_copy = pltpu.make_async_copy(signs, s32, sem.at[n])
    signs_copy.start()

    def rows_copy(i):
        at = pl.ds(pl.multiple_of(i * block, block), block)
        return pltpu.make_async_copy(e.at[at], e_kept.at[at], sem.at[i])

    for i in range(n):
        rows_copy(i).start()
    signs_copy.wait()
    s16[...] = s32[...].astype(jnp.bfloat16)

    def step(i, carry):
        rows_copy(i).wait()
        at = pl.ds(pl.multiple_of(i * block, block), block)
        sk = dot(e_kept[at, :], s16[...]) * in_scale
        sketch[at, :] = sk
        rounded_t[:, at] = sk.astype(jnp.bfloat16).T
        return carry

    lax.fori_loop(0, n, step, 0)
    outs = [pltpu.make_async_copy(sketch, sketch_out, out_sem.at[0])]
    outs[0].start()
    high, low = split(sketch[...])
    acc[...] = dot(rounded_t[...], low)
    acc[...] = (dot(rounded_t[...], high) + (acc[...] + acc[...].T)) * gram_scale
    own, in_plane, in_line = place()
    rows1, rows2 = row_classes(k, line)
    size1, size2 = rows1 // line, rows2 // line
    half = k // 2
    size = half // line
    group = 2 * PLANE * size2 + size
    for g in range(line):
        to = pl.ds(pl.multiple_of((in_line ^ g) * group + 2 * PLANE * size2, 8), size)
        for out, region in ((kept2, own), (class2, 1 - own)):
            out[to, :] = acc[pl.ds(pl.multiple_of(region * half + g * size, size), size), :]
    width = d // (2 * PLANE)
    for r, region in enumerate((1 - own, own)):
        for p in range(PLANE):
            at = pl.ds(pl.multiple_of((region * PLANE + (in_plane ^ p)) * width, width), width)
            value = dot(rounded_t[...], e_kept[:, at]) * scale
            for g in range(line):
                to = in_line ^ g
                for h in range(2):
                    part = value[:, h * width // 2 : (h + 1) * width // 2]
                    to1 = pl.multiple_of(p * 2 * rows1 + (2 * to + h) * size1, 8)
                    (class1, kept1)[r][pl.ds(to1, size1), :] = part[g * size1 : (g + 1) * size1]
                    to2 = pl.multiple_of(to * group + ((in_plane ^ p) * 2 + h) * size2, 8)
                    (class2, kept2)[r][pl.ds(to2, size2), :] = part[rows1 + g * size2 : rows1 + (g + 1) * size2]
            if r == 0:
                at = pl.ds(p * 2 * rows1, 2 * rows1)
                outs.append(pltpu.make_async_copy(class1.at[at], sent1[p], out_sem.at[1 + p]))
                outs[-1].start()
        if r == 0:
            outs.append(pltpu.make_async_copy(class2, sent2, out_sem.at[1 + PLANE]))
            outs[-1].start()
    for copy in outs:
        copy.wait()


def front_call(e, signs, rows_all, line):
    rows, d = e.shape
    k = signs.shape[1]
    copies = 4
    rows1, rows2 = row_classes(k, line)
    width = d // (4 * PLANE)
    classes = [(2 * PLANE * rows1, width), (2 * PLANE * rows2 + k // 2, width)]
    f32 = lambda *shape: jax.ShapeDtypeStruct(shape, jnp.float32)
    return pl.pallas_call(
        functools.partial(front_kernel, 1.0 / math.sqrt(d), 1.0 / rows_all, 1.0 / math.sqrt(rows_all), line),
        in_specs=[ANY_SPEC, ANY_SPEC],
        out_specs=[ANY_SPEC] * 2 + [VMEM_SPEC] * 2 + [ANY_SPEC] * PLANE,
        out_shape=[f32(rows, k), f32(*classes[1])]
        + [pltpu.VMEM(c, jnp.float32) for c in classes]
        + [f32(2 * rows1, width)] * PLANE,
        scratch_shapes=[
            pltpu.VMEM((rows, d), e.dtype),
            pltpu.VMEM((rows, k), jnp.float32),
            pltpu.VMEM((k, rows), jnp.bfloat16),
            pltpu.VMEM((d, k), jnp.int32),
            pltpu.VMEM((d, k), jnp.bfloat16),
            pltpu.VMEM((k, k), jnp.float32),
            pltpu.VMEM(classes[0], jnp.float32),
            pltpu.VMEM(classes[1], jnp.float32),
            pltpu.SemaphoreType.DMA((copies + 1,)),
            pltpu.SemaphoreType.DMA((2 + PLANE,)),
        ],
        compiler_params=pltpu.CompilerParams(vmem_limit_bytes=48 * MIB),
        cost_estimate=pl.CostEstimate(flops=4 * rows * d * k, bytes_accessed=rows * d * 2 + d * k * 4, transcendentals=0),
        name="front",
    )(e, pltpu.with_memory_space_constraint(signs, pltpu.HBM))


def factor_kernel(line, kept, got, triangle, inverse, work):
    k = triangle.shape[0]
    half = k // 2
    b = 64
    own, _, in_line = place()
    size = half // line
    for g in range(line):
        at = pl.ds(pl.multiple_of((in_line ^ g) * size, size), size)
        for rows, region in ((kept, own), (got, 1 - own)):
            work[pl.ds(pl.multiple_of(region * half + g * size, size), size), :k] = rows[at, :]
    rows_k = lax.broadcasted_iota(jnp.int32, (k, k), 0)
    cols_k = lax.broadcasted_iota(jnp.int32, (k, k), 1)
    work[:, k:] = jnp.where(rows_k == cols_k, 1.0, 0.0)
    lane = lax.broadcasted_iota(jnp.int32, (8, 2 * b), 1)
    sub = lax.broadcasted_iota(jnp.int32, (8, 2 * b), 0)

    def over_lanes(a, at):
        return jnp.broadcast_to(a[:, at : at + 1], (8, 2 * b))

    for n in range(k // b):
        first = (n % 2) * b
        pair = (n // 2) * 2 * b
        own_lanes = (lane >= first) & (lane < first + b)
        w = []
        for v in range(b // 8):
            a = work[n * b + 8 * v : n * b + 8 * v + 8, pair : pair + 2 * b]
            ident = jnp.where(lane == (b - first) + 8 * v + sub, 1.0, 0.0)
            w.append(jnp.where(own_lanes, a, ident))
        inv = []
        for q in range(b // 8):
            at = first + 8 * q
            row = [jnp.broadcast_to(w[q][i : i + 1, :], (8, 2 * b)) for i in range(8)]
            s = {(i, j): over_lanes(row[i], at + j) for i in range(8) for j in range(i, 8)}
            factor = {}
            scaled = []
            for j in range(8):
                r = 1.0 / s[j, j]
                for i in range(j + 1, 8):
                    factor[i, j] = s[j, i] * r
                    for m in range(i, 8):
                        s[i, m] = s[i, m] - factor[i, j] * s[j, m]
                    row[i] = row[i] - factor[i, j] * row[j]
                scaled.append(row[j] * r)
            new, pivots = row[0], s[0, 0]
            for i in range(1, 8):
                new = jnp.where(sub == i, row[i], new)
                pivots = jnp.where(sub == i, s[i, i], pivots)
            for v in range(q + 1, b // 8):
                col = [over_lanes(w[v], at + j) for j in range(8)]
                for j in range(8):
                    for m in range(j + 1, 8):
                        col[m] = col[m] - col[j] * factor[m, j]
                t = [col[j] * scaled[j] for j in range(8)]
                w[v] = w[v] - (((t[0] + t[1]) + (t[2] + t[3])) + ((t[4] + t[5]) + (t[6] + t[7])))
            moved = pltpu.roll(new * (1.0 / jnp.sqrt(pivots)), b, 1)
            inv.append(jnp.where(own_lanes, moved, 0.0))
        inv = jnp.concatenate(inv, axis=0)
        end = k + pair + 2 * b
        y = lax.dot_general(
            inv, work[pair : pair + 2 * b, pair:end], (((1,), (0,)), ((), ())),
            precision=lax.Precision.HIGHEST, preferred_element_type=jnp.float32,
        )
        r_rows, i_rows = y[:, : k - pair], y[:, k - pair :]
        at = lax.broadcasted_iota(jnp.int32, r_rows.shape, 0) + n * b
        to = lax.broadcasted_iota(jnp.int32, r_rows.shape, 1) + pair
        put = slice(n * b, (n + 1) * b)
        if pair:
            triangle[put, :pair] = jnp.zeros((b, pair), jnp.float32)
        triangle[put, pair:] = jnp.where(to >= at, r_rows, 0.0)
        i_at = lax.broadcasted_iota(jnp.int32, i_rows.shape, 0) + n * b
        i_to = lax.broadcasted_iota(jnp.int32, i_rows.shape, 1)
        for row, part in zip((n * b, k + n * b), split(jnp.where(i_to <= i_at, i_rows, 0.0))):
            inverse[row : row + b, : pair + 2 * b] = part
            if pair + 2 * b < k:
                inverse[row : row + b, pair + 2 * b :] = jnp.zeros((b, k - pair - 2 * b), part.dtype)
        if (n + 1) * b < k:
            rest = (n + 1) // 2 * 2 * b
            later = jnp.where(to >= (n + 1) * b, r_rows, 0.0)[:, rest - pair :]
            work[rest:, rest:end] -= lax.dot_general(
                later, y[:, rest - pair :], (((0,), (0,)), ((), ())),
                precision=lax.Precision.HIGHEST, preferred_element_type=jnp.float32,
            )


def factor_call(line, kept, got):
    k = kept.shape[1]
    return pl.pallas_call(
        functools.partial(factor_kernel, line),
        in_specs=[VMEM_SPEC] * 2,
        out_specs=[VMEM_SPEC] * 2,
        out_shape=[
            jax.ShapeDtypeStruct((k, k), jnp.float32),
            jax.ShapeDtypeStruct((2 * k, k), jnp.bfloat16),
        ],
        scratch_shapes=[pltpu.VMEM((k, 2 * k), jnp.float32)],
        compiler_params=pltpu.CompilerParams(vmem_limit_bytes=16 * MIB),
        cost_estimate=pl.CostEstimate(flops=10**10, bytes_accessed=k * k * 8, transcendentals=0),
        name="factor",
    )(kept, got)


def basis_kernel(sketch, inverse, out, value, sem):
    rows, k = sketch.shape
    n = sem.shape[0]
    right = ((1,), (1,))
    copies = []
    for i in range(n):
        at = pl.ds(i * (rows // n), rows // n)
        s_high, s_low = split(sketch[at, :])
        both = dot(s_high, inverse[...], right)
        value[at, :] = (both[:, :k] + (both[:, k:] + dot(s_low, inverse[:k, :], right))).astype(out.dtype)
        copies.append(pltpu.make_async_copy(value.at[at], out.at[at], sem.at[i]))
        copies[-1].start()
    for copy in copies:
        copy.wait()


def basis_call(sketch, inverse):
    rows, k = sketch.shape
    return pl.pallas_call(
        basis_kernel,
        in_specs=[VMEM_SPEC] * 2,
        out_specs=ANY_SPEC,
        out_shape=jax.ShapeDtypeStruct((rows, k), jnp.bfloat16),
        scratch_shapes=[pltpu.VMEM((rows, k), jnp.bfloat16), pltpu.SemaphoreType.DMA((4,))],
        compiler_params=pltpu.CompilerParams(vmem_limit_bytes=16 * MIB),
        cost_estimate=pl.CostEstimate(flops=6 * rows * k * k, bytes_accessed=rows * k * 6, transcendentals=0),
        name="basis",
    )(*pinned(sketch, inverse))


def project_kernel(line, is_own, inverse, *refs):
    *blocks, out, whole, value, sem = refs
    class1, class2 = blocks[-PLANE - 1 : -1], blocks[-1]
    k = inverse.shape[1]
    rows1, rows2 = row_classes(k, line)
    size1, size2 = rows1 // line, rows2 // line
    own, in_plane, in_line = place()
    region = own if is_own else 1 - own
    width = value.shape[2]
    copies = []
    for p in range(PLANE):
        for g in range(line):
            to = in_line ^ g
            for h in range(2):
                cols = slice(h * width // 2, (h + 1) * width // 2)
                to1 = pl.ds(pl.multiple_of(to * size1, 8), size1)
                whole[p, to1, cols] = class1[p][(2 * g + h) * size1 : (2 * g + h + 1) * size1, :]
                to2 = pl.ds(pl.multiple_of(rows1 + to * size2, 8), size2)
                at2 = pl.ds(pl.multiple_of(((g * PLANE + (in_plane ^ p)) * 2 + h) * size2, 8), size2)
                whole[p, to2, cols] = class2[at2, :]
        c_high, c_low = split(whole[p])
        both = dot(inverse[...], c_high)
        value[p] = both[:k] + (both[k:] + dot(inverse[:k, :], c_low))
        at = pl.ds(pl.multiple_of((region * PLANE + (in_plane ^ p)) * width, width), width)
        copies.append(pltpu.make_async_copy(value.at[p], out.at[:, at], sem.at[p]))
        copies[-1].start()
    for copy in copies:
        copy.wait()


def project_call(line, is_own, inverse, blocks, d, before):
    k = inverse.shape[1]
    width = d // (2 * PLANE)
    extra = [] if before is None else [before]
    return pl.pallas_call(
        functools.partial(project_kernel, line, is_own),
        in_specs=[VMEM_SPEC] + [ANY_SPEC] * len(extra) + [VMEM_SPEC] * len(blocks),
        out_specs=ANY_SPEC,
        out_shape=jax.ShapeDtypeStruct((k, d), jnp.float32),
        input_output_aliases={1: 0} if extra else {},
        scratch_shapes=[
            pltpu.VMEM((PLANE, k, width), jnp.float32),
            pltpu.VMEM((PLANE, k, width), jnp.float32),
            pltpu.SemaphoreType.DMA((PLANE,)),
        ],
        compiler_params=pltpu.CompilerParams(vmem_limit_bytes=16 * MIB),
        cost_estimate=pl.CostEstimate(flops=3 * k * k * d, bytes_accessed=k * d * 4, transcendentals=0),
        name="project",
    )(*pinned(inverse), *extra, *pinned(*blocks))


def solution(mesh):
    n_devices = math.prod(mesh.shape.values())
    line = n_devices // (2 * PLANE)

    def over(mask):
        pairs = [(i, i ^ mask) for i in range(n_devices)]
        return lambda a: lax.ppermute(a, AXES, pairs)

    with_pair = over(1)
    over_plane = [over(2 * g) for g in range(PLANE)]
    over_line = [over(2 * PLANE * g) for g in range(line)]

    def parts_of(a, n):
        size = a.shape[0] // n
        return [a[i * size : (i + 1) * size] for i in range(n)]

    def join(*arrays):
        return jnp.concatenate(arrays, axis=0)

    def shards(e, signs):
        rows_all = e.shape[0] * n_devices
        d = e.shape[1]
        k = signs.shape[1]
        rows1, rows2 = row_classes(k, line)
        last = []

        def in_turn(*arrays):
            arrays = lax.optimization_barrier((*arrays, *last[-1:]))[: len(arrays)]
            last.append(arrays[-1])
            return arrays if len(arrays) > 1 else arrays[0]

        sketch, sent2, kept1, kept2, *sent1 = front_call(e, signs, rows_all, line)
        got1 = [with_pair(a) for a in sent1[1:]]
        got2 = with_pair(sent2)
        kept1 = parts_of(kept1, PLANE)
        from_plane = []
        for g in range(1, PLANE):
            if g > 1:
                got1[g - 1] = in_turn(got1[g - 1])
            from_plane.append(over_plane[g](in_turn(kept1[g] + got1[g - 1])))
        a1 = kept1[0] + with_pair(sent1[0])
        parts2 = in_turn(*[a + b for a, b in zip(parts_of(kept2, line), parts_of(got2, line))])
        from_line = [over_line[g](parts2[g]) for g in range(1, line)]
        parts1 = in_turn(*parts_of(sum(from_plane, a1), line))
        a2 = sum(from_line, parts2[0])
        from_line = [over_line[g](parts1[g]) for g in range(1, line)]
        a2 = in_turn(a2)
        whole2 = [over_plane[g](a2) for g in range(1, PLANE)]
        a2 = (a2 + whole2[0]) + (whole2[1] + whole2[2])
        n2 = a2.shape[0] - k // 2 // line
        a1 = in_turn(join(sum(from_line, parts1[0]), a2[n2:]))
        gathered = [a1] + [over_line[g](a1) for g in range(1, line)]
        n1 = a1.shape[0] - k // 2 // line
        a1 = in_turn(join(*[a[:n1] for a in gathered]))
        class1 = [over_plane[g](a1) for g in range(1, PLANE)]
        gram = in_turn(join(*[a[n1:] for a in gathered]))
        gram_got = with_pair(gram)
        class2 = in_turn(a2[:n2])
        class2 = join(class2, over_line[1](class2))
        gram_got, class2 = in_turn(gram_got, class2)
        for bit in range(1, line.bit_length() - 1):
            class2 = join(class2, over_line[1 << bit](class2))
        a1 = in_turn(a1)
        their1 = with_pair(a1)
        triangle, inverse = factor_call(line, in_turn(gram), gram_got)
        their1, inverse = in_turn(their1, inverse)
        basis = in_turn(basis_call(in_turn(sketch), inverse))
        class2 = in_turn(class2)
        their2 = with_pair(class2)
        class1 = in_turn(*class1)
        theirs = [their1, *[with_pair(a) for a in class1], their2]
        projected = project_call(line, True, inverse, [a1, *class1, class2], d, None)
        projected = project_call(line, False, inverse, theirs, d, projected)
        return triangle, basis, projected

    return jax.shard_map(
        shards,
        mesh=mesh,
        in_specs=(P(AXES, None), P()),
        out_specs=(P(), P(AXES, None), P()),
        check_vma=False,
    )
```
